32 devices in a mesh: row: 2 (over core), col: 4 (over y, x), depth: 4 (over z).
Axes of the slice: x: 2, y: 2, z: 4, core: 2. Of those that a mesh axis runs over, the one named last changes fastest.
Arguments:
- blocks: float32 [512, 4, 4, 128, 128], P(('row', 'depth'), 'col'), may hold values from -0.9 to 0.9
- columns: int32 [512, 4, 4], P(('row', 'depth'), 'col'), may hold values from 0 to 127, as said below
- counts: int32 [512, 4], P(('row', 'depth'), 'col'), may hold values from 0 to 4, as said below
Outputs:
- purified: float32 [8, 4, 4, 128, 128], P(('row', 'depth'), 'col')
The draws below stay inside these ranges and needn't reach their ends.
Inputs may be any that keep to these rules, and one draw needn't show every extreme that they name: `columns`: the first counts[i, p] slots of block row i in panel p name distinct places; the panel that holds block column i names it in slot 0. `counts`: the panel that holds block column i has a count of 1 or more.
All inputs are finite; a program needn't handle non-finite values.
Results may differ from the reference program's by a relative error of at most 0.0003.
Values sent between devices are 32-bit elements; how exact they have to be, the bound alone decides.
A program may use at most 128 MiB of HBM per device.

```python
import jax
import jax.numpy as jnp
from jax import lax

BLOCK = 128
NB = 512
ROWS_WIN = 1
PANELS = 4
GROUP = 64
SLOTS_PANEL = 4
PANEL_COLS = 128
OUT_ROWS = 8


def pattern_parts(key):
    key = jax.random.fold_in(key, 17)
    first_key, second_key = jax.random.split(key)
    row_ids = jnp.arange(NB, dtype=jnp.int32)
    diag_panel = row_ids // GROUP % PANELS
    diag_place = row_ids // (GROUP * PANELS) * GROUP + row_ids % GROUP
    places = jnp.arange(PANEL_COLS, dtype=jnp.int32)
    panel_ids = jnp.arange(PANELS, dtype=jnp.int32)
    scores = jax.random.randint(first_key, (NB, PANELS, PANEL_COLS), 0, 1 << 20) * PANEL_COLS + places[None, None, :]
    on_diag = (panel_ids[None, :, None] == diag_panel[:, None, None]) & (places[None, None, :] == diag_place[:, None, None])
    scores = jnp.where(on_diag, jnp.int32(1 << 30), scores)
    top_scores, chosen = lax.top_k(scores, SLOTS_PANEL)
    used = jax.random.randint(second_key, (NB, PANELS), 0, SLOTS_PANEL + 1)
    holds_diag = panel_ids[None, :] == diag_panel[:, None]
    used = jnp.where(holds_diag, jnp.maximum(used, 1), used)
    return (chosen.astype(jnp.int32), used.astype(jnp.int32))


def draw_columns(key, part):
    chosen, used = pattern_parts(key)
    return chosen


def draw_counts(key, part):
    chosen, used = pattern_parts(key)
    return used


def block_scale(key, dims, shards, least, top_value):
    level = 1.0
    for position, blocks in shards:
        steps = jax.random.uniform(jax.random.fold_in(jax.random.fold_in(key, 6), position), (blocks,), jnp.float32, least / len(shards), top_value / len(shards))
        level = level * jnp.repeat(jnp.exp(steps), dims[position] // blocks).reshape((-1,) + (1,) * (len(dims) - 1 - position))
    return level


def noise(stream_key, shape, spread, most, cuts=(), kind=jnp.bfloat16):
    values = spread * jax.random.normal(stream_key, shape, jnp.float32)
    if cuts:
        values = values * block_scale(stream_key, shape, cuts, -0.22, 0.18)
    return jnp.clip(values, -most, most).astype(kind)


def setup_inputs(seed: int = 0) -> dict:
    seeds = jax.random.split(jax.random.key(seed), 4)
    return {
        "blocks": noise(seeds[0], (NB, PANELS, SLOTS_PANEL, BLOCK, BLOCK), 0.15, 0.9, ((0, 8), (1, 4)), jnp.float32),
        "columns": draw_columns(jax.random.fold_in(seeds[3], 71), 0),
        "counts": draw_counts(jax.random.fold_in(seeds[3], 71), 0),
    }


def row_product(left_side, left_cols, left_count, blocks, columns, counts):
    slot_ids = jnp.arange(left_cols.shape[-1], dtype=jnp.int32)
    panel_ids = jnp.arange(left_cols.shape[0], dtype=jnp.int32)
    left_valid = slot_ids[None, :] < left_count[:, None]
    inner_row = ((left_cols // GROUP) * (GROUP * PANELS) + panel_ids[:, None] * GROUP + left_cols % GROUP).astype(jnp.int32)
    taken_blocks = blocks[inner_row]
    taken_cols = columns[inner_row]
    taken_valid = slot_ids < counts[inner_row][..., None]
    matched = (taken_cols[..., None] == left_cols[None, None, :, None, :]) & taken_valid[..., None]
    matched = matched & left_valid[None, None, :, None, :] & left_valid[:, :, None, None, None]
    select = jnp.einsum("abqts,abqtyz->abqsyz", matched.astype(jnp.float32), taken_blocks, precision=lax.Precision.HIGHEST)
    return jnp.einsum("abxy,abqsyz->qsxz", left_side, select, precision=lax.Precision.HIGHEST)


def reference(blocks, columns, counts):
    out_ids = jnp.arange(OUT_ROWS, dtype=jnp.int32)
    window = ((out_ids // ROWS_WIN) * GROUP + out_ids % ROWS_WIN).astype(jnp.int32)

    def square_row(index):
        return row_product(blocks[index], columns[index], counts[index], blocks, columns, counts)

    square = lax.map(square_row, window)

    def cube_row(pair):
        return row_product(pair[0], columns[pair[1]], counts[pair[1]], blocks, columns, counts)

    cube_part = lax.map(cube_row, (square, window))
    return 3.0 * square - 2.0 * cube_part
```

```python
import functools

import jax
import jax.numpy as jnp
from jax import lax
from jax.experimental import pallas as pl
from jax.experimental.pallas import tpu as pltpu
from jax.sharding import PartitionSpec as P

MESH = pl.DeviceIdType.MESH
LANES = 128
SHORT = 2
SHORT_DIAG = 6
HEAD = 2


def position():
    return lax.axis_index("row"), lax.axis_index("col"), lax.axis_index("depth")


def meta_kernel(rows, cols, depths, meta_ref, all_ref, send_sem, recv_sem, own_sem):
    r, c, d = position()
    devices = rows * cols * depths
    me = (r * depths + d) * cols + c

    def target(other):
        q = other // cols
        return (q // depths, other % cols, q % depths)

    barrier = pltpu.get_barrier_semaphore()

    @pl.loop(1, devices)
    def _(off):
        pl.semaphore_signal(barrier, inc=1, device_id=target((me + off) % devices), device_id_type=MESH)

    own = pltpu.make_async_copy(meta_ref, all_ref.at[me], own_sem)
    own.start()
    pl.semaphore_wait(barrier, devices - 1)

    def copy(slot, other):
        return pltpu.make_async_remote_copy(
            src_ref=meta_ref,
            dst_ref=all_ref.at[slot],
            send_sem=send_sem.at[other],
            recv_sem=recv_sem.at[slot],
            device_id=target(other),
            device_id_type=MESH,
        )

    @pl.loop(1, devices)
    def _(off):
        copy(me, (me + off) % devices).start()

    own.wait()

    @pl.loop(1, devices)
    def _(off):
        other = (me + off) % devices
        copy(other, other).wait_recv()
        copy(me, other).wait_send()


def gather_meta(meta, sizes):
    devices = sizes[0] * sizes[1] * sizes[2]
    return pl.pallas_call(
        functools.partial(meta_kernel, *sizes),
        out_shape=jax.ShapeDtypeStruct((devices, 1, LANES), jnp.int32),
        in_specs=[pl.BlockSpec(memory_space=pltpu.VMEM)],
        out_specs=pl.BlockSpec(memory_space=pltpu.VMEM),
        scratch_shapes=[
            pltpu.SemaphoreType.DMA((devices,)),
            pltpu.SemaphoreType.DMA((devices,)),
            pltpu.SemaphoreType.DMA,
        ],
        compiler_params=pltpu.CompilerParams(collective_id=0, has_side_effects=True),
    )(meta)


def pack_kernel(sizes, dims, win_ref, cols_ref, blocks_ref, pack_ref, codes_ref, sems):
    rows, cols, depths = sizes
    local_rows, panels, slots = dims
    window = rows * depths
    most = slots * slots * panels
    r, c, d = position()
    me_q = r * depths + d
    owner = d // panels
    left_panel = d % panels
    diag = owner == c
    limit = jnp.where(diag, min(SHORT_DIAG, most), min(SHORT, most))
    counts_at = local_rows * panels * slots

    def entry(q, n, row, panel, slot):
        return pltpu.make_async_copy(
            blocks_ref.at[row, panel, slot], pack_ref.at[q, n], sems.at[q]
        )

    def pack_row(q, too_long):
        left_at = q * cols + owner
        out_at = q * cols + c
        left_count = win_ref[left_at, panels * slots + left_panel]

        def left_step(a, n):
            place = win_ref[left_at, left_panel * slots + a]
            row = place % local_rows

            def panel_step(panel, n):
                out_count = win_ref[out_at, panels * slots + panel]
                inner_count = cols_ref[counts_at + row * panels + panel]

                def inner_step(t, n):
                    column = cols_ref[(row * panels + panel) * slots + t]

                    def out_step(s, n):
                        hit = win_ref[out_at, panel * slots + s] == column

                        @pl.when(hit)
                        def _():
                            entry(q, n, row, panel, t).start()
                            codes_ref[q, 0, HEAD + n] = a * (panels * slots) + panel * slots + s

                        return n + hit.astype(jnp.int32)

                    return lax.fori_loop(0, out_count, out_step, n)

                return lax.fori_loop(0, inner_count, inner_step, n)

            mine = place // local_rows == r
            return lax.fori_loop(0, jnp.where(mine, panels, 0), panel_step, n)

        n = lax.fori_loop(0, left_count, left_step, jnp.int32(0))
        codes_ref[q, 0, 0] = n
        return too_long | ((n > limit) & (q != me_q)).astype(jnp.int32)

    too_long = lax.fori_loop(0, window, pack_row, jnp.int32(0))

    @pl.loop(0, window)
    def _(q):
        codes_ref[q, 0, 1] = too_long

        @pl.loop(0, codes_ref[q, 0, 0])
        def _(n):
            entry(q, 0, 0, 0, 0).wait()


def pack_lists(win, cols, blocks, sizes):
    local_rows, panels, slots, size, _ = blocks.shape
    window = sizes[0] * sizes[2]
    most = slots * slots * panels
    return pl.pallas_call(
        functools.partial(pack_kernel, sizes, (local_rows, panels, slots)),
        out_shape=(
            jax.ShapeDtypeStruct((window, most, size, size), jnp.float32),
            jax.ShapeDtypeStruct((window, 1, LANES), jnp.int32),
        ),
        in_specs=[
            pl.BlockSpec(memory_space=pltpu.SMEM),
            pl.BlockSpec(memory_space=pltpu.SMEM),
            pl.BlockSpec(memory_space=pl.ANY),
        ],
        out_specs=(pl.BlockSpec(memory_space=pl.ANY), pl.BlockSpec(memory_space=pltpu.SMEM)),
        scratch_shapes=[pltpu.SemaphoreType.DMA((window,))],
    )(win, cols, blocks)


def exchange_kernel(
    sizes, panels, short, short_diag, pack_ref, codes_ref, left_ref,
    got_ref, got_codes_ref, lefts_ref,
    send_sem, recv_sem, left_send, left_recv, own_sem,
):
    rows, cols, depths = sizes
    window = rows * depths
    most = pack_ref.shape[1]
    r, c, d = position()
    me = r * depths + d

    barrier = pltpu.get_barrier_semaphore()

    @pl.loop(1, window)
    def _(off):
        q = (me + off) % window
        pl.semaphore_signal(barrier, inc=1, device_id=(q // depths, c, q % depths), device_id_type=MESH)

    @pl.loop(1, cols)
    def _(off):
        pl.semaphore_signal(barrier, inc=1, device_id=(r, (c + off) % cols, d), device_id_type=MESH)

    own = [
        pltpu.make_async_copy(pack_ref.at[me], got_ref.at[me], own_sem.at[0]),
        pltpu.make_async_copy(codes_ref.at[me], got_codes_ref.at[me], own_sem.at[1]),
        pltpu.make_async_copy(left_ref, lefts_ref.at[c], own_sem.at[2]),
    ]
    for copy in own:
        copy.start()
    pl.semaphore_wait(barrier, window - 1 + cols - 1)

    def left_copy(slot, other):
        return pltpu.make_async_remote_copy(
            src_ref=left_ref,
            dst_ref=lefts_ref.at[slot],
            send_sem=left_send.at[other],
            recv_sem=left_recv.at[slot],
            device_id=(r, other, d),
            device_id_type=MESH,
        )

    def list_copy(kind, slot, other):
        if kind == 0:
            src, dst = codes_ref.at[other], got_codes_ref.at[slot]
        elif kind == 1:
            src = pack_ref.at[other, pl.ds(0, short)]
            dst = got_ref.at[slot, pl.ds(0, short)]
        else:
            src = pack_ref.at[other, pl.ds(short, short_diag - short)]
            dst = got_ref.at[slot, pl.ds(short, short_diag - short)]
        return pltpu.make_async_remote_copy(
            src_ref=src,
            dst_ref=dst,
            send_sem=send_sem.at[kind, other],
            recv_sem=recv_sem.at[kind, slot],
            device_id=(other // depths, c, other % depths),
            device_id_type=MESH,
        )

    @pl.loop(1, cols)
    def _(off):
        left_copy(c, (c + off) % cols).start()

    @pl.loop(1, window)
    def _(off):
        other = (me + off) % window
        list_copy(0, me, other).start()
        list_copy(1, me, other).start()
        if short_diag > short:
            @pl.when(d // panels == c)
            def _():
                list_copy(2, me, other).start()

    for copy in own:
        copy.wait()

    @pl.loop(1, cols)
    def _(off):
        other = (c + off) % cols
        left_copy(other, other).wait_recv()
        left_copy(c, other).wait_send()

    @pl.loop(1, window)
    def _(off):
        other = (me + off) % window
        list_copy(0, other, other).wait_recv()
        list_copy(0, me, other).wait_send()
        list_copy(1, other, other).wait_recv()
        list_copy(1, me, other).wait_send()
        if short_diag > short:
            @pl.when((other % depths) // panels == c)
            def _():
                list_copy(2, other, other).wait_recv()

            @pl.when(d // panels == c)
            def _():
                list_copy(2, me, other).wait_send()


def exchange(pack, codes, left, sizes, panels, short, short_diag, ident):
    window, most, size, _ = pack.shape
    cols = sizes[1]
    anywhere = pl.BlockSpec(memory_space=pl.ANY)
    return pl.pallas_call(
        functools.partial(exchange_kernel, sizes, panels, min(short, most), min(short_diag, most)),
        out_shape=(
            jax.ShapeDtypeStruct(pack.shape, jnp.float32),
            jax.ShapeDtypeStruct(codes.shape, jnp.int32),
            jax.ShapeDtypeStruct((cols,) + left.shape, jnp.float32),
        ),
        in_specs=[anywhere] * 3,
        out_specs=(anywhere,) * 3,
        scratch_shapes=[
            pltpu.SemaphoreType.DMA((3, window)),
            pltpu.SemaphoreType.DMA((3, window)),
            pltpu.SemaphoreType.DMA((cols,)),
            pltpu.SemaphoreType.DMA((cols,)),
            pltpu.SemaphoreType.DMA((3,)),
        ],
        compiler_params=pltpu.CompilerParams(collective_id=ident, has_side_effects=True),
    )(pack, codes, left)


def multiply_into(acc_ref, lefts_ref, got_ref, codes_ref, held, sems, depths, slots):
    window, most = got_ref.shape[:2]
    out_slots = acc_ref.shape[0]

    def fetch(q, n):
        return pltpu.make_async_copy(got_ref.at[q, n], held.at[q, n], sems.at[q, n])

    @pl.loop(0, window)
    def _(q):
        @pl.loop(0, codes_ref[q, 0, 0])
        def _(n):
            fetch(q, n).start()

    acc_ref[...] = jnp.zeros_like(acc_ref)

    @pl.loop(0, window)
    def _(q):
        @pl.loop(0, codes_ref[q, 0, 0])
        def _(n):
            fetch(q, n).wait()
            code = codes_ref[q, 0, HEAD + n]
            place = (q % depths) * slots + code // out_slots
            s = code % out_slots
            acc_ref[s] += jnp.dot(
                lefts_ref[place],
                held[q, n],
                precision=lax.Precision.HIGHEST,
                preferred_element_type=jnp.float32,
            )


def square_kernel(depths, slots, codes_ref, got_ref, lefts_ref, out_ref, flag_ref, held, sems):
    window = got_ref.shape[0]

    flag_ref[0, 0] = lax.fori_loop(
        0, window, lambda q, f: f | codes_ref[q, 0, 1], jnp.int32(0)
    )
    multiply_into(out_ref, lefts_ref, got_ref, codes_ref, held, sems, depths, slots)


def cube_kernel(depths, slots, codes_ref, got_ref, lefts_ref, square_ref, out_ref, held, sems):
    multiply_into(out_ref, lefts_ref, got_ref, codes_ref, held, sems, depths, slots)
    out_ref[...] = 3.0 * square_ref[...] - 2.0 * out_ref[...]


def local_product(kernel, codes, got, lefts, extra, out_shape, out_specs):
    vmem = pl.BlockSpec(memory_space=pltpu.VMEM)
    return pl.pallas_call(
        kernel,
        out_shape=out_shape,
        in_specs=[
            pl.BlockSpec(memory_space=pltpu.SMEM),
            pl.BlockSpec(memory_space=pl.ANY),
            vmem,
        ] + [vmem] * len(extra),
        out_specs=out_specs,
        scratch_shapes=[
            pltpu.VMEM(got.shape, jnp.float32),
            pltpu.SemaphoreType.DMA(got.shape[:2]),
        ],
        compiler_params=pltpu.CompilerParams(vmem_limit_bytes=32 << 20),
    )(codes, got, lefts, *extra)


def gather_kernel(cols, square_ref, flag_ref, squares_ref, flags_ref, send_sem, recv_sem, own_sem):
    r, c, d = position()
    barrier = pltpu.get_barrier_semaphore()

    @pl.loop(1, cols)
    def _(off):
        pl.semaphore_signal(barrier, inc=1, device_id=(r, (c + off) % cols, d), device_id_type=MESH)

    pairs = ((square_ref, squares_ref), (flag_ref, flags_ref))
    own = [
        pltpu.make_async_copy(src, dst.at[c], own_sem.at[i]) for i, (src, dst) in enumerate(pairs)
    ]
    for copy in own:
        copy.start()
    pl.semaphore_wait(barrier, cols - 1)

    def copies(slot, other):
        return [
            pltpu.make_async_remote_copy(
                src_ref=src,
                dst_ref=dst.at[slot],
                send_sem=send_sem.at[i, other],
                recv_sem=recv_sem.at[i, slot],
                device_id=(r, other, d),
                device_id_type=MESH,
            )
            for i, (src, dst) in enumerate(pairs)
        ]

    @pl.loop(1, cols)
    def _(off):
        for copy in copies(c, (c + off) % cols):
            copy.start()

    for copy in own:
        copy.wait()

    @pl.loop(1, cols)
    def _(off):
        other = (c + off) % cols
        for copy in copies(other, other):
            copy.wait_recv()
        for copy in copies(c, other):
            copy.wait_send()


def gather_square(square, flag, cols, ident):
    anywhere = pl.BlockSpec(memory_space=pl.ANY)
    return pl.pallas_call(
        functools.partial(gather_kernel, cols),
        out_shape=(
            jax.ShapeDtypeStruct((cols,) + square.shape, jnp.float32),
            jax.ShapeDtypeStruct((cols,) + flag.shape, jnp.int32),
        ),
        in_specs=[anywhere] * 2,
        out_specs=(anywhere,) * 2,
        scratch_shapes=[
            pltpu.SemaphoreType.DMA((2, cols)),
            pltpu.SemaphoreType.DMA((2, cols)),
            pltpu.SemaphoreType.DMA((2,)),
        ],
        compiler_params=pltpu.CompilerParams(collective_id=ident, has_side_effects=True),
    )(square, flag)


def body(sizes, blocks, columns, counts):
    rows, cols, depths = sizes
    local_rows, panels, slots, size, _ = blocks.shape
    most = slots * slots * panels
    out_slots = panels * slots
    meta = jnp.concatenate([columns[0].reshape(-1), counts[0].reshape(-1)])
    meta = jnp.pad(meta, (0, LANES - meta.shape[0]))[None, :]
    win = gather_meta(meta, sizes)[:, 0, :]
    local = jnp.concatenate([columns.reshape(-1), counts.reshape(-1)])
    pack, codes = pack_lists(win, local, blocks, sizes)
    left = blocks[0].reshape(out_slots, size, size)
    block_shape = jax.ShapeDtypeStruct((out_slots, size, size), jnp.float32)
    vmem = pl.BlockSpec(memory_space=pltpu.VMEM)

    def square_step(short, short_diag, ident):
        got, got_codes, lefts = exchange(
            pack, codes, left, sizes, panels, short, short_diag, ident
        )
        room = jnp.full((rows, depths), min(short, most), jnp.int32)
        at = jnp.arange(depths, dtype=jnp.int32)[None, :] // panels == lax.axis_index("col")
        room = jnp.where(at, min(short_diag, most), room)
        is_me = (jnp.arange(rows)[:, None] == lax.axis_index("row")) & (
            jnp.arange(depths)[None, :] == lax.axis_index("depth")
        )
        room = jnp.where(is_me, most, room).reshape(-1, 1, 1)
        head = jnp.arange(LANES)[None, None, :] == 0
        got_codes = jnp.where(head, jnp.minimum(got_codes, room), got_codes)
        square, flag = local_product(
            functools.partial(square_kernel, depths, slots),
            got_codes, got, lefts.reshape(cols * out_slots, size, size), (),
            (block_shape, jax.ShapeDtypeStruct((1, LANES), jnp.int32)),
            (vmem, pl.BlockSpec(memory_space=pltpu.SMEM)),
        )
        squares, flags = gather_square(square, flag, cols, ident + 1)
        return got, got_codes, square, squares, flags

    def cube_step(got, got_codes, square, squares):
        return local_product(
            functools.partial(cube_kernel, depths, slots),
            got_codes, got, squares.reshape(cols * out_slots, size, size), (square,),
            block_shape, vmem,
        )

    got, got_codes, square, squares, flags = square_step(SHORT, SHORT_DIAG, 1)
    too_long = jnp.any(flags[:, 0, 0] != 0)

    def again():
        got, got_codes, square, squares, _ = square_step(most, most, 3)
        return cube_step(got, got_codes, square, squares)

    out = lax.cond(
        too_long, again, lambda: cube_step(got, got_codes, square, squares)
    )
    return out.reshape(1, panels, slots, size, size)


def solution(mesh):
    placed = (
        P(("row", "depth"), "col", None, None, None),
        P(("row", "depth"), "col", None),
        P(("row", "depth"), "col"),
    )
    sizes = (mesh.shape["row"], mesh.shape["col"], mesh.shape["depth"])
    return jax.shard_map(
        functools.partial(body, sizes),
        mesh=mesh,
        in_specs=placed,
        out_specs=P(("row", "depth"), "col", None, None, None),
        check_vma=False,
    )
```

```python
import functools

import jax
import jax.numpy as jnp
from jax import lax
from jax.experimental import pallas as pl
from jax.experimental.pallas import tpu as pltpu
from jax.sharding import PartitionSpec as P

MESH = pl.DeviceIdType.MESH
LANES = 128
VMEM_LIMIT = 48 << 20
SHORT = 2
SHORT_DIAG = 6
HEAD = 2
SOURCE = LANES // 2


def position():
    return lax.axis_index("row"), lax.axis_index("col"), lax.axis_index("depth")


def meta_kernel(sizes, panels, local_ref, all_ref, send_sem, recv_sem, own_sem):
    rows, cols, depths = sizes
    window = rows * depths
    r, c, d = position()
    me_q = r * depths + d
    owner = d // panels
    meta_ref = local_ref.at[0]

    def column_mate(off):
        q = (me_q + off) % window
        return q, c

    def inner_mate(i):
        col = (c + 1 + i // (rows * panels)) % cols
        row = (i // panels) % rows
        return row * depths + c * panels + i % panels, col

    def left_source(i):
        return i, owner

    mates = window - 1
    inner = rows * panels * (cols - 1)
    sources = jnp.where(owner == c, 0, window)

    def device(q, col):
        return (q // depths, col, q % depths)

    barrier = pltpu.get_barrier_semaphore()

    def greet(q, col):
        pl.semaphore_signal(barrier, inc=1, device_id=device(q, col), device_id_type=MESH)

    @pl.loop(1, window)
    def _(off):
        greet(*column_mate(off))

    @pl.loop(0, sources)
    def _(i):
        greet(*left_source(i))

    own = pltpu.make_async_copy(meta_ref, all_ref.at[me_q * cols + c], own_sem)
    own.start()
    pl.semaphore_wait(barrier, mates + inner)

    def copy(slot, q, col):
        return pltpu.make_async_remote_copy(
            src_ref=meta_ref,
            dst_ref=all_ref.at[slot],
            send_sem=send_sem.at[q * cols + col],
            recv_sem=recv_sem.at[slot],
            device_id=device(q, col),
            device_id_type=MESH,
        )

    me = me_q * cols + c

    @pl.loop(0, inner)
    def _(i):
        copy(me, *inner_mate(i)).start()

    @pl.loop(1, window)
    def _(off):
        copy(me, *column_mate(off)).start()

    own.wait()

    @pl.loop(1, window)
    def _(off):
        q, col = column_mate(off)
        copy(q * cols + col, q, col).wait_recv()
        copy(me, q, col).wait_send()

    @pl.loop(0, sources)
    def _(i):
        q, col = left_source(i)
        copy(q * cols + col, q, col).wait_recv()

    @pl.loop(0, inner)
    def _(i):
        copy(me, *inner_mate(i)).wait_send()


def gather_meta(local, sizes, panels):
    devices = sizes[0] * sizes[1] * sizes[2]
    return pl.pallas_call(
        functools.partial(meta_kernel, sizes, panels),
        out_shape=jax.ShapeDtypeStruct((devices, 1, LANES), jnp.int32),
        in_specs=[pl.BlockSpec(memory_space=pltpu.VMEM)],
        out_specs=pl.BlockSpec(memory_space=pltpu.VMEM),
        scratch_shapes=[
            pltpu.SemaphoreType.DMA((devices,)),
            pltpu.SemaphoreType.DMA((devices,)),
            pltpu.SemaphoreType.DMA,
        ],
        compiler_params=pltpu.CompilerParams(collective_id=0, has_side_effects=True),
    )(local)


def pack_kernel(sizes, dims, short, win_ref, local_ref, blocks_ref, pack_ref, codes_ref, sem):
    rows, cols, depths = sizes
    local_rows, panels, slots = dims
    window = rows * depths
    capacity = pack_ref.shape[1]
    r, c, d = position()
    me_q = r * depths + d
    owner = d // panels
    left_panel = d % panels
    counts_at = panels * slots
    limit = jnp.where(owner == c, capacity, short)

    def entry(q, n, row, panel, slot):
        return pltpu.make_async_copy(blocks_ref.at[row, panel, slot], pack_ref.at[q, n], sem)

    def pack_row(q, carry):
        too_long, copies = carry
        left_at = q * cols + owner
        out_at = q * cols + c
        left_count = win_ref[left_at, 0, counts_at + left_panel]
        room = jnp.where(q == me_q, 0, limit)

        def left_step(a, n):
            place = win_ref[left_at, 0, left_panel * slots + a]
            row = place % local_rows

            def panel_step(panel, n):
                out_count = win_ref[out_at, 0, counts_at + panel]
                inner_count = local_ref[row, 0, counts_at + panel]

                def inner_step(t, n):
                    column = local_ref[row, 0, panel * slots + t]

                    def out_step(s, n):
                        hit = win_ref[out_at, 0, panel * slots + s] == column

                        @pl.when(hit)
                        def _():
                            codes_ref[q, 0, HEAD + n] = a * counts_at + panel * slots + s
                            codes_ref[q, 0, SOURCE + n] = (row * panels + panel) * slots + t

                        @pl.when(hit & (n < room))
                        def _():
                            entry(q, n, row, panel, t).start()

                        return n + hit.astype(jnp.int32)

                    return lax.fori_loop(0, out_count, out_step, n)

                return lax.fori_loop(0, inner_count, inner_step, n)

            mine = place // local_rows == r
            return lax.fori_loop(0, jnp.where(mine, panels, 0), panel_step, n)

        n = lax.fori_loop(0, left_count, left_step, jnp.int32(0))
        codes_ref[q, 0, 0] = n
        over = ((n > limit) & (q != me_q)).astype(jnp.int32)
        return too_long | over, copies + jnp.minimum(n, room)

    zero = jnp.int32(0)
    too_long, copies = lax.fori_loop(0, window, pack_row, (zero, zero))

    @pl.loop(0, window)
    def _(q):
        codes_ref[q, 0, 1] = too_long

    @pl.loop(0, copies)
    def _(n):
        entry(0, 0, 0, 0, 0).wait()


def pack_lists(win, local, blocks, sizes, short, capacity):
    local_rows, panels, slots, size, _ = blocks.shape
    window = sizes[0] * sizes[2]
    return pl.pallas_call(
        functools.partial(pack_kernel, sizes, (local_rows, panels, slots), short),
        out_shape=(
            jax.ShapeDtypeStruct((window, capacity, size, size), jnp.float32),
            jax.ShapeDtypeStruct((window, 1, LANES), jnp.int32),
        ),
        in_specs=[
            pl.BlockSpec(memory_space=pltpu.SMEM),
            pl.BlockSpec(memory_space=pltpu.SMEM),
            pl.BlockSpec(memory_space=pltpu.HBM),
        ],
        out_specs=(pl.BlockSpec(memory_space=pltpu.VMEM), pl.BlockSpec(memory_space=pltpu.SMEM)),
        scratch_shapes=[pltpu.SemaphoreType.DMA],
        compiler_params=pltpu.CompilerParams(vmem_limit_bytes=VMEM_LIMIT),
    )(win, local, blocks)


def exchange_kernel(
    sizes, panels, short, pack_ref, codes_ref, blocks_ref,
    got_ref, got_codes_ref, lefts_ref,
    send_sem, recv_sem, left_send, left_recv, own_sem,
):
    rows, cols, depths = sizes
    window = rows * depths
    short_diag = pack_ref.shape[1]
    left_ref = blocks_ref.at[0]
    r, c, d = position()
    me = r * depths + d

    barrier = pltpu.get_barrier_semaphore()

    @pl.loop(1, window)
    def _(off):
        q = (me + off) % window
        pl.semaphore_signal(barrier, inc=1, device_id=(q // depths, c, q % depths), device_id_type=MESH)

    @pl.loop(1, cols)
    def _(off):
        pl.semaphore_signal(barrier, inc=1, device_id=(r, (c + off) % cols, d), device_id_type=MESH)

    own = [
        pltpu.make_async_copy(codes_ref.at[me], got_codes_ref.at[me], own_sem.at[0]),
        pltpu.make_async_copy(left_ref, lefts_ref.at[c], own_sem.at[1]),
    ]
    for copy in own:
        copy.start()
    pl.semaphore_wait(barrier, window - 1 + cols - 1)

    def left_copy(slot, other):
        return pltpu.make_async_remote_copy(
            src_ref=left_ref,
            dst_ref=lefts_ref.at[slot],
            send_sem=left_send.at[other],
            recv_sem=left_recv.at[slot],
            device_id=(r, other, d),
            device_id_type=MESH,
        )

    def list_copy(kind, slot, other):
        if kind == 0:
            src, dst = codes_ref.at[other], got_codes_ref.at[slot]
        elif kind == 1:
            src = pack_ref.at[other, pl.ds(0, short)]
            dst = got_ref.at[slot, pl.ds(0, short)]
        else:
            src = pack_ref.at[other, pl.ds(short, short_diag - short)]
            dst = got_ref.at[slot, pl.ds(short, short_diag - short)]
        return pltpu.make_async_remote_copy(
            src_ref=src,
            dst_ref=dst,
            send_sem=send_sem.at[kind, other],
            recv_sem=recv_sem.at[kind, slot],
            device_id=(other // depths, c, other % depths),
            device_id_type=MESH,
        )

    @pl.loop(1, cols)
    def _(off):
        left_copy(c, (c + off) % cols).start()

    @pl.loop(1, window)
    def _(off):
        other = (me + off) % window
        list_copy(0, me, other).start()
        list_copy(1, me, other).start()
        if short_diag > short:
            @pl.when(d // panels == c)
            def _():
                list_copy(2, me, other).start()

    for copy in own:
        copy.wait()

    @pl.loop(1, cols)
    def _(off):
        other = (c + off) % cols
        left_copy(other, other).wait_recv()
        left_copy(c, other).wait_send()

    @pl.loop(1, window)
    def _(off):
        other = (me + off) % window
        list_copy(0, other, other).wait_recv()
        list_copy(0, me, other).wait_send()
        list_copy(1, other, other).wait_recv()
        list_copy(1, me, other).wait_send()
        if short_diag > short:
            @pl.when((other % depths) // panels == c)
            def _():
                list_copy(2, other, other).wait_recv()

            @pl.when(d // panels == c)
            def _():
                list_copy(2, me, other).wait_send()


def exchange(pack, codes, blocks, sizes, short, ident):
    window = pack.shape[0]
    cols = sizes[1]
    panels = blocks.shape[1]
    vmem = pl.BlockSpec(memory_space=pltpu.VMEM)
    return pl.pallas_call(
        functools.partial(exchange_kernel, sizes, panels, short),
        out_shape=(
            jax.ShapeDtypeStruct(pack.shape, jnp.float32),
            jax.ShapeDtypeStruct(codes.shape, jnp.int32),
            jax.ShapeDtypeStruct((cols,) + blocks.shape[1:], jnp.float32),
        ),
        in_specs=[vmem, vmem, pl.BlockSpec(memory_space=pltpu.HBM)],
        out_specs=(vmem,) * 3,
        scratch_shapes=[
            pltpu.SemaphoreType.DMA((3, window)),
            pltpu.SemaphoreType.DMA((3, window)),
            pltpu.SemaphoreType.DMA((cols,)),
            pltpu.SemaphoreType.DMA((cols,)),
            pltpu.SemaphoreType.DMA((2,)),
        ],
        compiler_params=pltpu.CompilerParams(
            collective_id=ident, has_side_effects=True, vmem_limit_bytes=VMEM_LIMIT
        ),
    )(pack, codes, blocks)


def multiply_into(acc_ref, lefts_ref, got_ref, blocks_ref, codes_ref, held, sems, sizes, short):
    rows, cols, depths = sizes
    window, capacity = got_ref.shape[:2]
    panels, slots = blocks_ref.shape[1:3]
    out_slots = panels * slots
    r, c, d = position()
    me_q = r * depths + d
    own = codes_ref[me_q, 0, 0]

    def fetch(n):
        at = codes_ref[me_q, 0, SOURCE + n]
        row = at // out_slots
        block = blocks_ref.at[row, (at // slots) % panels, at % slots]
        return pltpu.make_async_copy(block, held.at[n], sems.at[n])

    @pl.loop(0, own)
    def _(n):
        fetch(n).start()

    acc_ref[...] = jnp.zeros_like(acc_ref)

    def add(q, n, right):
        code = codes_ref[q, 0, HEAD + n]
        depth = q % depths
        left = lefts_ref[depth // panels, depth % panels, code // out_slots]
        s = code % out_slots
        acc_ref[s // slots, s % slots] += jnp.dot(
            left, right, precision=lax.Precision.HIGHEST, preferred_element_type=jnp.float32
        )

    @pl.loop(0, window)
    def _(q):
        room = jnp.where((q % depths) // panels == c, capacity, short)
        room = jnp.where(q == me_q, 0, room)

        @pl.loop(0, jnp.minimum(codes_ref[q, 0, 0], room))
        def _(n):
            add(q, n, got_ref[q, n])

    @pl.loop(0, own)
    def _(n):
        fetch(n).wait()
        add(me_q, n, held[n])


def square_kernel(
    sizes, short, codes_ref, got_ref, blocks_ref, lefts_ref, out_ref, flag_ref, held, sems
):
    flag_ref[0, 0] = lax.fori_loop(
        0, got_ref.shape[0], lambda q, f: f | codes_ref[q, 0, 1], jnp.int32(0)
    )
    multiply_into(out_ref, lefts_ref, got_ref, blocks_ref, codes_ref, held, sems, sizes, short)


def cube_kernel(
    sizes, short, codes_ref, got_ref, blocks_ref, lefts_ref, square_ref, out_ref, held, sems
):
    multiply_into(out_ref, lefts_ref, got_ref, blocks_ref, codes_ref, held, sems, sizes, short)
    out_ref[...] = 3.0 * square_ref[...] - 2.0 * out_ref[...]


def local_product(kernel, codes, got, blocks, lefts, extra, out_shape, out_specs):
    vmem = pl.BlockSpec(memory_space=pltpu.VMEM)
    _, panels, slots, size, _ = blocks.shape
    most = slots * slots * panels
    return pl.pallas_call(
        kernel,
        out_shape=out_shape,
        in_specs=[
            pl.BlockSpec(memory_space=pltpu.SMEM),
            vmem,
            pl.BlockSpec(memory_space=pltpu.HBM),
            vmem,
        ] + [vmem] * len(extra),
        out_specs=out_specs,
        scratch_shapes=[
            pltpu.VMEM((most, size, size), jnp.float32),
            pltpu.SemaphoreType.DMA((most,)),
        ],
        compiler_params=pltpu.CompilerParams(vmem_limit_bytes=VMEM_LIMIT),
    )(codes, got, blocks, lefts, *extra)


def gather_kernel(cols, square_ref, flag_ref, squares_ref, flags_ref, send_sem, recv_sem, own_sem):
    r, c, d = position()
    barrier = pltpu.get_barrier_semaphore()

    @pl.loop(1, cols)
    def _(off):
        pl.semaphore_signal(barrier, inc=1, device_id=(r, (c + off) % cols, d), device_id_type=MESH)

    pairs = ((square_ref, squares_ref), (flag_ref, flags_ref))
    own = [
        pltpu.make_async_copy(src, dst.at[c], own_sem.at[i]) for i, (src, dst) in enumerate(pairs)
    ]
    for copy in own:
        copy.start()
    pl.semaphore_wait(barrier, cols - 1)

    def copies(slot, other):
        return [
            pltpu.make_async_remote_copy(
                src_ref=src,
                dst_ref=dst.at[slot],
                send_sem=send_sem.at[i, other],
                recv_sem=recv_sem.at[i, slot],
                device_id=(r, other, d),
                device_id_type=MESH,
            )
            for i, (src, dst) in enumerate(pairs)
        ]

    @pl.loop(1, cols)
    def _(off):
        for copy in copies(c, (c + off) % cols):
            copy.start()

    for copy in own:
        copy.wait()

    @pl.loop(1, cols)
    def _(off):
        other = (c + off) % cols
        for copy in copies(other, other):
            copy.wait_recv()
        for copy in copies(c, other):
            copy.wait_send()


def gather_square(square, flag, cols, ident):
    vmem = pl.BlockSpec(memory_space=pltpu.VMEM)
    return pl.pallas_call(
        functools.partial(gather_kernel, cols),
        out_shape=(
            jax.ShapeDtypeStruct((cols,) + square.shape, jnp.float32),
            jax.ShapeDtypeStruct((cols,) + flag.shape, jnp.int32),
        ),
        in_specs=[vmem] * 2,
        out_specs=(vmem,) * 2,
        scratch_shapes=[
            pltpu.SemaphoreType.DMA((2, cols)),
            pltpu.SemaphoreType.DMA((2, cols)),
            pltpu.SemaphoreType.DMA((2,)),
        ],
        compiler_params=pltpu.CompilerParams(collective_id=ident, has_side_effects=True),
    )(square, flag)


def body(sizes, blocks, columns, counts):
    rows, cols, depths = sizes
    local_rows, panels, slots, size, _ = blocks.shape
    most = slots * slots * panels
    local = jnp.concatenate([columns.reshape(local_rows, 1, panels * slots), counts[:, None, :]], 2)
    local = jnp.pad(local, ((0, 0), (0, 0), (0, LANES - local.shape[2])))
    win = gather_meta(local, sizes, panels)
    block_shape = jax.ShapeDtypeStruct(blocks.shape[1:], jnp.float32)
    vmem = pl.BlockSpec(memory_space=pltpu.VMEM)

    def square_step(short, capacity, ident):
        pack, codes = pack_lists(win, local, blocks, sizes, short, capacity)
        got, got_codes, lefts = exchange(pack, codes, blocks, sizes, short, ident)
        square, flag = local_product(
            functools.partial(square_kernel, sizes, short),
            got_codes, got, blocks, lefts, (),
            (block_shape, jax.ShapeDtypeStruct((1, LANES), jnp.int32)),
            (vmem, pl.BlockSpec(memory_space=pltpu.SMEM)),
        )
        squares, flags = gather_square(square, flag, cols, ident + 1)
        return got, got_codes, square, squares, flags

    def cube_step(short, got, got_codes, square, squares):
        return local_product(
            functools.partial(cube_kernel, sizes, short),
            got_codes, got, blocks, squares, (square,), block_shape, vmem,
        )

    short = min(SHORT, most)
    *lists, flags = square_step(short, min(SHORT_DIAG, most), 1)

    def again():
        *lists, _ = square_step(most, most, 3)
        return cube_step(most, *lists)

    out = lax.cond(jnp.any(flags[:, 0, 0] != 0), again, lambda: cube_step(short, *lists))
    return out[None]


def solution(mesh):
    placed = (
        P(("row", "depth"), "col", None, None, None),
        P(("row", "depth"), "col", None),
        P(("row", "depth"), "col"),
    )
    sizes = (mesh.shape["row"], mesh.shape["col"], mesh.shape["depth"])
    return jax.shard_map(
        functools.partial(body, sizes),
        mesh=mesh,
        in_specs=placed,
        out_specs=P(("row", "depth"), "col", None, None, None),
        check_vma=False,
    )
```

```python
import functools

import jax
import jax.numpy as jnp
from jax import lax
from jax.experimental import pallas as pl
from jax.experimental.pallas import tpu as pltpu
from jax.sharding import PartitionSpec as P

MESH = pl.DeviceIdType.MESH
LANES = 128
VMEM_LIMIT = 48 << 20
SHORT = 2
SHORT_DIAG = 6
HEAD = 2
SOURCE = LANES // 2


def position():
    return lax.axis_index("row"), lax.axis_index("col"), lax.axis_index("depth")


def meta_kernel(
    sizes, panels, local_ref, all_ref, sibling_ref, send_sem, recv_sem, own_sem, swap_sems
):
    rows, cols, depths = sizes
    window = rows * depths
    r, c, d = position()
    me_q = r * depths + d
    owner = d // panels
    meta_ref = local_ref.at[0]

    def column_mate(off):
        q = (me_q + off) % window
        return q, c

    def inner_mate(i):
        col = (c + 1 + i // (rows * panels)) % cols
        row = (i // panels) % rows
        return row * depths + c * panels + i % panels, col

    def left_source(i):
        return i, owner

    mates = window - 1
    inner = rows * panels * (cols - 1)
    sources = jnp.where(owner == c, 0, window)

    def device(q, col):
        return (q // depths, col, q % depths)

    barrier = pltpu.get_barrier_semaphore()

    def greet(q, col):
        pl.semaphore_signal(barrier, inc=1, device_id=device(q, col), device_id_type=MESH)

    @pl.loop(1, window)
    def _(off):
        greet(*column_mate(off))

    @pl.loop(0, sources)
    def _(i):
        greet(*left_source(i))

    own = pltpu.make_async_copy(meta_ref, all_ref.at[me_q * cols + c], own_sem)
    own.start()
    pl.semaphore_wait(barrier, mates + inner)

    def copy(slot, q, col):
        return pltpu.make_async_remote_copy(
            src_ref=meta_ref,
            dst_ref=all_ref.at[slot],
            send_sem=send_sem.at[q * cols + col],
            recv_sem=recv_sem.at[slot],
            device_id=device(q, col),
            device_id_type=MESH,
        )

    me = me_q * cols + c
    swap = pltpu.make_async_remote_copy(
        src_ref=local_ref,
        dst_ref=sibling_ref,
        send_sem=swap_sems.at[0],
        recv_sem=swap_sems.at[1],
        device_id=(1 - r, c, d),
        device_id_type=MESH,
    )

    @pl.loop(0, inner)
    def _(i):
        copy(me, *inner_mate(i)).start()

    @pl.loop(1, window)
    def _(off):
        copy(me, *column_mate(off)).start()

    swap.start()
    own.wait()

    @pl.loop(1, window)
    def _(off):
        q, col = column_mate(off)
        copy(q * cols + col, q, col).wait_recv()
        copy(me, q, col).wait_send()

    @pl.loop(0, sources)
    def _(i):
        q, col = left_source(i)
        copy(q * cols + col, q, col).wait_recv()

    @pl.loop(0, inner)
    def _(i):
        copy(me, *inner_mate(i)).wait_send()

    swap.wait()


def gather_meta(local, sizes, panels):
    devices = sizes[0] * sizes[1] * sizes[2]
    return pl.pallas_call(
        functools.partial(meta_kernel, sizes, panels),
        out_shape=(
            jax.ShapeDtypeStruct((devices, 1, LANES), jnp.int32),
            jax.ShapeDtypeStruct(local.shape, jnp.int32),
        ),
        in_specs=[pl.BlockSpec(memory_space=pltpu.VMEM)],
        out_specs=(pl.BlockSpec(memory_space=pltpu.VMEM),) * 2,
        scratch_shapes=[
            pltpu.SemaphoreType.DMA((devices,)),
            pltpu.SemaphoreType.DMA((devices,)),
            pltpu.SemaphoreType.DMA,
            pltpu.SemaphoreType.DMA((2,)),
        ],
        compiler_params=pltpu.CompilerParams(collective_id=0, has_side_effects=True),
    )(local)


def pack_kernel(
    sizes, dims, short, win_ref, local_ref, sibling_ref, blocks_ref, pack_ref, codes_ref, sem
):
    rows, cols, depths = sizes
    local_rows, panels, slots = dims
    window = rows * depths
    capacity = pack_ref.shape[1]
    r, c, d = position()
    me_q = r * depths + d
    owner = d // panels
    left_panel = d % panels
    counts_at = panels * slots
    limit = jnp.where(owner == c, capacity, short)

    def entry(q, n, row, panel, slot):
        return pltpu.make_async_copy(blocks_ref.at[row, panel, slot], pack_ref.at[q, n], sem)

    pack_ref[...] = jnp.zeros_like(pack_ref)

    def pack_row(q, carry):
        too_long, copies = carry
        left_at = q * cols + owner
        out_at = q * cols + c
        left_count = win_ref[left_at, 0, counts_at + left_panel]
        on_chip = q % depths == d
        limit_q = jnp.where(on_chip, capacity, limit)
        room = jnp.where(q == me_q, 0, limit_q)
        from_back = (r == 1) & jnp.logical_not(on_chip)

        def left_step(a, counts):
            place = win_ref[left_at, 0, left_panel * slots + a]
            row = place % local_rows
            mine = place // local_rows == r

            def matches(inner_ref, found, n):
                def panel_step(panel, n):
                    out_count = win_ref[out_at, 0, counts_at + panel]
                    inner_count = inner_ref[row, 0, counts_at + panel]

                    def inner_step(t, n):
                        column = inner_ref[row, 0, panel * slots + t]

                        def out_step(s, n):
                            hit = win_ref[out_at, 0, panel * slots + s] == column
                            found(hit, n, panel, t, s)
                            return n + hit.astype(jnp.int32)

                        return lax.fori_loop(0, out_count, out_step, n)

                    return lax.fori_loop(0, inner_count, inner_step, n)

                return lax.fori_loop(0, panels, panel_step, n)

            def keep(hit, n, panel, t, s):
                @pl.when(hit)
                def _():
                    codes_ref[q, 0, HEAD + n] = a * counts_at + panel * slots + s
                    codes_ref[q, 0, SOURCE + n] = (row * panels + panel) * slots + t

                @pl.when(hit & (n < room))
                def _():
                    entry(q, jnp.where(from_back, limit - 1 - n, n), row, panel, t).start()

            def skip(hit, n, panel, t, s):
                pass

            n, other = counts
            return lax.cond(
                mine,
                lambda: (matches(local_ref, keep, n), other),
                lambda: (n, matches(sibling_ref, skip, other)),
            )

        zero = jnp.int32(0)
        n, other = lax.fori_loop(0, left_count, left_step, (zero, zero))
        codes_ref[q, 0, 0] = n
        total = jnp.where(on_chip, n, n + other)
        over = ((total > limit_q) & (q != me_q)).astype(jnp.int32)
        return too_long | over, copies + jnp.minimum(n, room)

    zero = jnp.int32(0)
    too_long, copies = lax.fori_loop(0, window, pack_row, (zero, zero))

    @pl.loop(0, window)
    def _(q):
        codes_ref[q, 0, 1] = too_long

    @pl.loop(0, copies)
    def _(n):
        entry(0, 0, 0, 0, 0).wait()


def pack_lists(win, local, sibling, blocks, sizes, short, capacity):
    local_rows, panels, slots, size, _ = blocks.shape
    window = sizes[0] * sizes[2]
    smem = pl.BlockSpec(memory_space=pltpu.SMEM)
    return pl.pallas_call(
        functools.partial(pack_kernel, sizes, (local_rows, panels, slots), short),
        out_shape=(
            jax.ShapeDtypeStruct((window, capacity, size, size), jnp.float32),
            jax.ShapeDtypeStruct((window, 1, LANES), jnp.int32),
        ),
        in_specs=[smem, smem, smem, pl.BlockSpec(memory_space=pltpu.HBM)],
        out_specs=(pl.BlockSpec(memory_space=pltpu.VMEM), smem),
        scratch_shapes=[pltpu.SemaphoreType.DMA],
        compiler_params=pltpu.CompilerParams(vmem_limit_bytes=VMEM_LIMIT),
    )(win, local, sibling, blocks)


def exchange_kernel(
    sizes, panels, short, pack_ref, codes_ref, blocks_ref,
    got_ref, got_codes_ref, lefts_ref,
    merged_ref, code_send, code_recv, left_send, left_recv,
    swap_send, swap_recv, list_send, list_recv, own_sem,
):
    rows, cols, depths = sizes
    window = rows * depths
    capacity = pack_ref.shape[1]
    left_ref = blocks_ref.at[0]
    r, c, d = position()
    me = r * depths + d
    diag = d // panels == c
    parts = [(0, short)]
    if capacity > short:
        parts.append((short, capacity - short))

    barrier = pltpu.get_barrier_semaphore()

    @pl.loop(1, window)
    def _(off):
        q = (me + off) % window
        pl.semaphore_signal(barrier, inc=1, device_id=(q // depths, c, q % depths), device_id_type=MESH)

    @pl.loop(1, cols)
    def _(off):
        pl.semaphore_signal(barrier, inc=1, device_id=(r, (c + off) % cols, d), device_id_type=MESH)

    own = [
        pltpu.make_async_copy(codes_ref.at[me], got_codes_ref.at[me], own_sem.at[0]),
        pltpu.make_async_copy(left_ref, lefts_ref.at[c], own_sem.at[1]),
    ]
    for copy in own:
        copy.start()
    pl.semaphore_wait(barrier, window - 1 + cols - 1)

    def remote(src, dst, send, recv, device):
        return pltpu.make_async_remote_copy(
            src_ref=src, dst_ref=dst, send_sem=send, recv_sem=recv,
            device_id=device, device_id_type=MESH,
        )

    def left_copy(slot, other):
        return remote(
            left_ref, lefts_ref.at[slot], left_send.at[other], left_recv.at[slot], (r, other, d)
        )

    def code_copy(slot, other):
        return remote(
            codes_ref.at[other], got_codes_ref.at[slot], code_send.at[other], code_recv.at[slot],
            (other // depths, c, other % depths),
        )

    def swap_copy(part, depth):
        first, length = parts[part]
        there = pl.ds(first, length)
        return remote(
            pack_ref.at[(1 - r) * depths + depth, there], merged_ref.at[depth, there],
            swap_send.at[part, depth], swap_recv.at[part, depth], (1 - r, c, d),
        )

    def chip_copy():
        return remote(
            pack_ref.at[(1 - r) * depths + d], got_ref.at[d],
            swap_send.at[0, d], swap_recv.at[0, d], (1 - r, c, d),
        )

    def list_copy(part, slot, depth):
        first, length = parts[part]
        there = pl.ds(first, length)
        return remote(
            merged_ref.at[depth, there], got_ref.at[slot, there],
            list_send.at[part, depth], list_recv.at[part, slot], (r, c, depth),
        )

    def each_part(wide, action):
        action(0)
        if len(parts) > 1:
            @pl.when(wide)
            def _():
                action(1)

    @pl.loop(1, depths)
    def _(off):
        depth = (d + off) % depths
        each_part(diag, lambda part: swap_copy(part, depth).start())

    @pl.loop(1, cols)
    def _(off):
        left_copy(c, (c + off) % cols).start()

    @pl.loop(1, depths)
    def _(off):
        depth = (d + off) % depths

        def forward(part):
            swap_copy(part, depth).wait_recv()
            first, length = parts[part]
            there = pl.ds(first, length)
            merged_ref[depth, there] += pack_ref[r * depths + depth, there]
            list_copy(part, d, depth).start()

        each_part(diag, forward)

    chip_copy().start()

    @pl.loop(1, window)
    def _(off):
        code_copy(me, (me + off) % window).start()

    for copy in own:
        copy.wait()

    @pl.loop(1, cols)
    def _(off):
        other = (c + off) % cols
        left_copy(other, other).wait_recv()
        left_copy(c, other).wait_send()

    @pl.loop(1, window)
    def _(off):
        other = (me + off) % window
        code_copy(other, other).wait_recv()
        code_copy(me, other).wait_send()

    chip_copy().wait()

    @pl.loop(1, depths)
    def _(off):
        depth = (d + off) % depths
        each_part(diag, lambda part: swap_copy(part, depth).wait_send())
        each_part(depth // panels == c, lambda part: list_copy(part, depth, depth).wait_recv())
        each_part(diag, lambda part: list_copy(part, d, depth).wait_send())


def exchange(pack, codes, blocks, sizes, short, ident):
    window, capacity, size, _ = pack.shape
    rows, cols, depths = sizes
    panels = blocks.shape[1]
    vmem = pl.BlockSpec(memory_space=pltpu.VMEM)
    lists = (depths, capacity, size, size)
    sem = pltpu.SemaphoreType.DMA
    return pl.pallas_call(
        functools.partial(exchange_kernel, sizes, panels, short),
        out_shape=(
            jax.ShapeDtypeStruct(lists, jnp.float32),
            jax.ShapeDtypeStruct(codes.shape, jnp.int32),
            jax.ShapeDtypeStruct((cols,) + blocks.shape[1:], jnp.float32),
        ),
        in_specs=[vmem, vmem, pl.BlockSpec(memory_space=pltpu.HBM)],
        out_specs=(vmem,) * 3,
        scratch_shapes=[
            pltpu.VMEM(lists, jnp.float32),
            sem((window,)), sem((window,)), sem((cols,)), sem((cols,)),
            sem((2, depths)), sem((2, depths)), sem((2, depths)), sem((2, depths)), sem((2,)),
        ],
        compiler_params=pltpu.CompilerParams(
            collective_id=ident, has_side_effects=True, vmem_limit_bytes=VMEM_LIMIT
        ),
    )(pack, codes, blocks)


def multiply_into(acc_ref, lefts_ref, got_ref, blocks_ref, codes_ref, held, sems, sizes, short):
    rows, cols, depths = sizes
    window = rows * depths
    capacity = got_ref.shape[1]
    panels, slots = blocks_ref.shape[1:3]
    out_slots = panels * slots
    r, c, d = position()
    me_q = r * depths + d
    own = codes_ref[me_q, 0, 0]

    def fetch(n):
        at = codes_ref[me_q, 0, SOURCE + n]
        row = at // out_slots
        block = blocks_ref.at[row, (at // slots) % panels, at % slots]
        return pltpu.make_async_copy(block, held.at[n], sems.at[n])

    @pl.loop(0, own)
    def _(n):
        fetch(n).start()

    acc_ref[...] = jnp.zeros_like(acc_ref)

    def add(q, n, right):
        code = codes_ref[q, 0, HEAD + n]
        depth = q % depths
        left = lefts_ref[depth // panels, depth % panels, code // out_slots]
        s = code % out_slots
        acc_ref[s // slots, s % slots] += jnp.dot(
            left, right, precision=lax.Precision.HIGHEST, preferred_element_type=jnp.float32
        )

    @pl.loop(0, window)
    def _(q):
        depth = q % depths
        on_chip = depth == d
        room = jnp.where(on_chip | (depth // panels == c), capacity, short)
        from_back = (q // depths == 1) & jnp.logical_not(on_chip)
        count = jnp.where(q == me_q, 0, jnp.minimum(codes_ref[q, 0, 0], room))

        @pl.loop(0, count)
        def _(n):
            add(q, n, got_ref[depth, jnp.where(from_back, room - 1 - n, n)])

    @pl.loop(0, own)
    def _(n):
        fetch(n).wait()
        add(me_q, n, held[n])


def square_kernel(
    sizes, short, codes_ref, got_ref, blocks_ref, lefts_ref, out_ref, flag_ref, held, sems
):
    flag_ref[0, 0] = lax.fori_loop(
        0, codes_ref.shape[0], lambda q, f: f | codes_ref[q, 0, 1], jnp.int32(0)
    )
    multiply_into(out_ref, lefts_ref, got_ref, blocks_ref, codes_ref, held, sems, sizes, short)


def cube_kernel(
    sizes, short, codes_ref, got_ref, blocks_ref, lefts_ref, square_ref, out_ref, held, sems
):
    multiply_into(out_ref, lefts_ref, got_ref, blocks_ref, codes_ref, held, sems, sizes, short)
    out_ref[...] = 3.0 * square_ref[...] - 2.0 * out_ref[...]


def local_product(kernel, codes, got, blocks, lefts, extra, out_shape, out_specs):
    vmem = pl.BlockSpec(memory_space=pltpu.VMEM)
    _, panels, slots, size, _ = blocks.shape
    most = slots * slots * panels
    return pl.pallas_call(
        kernel,
        out_shape=out_shape,
        in_specs=[
            pl.BlockSpec(memory_space=pltpu.SMEM),
            vmem,
            pl.BlockSpec(memory_space=pltpu.HBM),
            vmem,
        ] + [vmem] * len(extra),
        out_specs=out_specs,
        scratch_shapes=[
            pltpu.VMEM((most, size, size), jnp.float32),
            pltpu.SemaphoreType.DMA((most,)),
        ],
        compiler_params=pltpu.CompilerParams(vmem_limit_bytes=VMEM_LIMIT),
    )(codes, got, blocks, lefts, *extra)


def gather_kernel(cols, square_ref, flag_ref, squares_ref, flags_ref, send_sem, recv_sem, own_sem):
    r, c, d = position()
    barrier = pltpu.get_barrier_semaphore()

    @pl.loop(1, cols)
    def _(off):
        pl.semaphore_signal(barrier, inc=1, device_id=(r, (c + off) % cols, d), device_id_type=MESH)

    pairs = ((square_ref, squares_ref), (flag_ref, flags_ref))
    own = [
        pltpu.make_async_copy(src, dst.at[c], own_sem.at[i]) for i, (src, dst) in enumerate(pairs)
    ]
    for copy in own:
        copy.start()
    pl.semaphore_wait(barrier, cols - 1)

    def copies(slot, other):
        return [
            pltpu.make_async_remote_copy(
                src_ref=src,
                dst_ref=dst.at[slot],
                send_sem=send_sem.at[i, other],
                recv_sem=recv_sem.at[i, slot],
                device_id=(r, other, d),
                device_id_type=MESH,
            )
            for i, (src, dst) in enumerate(pairs)
        ]

    @pl.loop(1, cols)
    def _(off):
        for copy in copies(c, (c + off) % cols):
            copy.start()

    for copy in own:
        copy.wait()

    @pl.loop(1, cols)
    def _(off):
        other = (c + off) % cols
        for copy in copies(other, other):
            copy.wait_recv()
        for copy in copies(c, other):
            copy.wait_send()


def gather_square(square, flag, cols, ident):
    vmem = pl.BlockSpec(memory_space=pltpu.VMEM)
    return pl.pallas_call(
        functools.partial(gather_kernel, cols),
        out_shape=(
            jax.ShapeDtypeStruct((cols,) + square.shape, jnp.float32),
            jax.ShapeDtypeStruct((cols,) + flag.shape, jnp.int32),
        ),
        in_specs=[vmem] * 2,
        out_specs=(vmem,) * 2,
        scratch_shapes=[
            pltpu.SemaphoreType.DMA((2, cols)),
            pltpu.SemaphoreType.DMA((2, cols)),
            pltpu.SemaphoreType.DMA((2,)),
        ],
        compiler_params=pltpu.CompilerParams(collective_id=ident, has_side_effects=True),
    )(square, flag)


def body(sizes, blocks, columns, counts):
    rows, cols, depths = sizes
    local_rows, panels, slots, size, _ = blocks.shape
    most = slots * slots * panels
    local = jnp.concatenate([columns.reshape(local_rows, 1, panels * slots), counts[:, None, :]], 2)
    local = jnp.pad(local, ((0, 0), (0, 0), (0, LANES - local.shape[2])))
    win, sibling = gather_meta(local, sizes, panels)
    block_shape = jax.ShapeDtypeStruct(blocks.shape[1:], jnp.float32)
    vmem = pl.BlockSpec(memory_space=pltpu.VMEM)

    def square_step(short, capacity, ident):
        pack, codes = pack_lists(win, local, sibling, blocks, sizes, short, capacity)
        got, got_codes, lefts = exchange(pack, codes, blocks, sizes, short, ident)
        square, flag = local_product(
            functools.partial(square_kernel, sizes, short),
            got_codes, got, blocks, lefts, (),
            (block_shape, jax.ShapeDtypeStruct((1, LANES), jnp.int32)),
            (vmem, pl.BlockSpec(memory_space=pltpu.SMEM)),
        )
        squares, flags = gather_square(square, flag, cols, ident + 1)
        return got, got_codes, square, squares, flags

    def cube_step(short, got, got_codes, square, squares):
        return local_product(
            functools.partial(cube_kernel, sizes, short),
            got_codes, got, blocks, squares, (square,), block_shape, vmem,
        )

    short = min(SHORT, most)
    *lists, flags = square_step(short, min(SHORT_DIAG, most), 1)

    def again():
        *lists, _ = square_step(most, most, 3)
        return cube_step(most, *lists)

    out = lax.cond(jnp.any(flags[:, 0, 0] != 0), again, lambda: cube_step(short, *lists))
    return out[None]


def solution(mesh):
    placed = (
        P(("row", "depth"), "col", None, None, None),
        P(("row", "depth"), "col", None),
        P(("row", "depth"), "col"),
    )
    sizes = (mesh.shape["row"], mesh.shape["col"], mesh.shape["depth"])
    return jax.shard_map(
        functools.partial(body, sizes),
        mesh=mesh,
        in_specs=placed,
        out_specs=P(("row", "depth"), "col", None, None, None),
        check_vma=False,
    )
```

```python
import functools

import jax
import jax.numpy as jnp
from jax import lax
from jax.experimental import pallas as pl
from jax.experimental.pallas import tpu as pltpu
from jax.sharding import PartitionSpec as P

MESH = pl.DeviceIdType.MESH
LANES = 128
VMEM_LIMIT = 48 << 20
SHORT = 2
SHORT_DIAG = 6
HEAD = 2
SOURCE = LANES // 2


def position():
    return lax.axis_index("row"), lax.axis_index("col"), lax.axis_index("depth")


def meta_kernel(
    sizes, panels, local_ref, all_ref, sibling_ref, send_sem, recv_sem, own_sem, swap_sems
):
    rows, cols, depths = sizes
    window = rows * depths
    r, c, d = position()
    me_q = r * depths + d
    owner = d // panels
    meta_ref = local_ref.at[0]

    def column_mate(off):
        q = (me_q + off) % window
        return q, c

    def inner_mate(i):
        col = (c + 1 + i // (rows * panels)) % cols
        row = (i // panels) % rows
        return row * depths + c * panels + i % panels, col

    def left_source(i):
        return i, owner

    mates = window - 1
    inner = rows * panels * (cols - 1)
    sources = jnp.where(owner == c, 0, window)

    def device(q, col):
        return (q // depths, col, q % depths)

    barrier = pltpu.get_barrier_semaphore()

    def greet(q, col):
        pl.semaphore_signal(barrier, inc=1, device_id=device(q, col), device_id_type=MESH)

    @pl.loop(1, window)
    def _(off):
        greet(*column_mate(off))

    @pl.loop(0, sources)
    def _(i):
        greet(*left_source(i))

    own = pltpu.make_async_copy(meta_ref, all_ref.at[me_q * cols + c], own_sem)
    own.start()
    pl.semaphore_wait(barrier, mates + inner)

    def copy(slot, q, col):
        return pltpu.make_async_remote_copy(
            src_ref=meta_ref,
            dst_ref=all_ref.at[slot],
            send_sem=send_sem.at[q * cols + col],
            recv_sem=recv_sem.at[slot],
            device_id=device(q, col),
            device_id_type=MESH,
        )

    me = me_q * cols + c
    swap = pltpu.make_async_remote_copy(
        src_ref=local_ref,
        dst_ref=sibling_ref,
        send_sem=swap_sems.at[0],
        recv_sem=swap_sems.at[1],
        device_id=(1 - r, c, d),
        device_id_type=MESH,
    )

    @pl.loop(0, inner)
    def _(i):
        copy(me, *inner_mate(i)).start()

    @pl.loop(1, window)
    def _(off):
        copy(me, *column_mate(off)).start()

    swap.start()
    own.wait()

    @pl.loop(1, window)
    def _(off):
        q, col = column_mate(off)
        copy(q * cols + col, q, col).wait_recv()
        copy(me, q, col).wait_send()

    @pl.loop(0, sources)
    def _(i):
        q, col = left_source(i)
        copy(q * cols + col, q, col).wait_recv()

    @pl.loop(0, inner)
    def _(i):
        copy(me, *inner_mate(i)).wait_send()

    swap.wait()


def gather_meta(local, sizes, panels):
    devices = sizes[0] * sizes[1] * sizes[2]
    return pl.pallas_call(
        functools.partial(meta_kernel, sizes, panels),
        out_shape=(
            jax.ShapeDtypeStruct((devices, 1, LANES), jnp.int32),
            jax.ShapeDtypeStruct(local.shape, jnp.int32),
        ),
        in_specs=[pl.BlockSpec(memory_space=pltpu.VMEM)],
        out_specs=(pl.BlockSpec(memory_space=pltpu.VMEM),) * 2,
        scratch_shapes=[
            pltpu.SemaphoreType.DMA((devices,)),
            pltpu.SemaphoreType.DMA((devices,)),
            pltpu.SemaphoreType.DMA,
            pltpu.SemaphoreType.DMA((2,)),
        ],
        compiler_params=pltpu.CompilerParams(collective_id=0, has_side_effects=True),
    )(local)


def pack_kernel(
    sizes, dims, short, win_ref, local_ref, sibling_ref, blocks_ref, pack_ref, codes_ref, sem
):
    rows, cols, depths = sizes
    local_rows, panels, slots = dims
    window = rows * depths
    capacity = pack_ref.shape[1]
    r, c, d = position()
    me_q = r * depths + d
    owner = d // panels
    left_panel = d % panels
    counts_at = panels * slots
    limit = jnp.where(owner == c, capacity, short)

    def entry(q, n, row, panel, slot):
        return pltpu.make_async_copy(blocks_ref.at[row, panel, slot], pack_ref.at[q, n], sem)

    pack_ref[...] = jnp.zeros_like(pack_ref)

    def pack_row(q, carry):
        too_long, copies = carry
        left_at = q * cols + owner
        out_at = q * cols + c
        left_count = win_ref[left_at, 0, counts_at + left_panel]
        on_chip = q % depths == d
        limit_q = jnp.where(on_chip, capacity, limit)
        room = jnp.where(q == me_q, 0, limit_q)
        from_back = (r == 1) & jnp.logical_not(on_chip)

        def left_step(a, counts):
            place = win_ref[left_at, 0, left_panel * slots + a]
            row = place % local_rows
            mine = place // local_rows == r

            def matches(inner_ref, found, n):
                def panel_step(panel, n):
                    out_count = win_ref[out_at, 0, counts_at + panel]
                    inner_count = inner_ref[row, 0, counts_at + panel]

                    def inner_step(t, n):
                        column = inner_ref[row, 0, panel * slots + t]

                        def out_step(s, n):
                            hit = win_ref[out_at, 0, panel * slots + s] == column
                            found(hit, n, panel, t, s)
                            return n + hit.astype(jnp.int32)

                        return lax.fori_loop(0, out_count, out_step, n)

                    return lax.fori_loop(0, inner_count, inner_step, n)

                return lax.fori_loop(0, panels, panel_step, n)

            def keep(hit, n, panel, t, s):
                @pl.when(hit)
                def _():
                    codes_ref[q, 0, HEAD + n] = a * counts_at + panel * slots + s
                    codes_ref[q, 0, SOURCE + n] = (row * panels + panel) * slots + t

                @pl.when(hit & (n < room))
                def _():
                    entry(q, jnp.where(from_back, limit - 1 - n, n), row, panel, t).start()

            def skip(hit, n, panel, t, s):
                pass

            n, other = counts
            return lax.cond(
                mine,
                lambda: (matches(local_ref, keep, n), other),
                lambda: (n, matches(sibling_ref, skip, other)),
            )

        zero = jnp.int32(0)
        n, other = lax.fori_loop(0, left_count, left_step, (zero, zero))
        codes_ref[q, 0, 0] = n
        total = jnp.where(on_chip, n, n + other)
        over = ((total > limit_q) & (q != me_q)).astype(jnp.int32)
        return too_long | over, copies + jnp.minimum(n, room)

    zero = jnp.int32(0)
    too_long, copies = lax.fori_loop(0, window, pack_row, (zero, zero))

    @pl.loop(0, window)
    def _(q):
        codes_ref[q, 0, 1] = too_long

    @pl.loop(0, copies)
    def _(n):
        entry(0, 0, 0, 0, 0).wait()


def pack_lists(win, local, sibling, blocks, sizes, short, capacity):
    local_rows, panels, slots, size, _ = blocks.shape
    window = sizes[0] * sizes[2]
    smem = pl.BlockSpec(memory_space=pltpu.SMEM)
    return pl.pallas_call(
        functools.partial(pack_kernel, sizes, (local_rows, panels, slots), short),
        out_shape=(
            jax.ShapeDtypeStruct((window, capacity, size, size), jnp.float32),
            jax.ShapeDtypeStruct((window, 1, LANES), jnp.int32),
        ),
        in_specs=[smem, smem, smem, pl.BlockSpec(memory_space=pltpu.HBM)],
        out_specs=(pl.BlockSpec(memory_space=pltpu.VMEM), smem),
        scratch_shapes=[pltpu.SemaphoreType.DMA],
        compiler_params=pltpu.CompilerParams(vmem_limit_bytes=VMEM_LIMIT),
    )(win, local, sibling, blocks)


def exchange_kernel(
    sizes, panels, short, pack_ref, codes_ref, blocks_ref,
    got_ref, got_codes_ref, lefts_ref,
    merged_ref, code_send, code_recv, left_send, left_recv,
    swap_send, swap_recv, list_send, list_recv, relay_ref, relay_send, relay_recv, own_sem,
):
    rows, cols, depths = sizes
    window = rows * depths
    capacity = pack_ref.shape[1]
    left_ref = blocks_ref.at[0]
    r, c, d = position()
    me = r * depths + d
    diag = d // panels == c
    parts = [(0, short, 0)]
    extra = capacity - short
    ways = [1, 2] if cols == 4 and extra >= 4 else []
    straight = extra // 4 if ways else extra
    if extra:
        parts.append((short, straight, 0))
    if ways:
        parts.append((short + straight, straight, 1))
        parts.append((short + 2 * straight, extra - 2 * straight, 2))

    barrier = pltpu.get_barrier_semaphore()

    @pl.loop(1, window)
    def _(off):
        q = (me + off) % window
        pl.semaphore_signal(barrier, inc=1, device_id=(q // depths, c, q % depths), device_id_type=MESH)

    @pl.loop(1, cols)
    def _(off):
        pl.semaphore_signal(barrier, inc=1, device_id=(r, (c + off) % cols, d), device_id_type=MESH)

    for way in ways:
        @pl.loop(1, depths)
        def _(off):
            device = (r, c ^ way, (d + off) % depths)
            pl.semaphore_signal(barrier, inc=1, device_id=device, device_id_type=MESH)

    own = [
        pltpu.make_async_copy(codes_ref.at[me], got_codes_ref.at[me], own_sem.at[0]),
        pltpu.make_async_copy(left_ref, lefts_ref.at[c], own_sem.at[1]),
    ]
    for copy in own:
        copy.start()
    pl.semaphore_wait(barrier, window - 1 + cols - 1 + len(ways) * (depths - 1))

    def remote(src, dst, send, recv, device):
        return pltpu.make_async_remote_copy(
            src_ref=src, dst_ref=dst, send_sem=send, recv_sem=recv,
            device_id=device, device_id_type=MESH,
        )

    def left_copy(slot, other):
        return remote(
            left_ref, lefts_ref.at[slot], left_send.at[other], left_recv.at[slot], (r, other, d)
        )

    def code_copy(slot, other):
        return remote(
            codes_ref.at[other], got_codes_ref.at[slot], code_send.at[other], code_recv.at[slot],
            (other // depths, c, other % depths),
        )

    def swap_copy(part, depth):
        first, length, way = parts[part]
        there = pl.ds(first, length)
        return remote(
            pack_ref.at[(1 - r) * depths + depth, there], merged_ref.at[depth, there],
            swap_send.at[part, depth], swap_recv.at[part, depth], (1 - r, c, d),
        )

    def chip_copy():
        return remote(
            pack_ref.at[(1 - r) * depths + d], got_ref.at[d],
            swap_send.at[0, d], swap_recv.at[0, d], (1 - r, c, d),
        )

    def list_copy(part, slot, depth):
        first, length, way = parts[part]
        there = pl.ds(first, length)
        target = relay_ref.at[way - 1, slot % panels, pl.ds(0, length)] if way else got_ref.at[slot, there]
        return remote(
            merged_ref.at[depth, there], target,
            list_send.at[part, depth], list_recv.at[part, slot], (r, c ^ way, depth),
        )

    def relay_copy(part, depth):
        first, length, way = parts[part]
        return remote(
            relay_ref.at[way - 1, depth % panels, pl.ds(0, length)],
            got_ref.at[depth, pl.ds(first, length)],
            relay_send.at[part, depth], relay_recv.at[part, depth], (r, c ^ way, d),
        )

    def each_part(wide, action):
        action(0)
        if len(parts) > 1:
            @pl.when(wide)
            def _():
                for part in range(1, len(parts)):
                    action(part)

    def arrival(part, depth):
        return list_copy(part, depth, depth)

    def each_relay(action):
        for part, (first, length, way) in enumerate(parts):
            if way:
                for i in range(panels):
                    depth = (c ^ way) * panels + i

                    @pl.when(depth != d)
                    def _():
                        action(part, depth)

    @pl.loop(1, depths)
    def _(off):
        depth = (d + off) % depths
        each_part(diag, lambda part: swap_copy(part, depth).start())

    @pl.loop(1, cols)
    def _(off):
        left_copy(c, (c + off) % cols).start()

    @pl.loop(1, depths)
    def _(off):
        depth = (d + off) % depths

        def forward(part):
            swap_copy(part, depth).wait_recv()
            first, length, way = parts[part]
            there = pl.ds(first, length)
            merged_ref[depth, there] += pack_ref[r * depths + depth, there]
            list_copy(part, d, depth).start()

        each_part(diag, forward)

    chip_copy().start()

    @pl.loop(1, window)
    def _(off):
        code_copy(me, (me + off) % window).start()

    def pass_on(part, depth):
        list_copy(part, depth, d).wait_recv()
        relay_copy(part, depth).start()

    each_relay(pass_on)

    for copy in own:
        copy.wait()

    @pl.loop(1, cols)
    def _(off):
        other = (c + off) % cols
        left_copy(other, other).wait_recv()
        left_copy(c, other).wait_send()

    @pl.loop(1, window)
    def _(off):
        other = (me + off) % window
        code_copy(other, other).wait_recv()
        code_copy(me, other).wait_send()

    chip_copy().wait()

    @pl.loop(1, depths)
    def _(off):
        depth = (d + off) % depths
        each_part(diag, lambda part: swap_copy(part, depth).wait_send())
        each_part(
            depth // panels == c,
            lambda part: (relay_copy if parts[part][2] else arrival)(part, depth).wait_recv(),
        )
        each_part(diag, lambda part: list_copy(part, d, depth).wait_send())

    each_relay(lambda part, depth: relay_copy(part, depth).wait_send())


def exchange(pack, codes, blocks, sizes, short, ident):
    window, capacity, size, _ = pack.shape
    rows, cols, depths = sizes
    panels = blocks.shape[1]
    vmem = pl.BlockSpec(memory_space=pltpu.VMEM)
    lists = (depths, capacity, size, size)
    sem = pltpu.SemaphoreType.DMA
    return pl.pallas_call(
        functools.partial(exchange_kernel, sizes, panels, short),
        out_shape=(
            jax.ShapeDtypeStruct(lists, jnp.float32),
            jax.ShapeDtypeStruct(codes.shape, jnp.int32),
            jax.ShapeDtypeStruct((cols,) + blocks.shape[1:], jnp.float32),
        ),
        in_specs=[vmem, vmem, pl.BlockSpec(memory_space=pltpu.HBM)],
        out_specs=(vmem,) * 3,
        scratch_shapes=[
            pltpu.VMEM(lists, jnp.float32),
            sem((window,)), sem((window,)), sem((cols,)), sem((cols,)),
            sem((4, depths)), sem((4, depths)), sem((4, depths)), sem((4, depths)),
            pltpu.VMEM((2, panels, capacity, size, size), jnp.float32),
            sem((4, depths)), sem((4, depths)), sem((2,)),
        ],
        compiler_params=pltpu.CompilerParams(
            collective_id=ident, has_side_effects=True, vmem_limit_bytes=VMEM_LIMIT
        ),
    )(pack, codes, blocks)


def multiply_into(acc_ref, lefts_ref, got_ref, blocks_ref, codes_ref, held, sems, sizes, short):
    rows, cols, depths = sizes
    window = rows * depths
    capacity = got_ref.shape[1]
    panels, slots = blocks_ref.shape[1:3]
    out_slots = panels * slots
    r, c, d = position()
    me_q = r * depths + d
    own = codes_ref[me_q, 0, 0]

    def fetch(n):
        at = codes_ref[me_q, 0, SOURCE + n]
        row = at // out_slots
        block = blocks_ref.at[row, (at // slots) % panels, at % slots]
        return pltpu.make_async_copy(block, held.at[n], sems.at[n])

    @pl.loop(0, own)
    def _(n):
        fetch(n).start()

    acc_ref[...] = jnp.zeros_like(acc_ref)

    def add(q, n, right):
        code = codes_ref[q, 0, HEAD + n]
        depth = q % depths
        left = lefts_ref[depth // panels, depth % panels, code // out_slots]
        s = code % out_slots
        acc_ref[s // slots, s % slots] += jnp.dot(
            left, right, precision=lax.Precision.HIGHEST, preferred_element_type=jnp.float32
        )

    @pl.loop(0, window)
    def _(q):
        depth = q % depths
        on_chip = depth == d
        room = jnp.where(on_chip | (depth // panels == c), capacity, short)
        from_back = (q // depths == 1) & jnp.logical_not(on_chip)
        count = jnp.where(q == me_q, 0, jnp.minimum(codes_ref[q, 0, 0], room))

        @pl.loop(0, count)
        def _(n):
            add(q, n, got_ref[depth, jnp.where(from_back, room - 1 - n, n)])

    @pl.loop(0, own)
    def _(n):
        fetch(n).wait()
        add(me_q, n, held[n])


def square_kernel(
    sizes, short, codes_ref, got_ref, blocks_ref, lefts_ref, out_ref, flag_ref, held, sems
):
    flag = lax.fori_loop(0, codes_ref.shape[0], lambda q, f: f | codes_ref[q, 0, 1], jnp.int32(0))
    flag_ref[...] = jnp.full(flag_ref.shape, flag, jnp.int32)
    multiply_into(out_ref, lefts_ref, got_ref, blocks_ref, codes_ref, held, sems, sizes, short)


def cube_kernel(
    sizes, short, codes_ref, got_ref, blocks_ref, lefts_ref, square_ref, out_ref, held, sems
):
    multiply_into(out_ref, lefts_ref, got_ref, blocks_ref, codes_ref, held, sems, sizes, short)
    out_ref[...] = 3.0 * square_ref[...] - 2.0 * out_ref[...]


def local_product(kernel, codes, got, blocks, lefts, extra, out_shape, out_specs):
    vmem = pl.BlockSpec(memory_space=pltpu.VMEM)
    _, panels, slots, size, _ = blocks.shape
    most = slots * slots * panels
    return pl.pallas_call(
        kernel,
        out_shape=out_shape,
        in_specs=[
            pl.BlockSpec(memory_space=pltpu.SMEM),
            vmem,
            pl.BlockSpec(memory_space=pltpu.HBM),
            vmem,
        ] + [vmem] * len(extra),
        out_specs=out_specs,
        scratch_shapes=[
            pltpu.VMEM((most, size, size), jnp.float32),
            pltpu.SemaphoreType.DMA((most,)),
        ],
        compiler_params=pltpu.CompilerParams(vmem_limit_bytes=VMEM_LIMIT),
    )(codes, got, blocks, lefts, *extra)


def gather_kernel(
    cols, square_ref, flag_ref, squares_ref, any_ref, flags_ref, send_sem, recv_sem, own_sem
):
    r, c, d = position()
    barrier = pltpu.get_barrier_semaphore()

    @pl.loop(1, cols)
    def _(off):
        pl.semaphore_signal(barrier, inc=1, device_id=(r, (c + off) % cols, d), device_id_type=MESH)

    pairs = ((square_ref, squares_ref), (flag_ref, flags_ref))
    own = [
        pltpu.make_async_copy(src, dst.at[c], own_sem.at[i]) for i, (src, dst) in enumerate(pairs)
    ]
    for copy in own:
        copy.start()
    pl.semaphore_wait(barrier, cols - 1)

    def copies(slot, other):
        return [
            pltpu.make_async_remote_copy(
                src_ref=src,
                dst_ref=dst.at[slot],
                send_sem=send_sem.at[i, other],
                recv_sem=recv_sem.at[i, slot],
                device_id=(r, other, d),
                device_id_type=MESH,
            )
            for i, (src, dst) in enumerate(pairs)
        ]

    @pl.loop(1, cols)
    def _(off):
        for copy in copies(c, (c + off) % cols):
            copy.start()

    for copy in own:
        copy.wait()

    @pl.loop(1, cols)
    def _(off):
        other = (c + off) % cols
        for copy in copies(other, other):
            copy.wait_recv()
        for copy in copies(c, other):
            copy.wait_send()

    any_ref[...] = jnp.max(flags_ref[...], axis=0)


def gather_square(square, flag, cols, ident):
    vmem = pl.BlockSpec(memory_space=pltpu.VMEM)
    return pl.pallas_call(
        functools.partial(gather_kernel, cols),
        out_shape=(
            jax.ShapeDtypeStruct((cols,) + square.shape, jnp.float32),
            jax.ShapeDtypeStruct(flag.shape, jnp.int32),
        ),
        in_specs=[vmem] * 2,
        out_specs=(vmem,) * 2,
        scratch_shapes=[
            pltpu.VMEM((cols,) + flag.shape, jnp.int32),
            pltpu.SemaphoreType.DMA((2, cols)),
            pltpu.SemaphoreType.DMA((2, cols)),
            pltpu.SemaphoreType.DMA((2,)),
        ],
        compiler_params=pltpu.CompilerParams(collective_id=ident, has_side_effects=True),
    )(square, flag)


def body(sizes, blocks, columns, counts):
    rows, cols, depths = sizes
    local_rows, panels, slots, size, _ = blocks.shape
    most = slots * slots * panels
    local = jnp.concatenate([columns.reshape(local_rows, 1, panels * slots), counts[:, None, :]], 2)
    local = jnp.pad(local, ((0, 0), (0, 0), (0, LANES - local.shape[2])))
    win, sibling = gather_meta(local, sizes, panels)
    block_shape = jax.ShapeDtypeStruct(blocks.shape[1:], jnp.float32)
    vmem = pl.BlockSpec(memory_space=pltpu.VMEM)

    def square_step(short, capacity, ident):
        pack, codes = pack_lists(win, local, sibling, blocks, sizes, short, capacity)
        got, got_codes, lefts = exchange(pack, codes, blocks, sizes, short, ident)
        square, flag = local_product(
            functools.partial(square_kernel, sizes, short),
            got_codes, got, blocks, lefts, (),
            (block_shape, jax.ShapeDtypeStruct((1, LANES), jnp.int32)),
            (vmem, vmem),
        )
        squares, too_long = gather_square(square, flag, cols, ident + 1)
        return got, got_codes, square, squares, too_long

    def cube_step(short, got, got_codes, square, squares):
        return local_product(
            functools.partial(cube_kernel, sizes, short),
            got_codes, got, blocks, squares, (square,), block_shape, vmem,
        )

    short = min(SHORT, most)
    *lists, too_long = square_step(short, min(SHORT_DIAG, most), 1)

    def again():
        *lists, _ = square_step(most, most, 3)
        return cube_step(most, *lists)

    out = lax.cond(too_long[0, 0] != 0, again, lambda: cube_step(short, *lists))
    return out[None]


def solution(mesh):
    placed = (
        P(("row", "depth"), "col", None, None, None),
        P(("row", "depth"), "col", None),
        P(("row", "depth"), "col"),
    )
    sizes = (mesh.shape["row"], mesh.shape["col"], mesh.shape["depth"])
    return jax.shard_map(
        functools.partial(body, sizes),
        mesh=mesh,
        in_specs=placed,
        out_specs=P(("row", "depth"), "col", None, None, None),
        check_vma=False,
    )
```

```python
import functools

import jax
import jax.numpy as jnp
from jax import lax
from jax.experimental import pallas as pl
from jax.experimental.pallas import tpu as pltpu
from jax.sharding import PartitionSpec as P

MESH = pl.DeviceIdType.MESH
LANES = 128
VMEM_LIMIT = 48 << 20
SHORT = 2
SHORT_DIAG = 6
HEAD = 2
SOURCE = LANES // 2


def position():
    return lax.axis_index("row"), lax.axis_index("col"), lax.axis_index("depth")


def spread(cols, slots, src_ref, dst_ref, send, recv):
    r, c, d = position()

    def remote(src, dst, send, recv, column):
        return pltpu.make_async_remote_copy(
            src_ref=src, dst_ref=dst, send_sem=send, recv_sem=recv,
            device_id=(r, column, d), device_id_type=MESH,
        )

    if cols != 4 or slots % 2:
        def copy(slot, other):
            return remote(src_ref, dst_ref.at[slot], send.at[0, other], recv.at[0, slot], other)

        def begin():
            @pl.loop(1, cols)
            def _(off):
                copy(c, (c + off) % cols).start()

        def end():
            @pl.loop(1, cols)
            def _(off):
                other = (c + off) % cols
                copy(other, other).wait_recv()
                copy(c, other).wait_send()

        return begin, lambda: None, end

    def half(ref, h):
        return ref.at[:, pl.ds(h * (slots // 2), slots // 2)]

    def direct(h, way):
        return remote(
            half(src_ref, h), half(dst_ref.at[c], h), send.at[h, way - 1], recv.at[h, c], c ^ way
        )

    def arrival(h, way):
        there = half(dst_ref.at[c ^ way], h)
        return remote(half(src_ref, h), there, send.at[h, 0], recv.at[h, c ^ way], c ^ 1)

    def onward(h):
        origin = c ^ (1 + h)
        there = half(dst_ref.at[origin], h)
        return remote(there, there, send.at[h, 2], recv.at[h, origin], c ^ (2 - h))

    sent = [(0, 1), (1, 2), (1, 1), (0, 2)]

    def begin():
        for h, way in sent:
            direct(h, way).start()

    def pass_on():
        for h in (0, 1):
            arrival(h, 1 + h).wait_recv()
            onward(h).start()

    def end():
        for h, way in ((1, 1), (0, 2), (0, 3), (1, 3)):
            arrival(h, way).wait_recv()
        for h, way in sent:
            direct(h, way).wait_send()
        for h in (0, 1):
            onward(h).wait_send()

    return begin, pass_on, end


def meta_kernel(
    sizes, panels, local_ref, all_ref, sibling_ref, send_sem, recv_sem, own_sem, swap_sems
):
    rows, cols, depths = sizes
    window = rows * depths
    r, c, d = position()
    me_q = r * depths + d
    owner = d // panels
    meta_ref = local_ref.at[0]

    def column_mate(off):
        q = (me_q + off) % window
        return q, c

    def inner_mate(i):
        col = (c + 1 + i // (rows * panels)) % cols
        row = (i // panels) % rows
        return row * depths + c * panels + i % panels, col

    def left_source(i):
        return i, owner

    mates = window - 1
    inner = rows * panels * (cols - 1)
    sources = jnp.where(owner == c, 0, window)

    def device(q, col):
        return (q // depths, col, q % depths)

    barrier = pltpu.get_barrier_semaphore()

    def greet(q, col):
        pl.semaphore_signal(barrier, inc=1, device_id=device(q, col), device_id_type=MESH)

    @pl.loop(1, window)
    def _(off):
        greet(*column_mate(off))

    @pl.loop(0, sources)
    def _(i):
        greet(*left_source(i))

    own = pltpu.make_async_copy(meta_ref, all_ref.at[me_q * cols + c], own_sem)
    own.start()
    pl.semaphore_wait(barrier, mates + inner)

    def copy(slot, q, col):
        return pltpu.make_async_remote_copy(
            src_ref=meta_ref,
            dst_ref=all_ref.at[slot],
            send_sem=send_sem.at[q * cols + col],
            recv_sem=recv_sem.at[slot],
            device_id=device(q, col),
            device_id_type=MESH,
        )

    me = me_q * cols + c
    swap = pltpu.make_async_remote_copy(
        src_ref=local_ref,
        dst_ref=sibling_ref,
        send_sem=swap_sems.at[0],
        recv_sem=swap_sems.at[1],
        device_id=(1 - r, c, d),
        device_id_type=MESH,
    )

    @pl.loop(0, inner)
    def _(i):
        copy(me, *inner_mate(i)).start()

    @pl.loop(1, window)
    def _(off):
        copy(me, *column_mate(off)).start()

    swap.start()
    own.wait()

    @pl.loop(1, window)
    def _(off):
        q, col = column_mate(off)
        copy(q * cols + col, q, col).wait_recv()
        copy(me, q, col).wait_send()

    @pl.loop(0, sources)
    def _(i):
        q, col = left_source(i)
        copy(q * cols + col, q, col).wait_recv()

    @pl.loop(0, inner)
    def _(i):
        copy(me, *inner_mate(i)).wait_send()

    swap.wait()


def gather_meta(local, sizes, panels):
    devices = sizes[0] * sizes[1] * sizes[2]
    return pl.pallas_call(
        functools.partial(meta_kernel, sizes, panels),
        out_shape=(
            jax.ShapeDtypeStruct((devices, 1, LANES), jnp.int32),
            jax.ShapeDtypeStruct(local.shape, jnp.int32),
        ),
        in_specs=[pl.BlockSpec(memory_space=pltpu.VMEM)],
        out_specs=(pl.BlockSpec(memory_space=pltpu.VMEM),) * 2,
        scratch_shapes=[
            pltpu.SemaphoreType.DMA((devices,)),
            pltpu.SemaphoreType.DMA((devices,)),
            pltpu.SemaphoreType.DMA,
            pltpu.SemaphoreType.DMA((2,)),
        ],
        compiler_params=pltpu.CompilerParams(collective_id=0, has_side_effects=True),
    )(local)


def pack_kernel(
    sizes, dims, short, win_ref, local_ref, sibling_ref, blocks_ref, pack_ref, codes_ref, sem
):
    rows, cols, depths = sizes
    local_rows, panels, slots = dims
    window = rows * depths
    capacity = pack_ref.shape[1]
    r, c, d = position()
    me_q = r * depths + d
    owner = d // panels
    left_panel = d % panels
    counts_at = panels * slots
    limit = jnp.where(owner == c, capacity, short)

    def entry(q, n, row, panel, slot):
        return pltpu.make_async_copy(blocks_ref.at[row, panel, slot], pack_ref.at[q, n], sem)

    def pack_row(q, carry):
        too_long, copies = carry
        left_at = q * cols + owner
        out_at = q * cols + c
        left_count = win_ref[left_at, 0, counts_at + left_panel]
        on_chip = q % depths == d
        limit_q = jnp.where(on_chip, capacity, limit)
        room = jnp.where(q == me_q, 0, limit_q)
        from_back = (r == 1) & jnp.logical_not(on_chip)

        def left_step(a, counts):
            place = win_ref[left_at, 0, left_panel * slots + a]
            row = place % local_rows
            mine = place // local_rows == r

            def matches(inner_ref, found, n):
                def panel_step(panel, n):
                    out_count = win_ref[out_at, 0, counts_at + panel]
                    inner_count = inner_ref[row, 0, counts_at + panel]

                    def inner_step(t, n):
                        column = inner_ref[row, 0, panel * slots + t]

                        def out_step(s, n):
                            hit = win_ref[out_at, 0, panel * slots + s] == column
                            found(hit, n, panel, t, s)
                            return n + hit.astype(jnp.int32)

                        return lax.fori_loop(0, out_count, out_step, n)

                    return lax.fori_loop(0, inner_count, inner_step, n)

                return lax.fori_loop(0, panels, panel_step, n)

            def keep(hit, n, panel, t, s):
                @pl.when(hit)
                def _():
                    codes_ref[q, 0, HEAD + n] = a * counts_at + panel * slots + s
                    codes_ref[q, 0, SOURCE + n] = (row * panels + panel) * slots + t

                @pl.when(hit & (n < room))
                def _():
                    entry(q, jnp.where(from_back, limit - 1 - n, n), row, panel, t).start()

            def skip(hit, n, panel, t, s):
                pass

            n, other = counts
            return lax.cond(
                mine,
                lambda: (matches(local_ref, keep, n), other),
                lambda: (n, matches(sibling_ref, skip, other)),
            )

        zero = jnp.int32(0)
        n, other = lax.fori_loop(0, left_count, left_step, (zero, zero))
        codes_ref[q, 0, 0] = n
        total = jnp.where(on_chip, n, n + other)
        over = ((total > limit_q) & (q != me_q)).astype(jnp.int32)
        return too_long | over, copies + jnp.minimum(n, room)

    zero = jnp.int32(0)
    too_long, copies = lax.fori_loop(0, window, pack_row, (zero, zero))

    @pl.loop(0, window)
    def _(q):
        codes_ref[q, 0, 1] = too_long

    @pl.loop(0, copies)
    def _(n):
        entry(0, 0, 0, 0, 0).wait()


def pack_lists(win, local, sibling, blocks, sizes, short, capacity):
    local_rows, panels, slots, size, _ = blocks.shape
    window = sizes[0] * sizes[2]
    smem = pl.BlockSpec(memory_space=pltpu.SMEM)
    return pl.pallas_call(
        functools.partial(pack_kernel, sizes, (local_rows, panels, slots), short),
        out_shape=(
            jax.ShapeDtypeStruct((window, capacity, size, size), jnp.float32),
            jax.ShapeDtypeStruct((window, 1, LANES), jnp.int32),
        ),
        in_specs=[smem, smem, smem, pl.BlockSpec(memory_space=pltpu.HBM)],
        out_specs=(pl.BlockSpec(memory_space=pltpu.VMEM), smem),
        scratch_shapes=[pltpu.SemaphoreType.DMA],
        compiler_params=pltpu.CompilerParams(vmem_limit_bytes=VMEM_LIMIT),
    )(win, local, sibling, blocks)


def exchange_kernel(
    sizes, panels, short, pack_ref, codes_ref, blocks_ref,
    got_ref, got_codes_ref, lefts_ref,
    merged_ref, code_send, code_recv, left_send, left_recv,
    swap_send, swap_recv, list_send, list_recv, own_sem,
):
    rows, cols, depths = sizes
    window = rows * depths
    capacity = pack_ref.shape[1]
    left_ref = blocks_ref.at[0]
    r, c, d = position()
    me = r * depths + d
    diag = d // panels == c
    parts = [(0, short)]
    if capacity > short:
        parts.append((short, capacity - short))

    barrier = pltpu.get_barrier_semaphore()

    @pl.loop(1, window)
    def _(off):
        q = (me + off) % window
        pl.semaphore_signal(barrier, inc=1, device_id=(q // depths, c, q % depths), device_id_type=MESH)

    @pl.loop(1, cols)
    def _(off):
        pl.semaphore_signal(barrier, inc=1, device_id=(r, (c + off) % cols, d), device_id_type=MESH)

    own = [
        pltpu.make_async_copy(codes_ref.at[me], got_codes_ref.at[me], own_sem.at[0]),
        pltpu.make_async_copy(left_ref, lefts_ref.at[c], own_sem.at[1]),
    ]
    for copy in own:
        copy.start()
    pl.semaphore_wait(barrier, window - 1 + cols - 1)

    def remote(src, dst, send, recv, device):
        return pltpu.make_async_remote_copy(
            src_ref=src, dst_ref=dst, send_sem=send, recv_sem=recv,
            device_id=device, device_id_type=MESH,
        )

    begin, pass_on, end = spread(
        cols, blocks_ref.shape[2], left_ref, lefts_ref, left_send, left_recv
    )

    def code_copy(slot, other):
        return remote(
            codes_ref.at[other], got_codes_ref.at[slot], code_send.at[other], code_recv.at[slot],
            (other // depths, c, other % depths),
        )

    def swap_copy(part, depth):
        first, length = parts[part]
        there = pl.ds(first, length)
        return remote(
            pack_ref.at[(1 - r) * depths + depth, there], merged_ref.at[depth, there],
            swap_send.at[part, depth], swap_recv.at[part, depth], (1 - r, c, d),
        )

    def chip_copy():
        return remote(
            pack_ref.at[(1 - r) * depths + d], got_ref.at[d],
            swap_send.at[0, d], swap_recv.at[0, d], (1 - r, c, d),
        )

    def list_copy(part, slot, depth):
        first, length = parts[part]
        there = pl.ds(first, length)
        return remote(
            merged_ref.at[depth, there], got_ref.at[slot, there],
            list_send.at[part, depth], list_recv.at[part, slot], (r, c, depth),
        )

    def each_part(wide, action):
        action(0)
        if len(parts) > 1:
            @pl.when(wide)
            def _():
                action(1)

    @pl.loop(1, depths)
    def _(off):
        depth = (d + off) % depths
        each_part(diag, lambda part: swap_copy(part, depth).start())

    begin()

    @pl.loop(1, depths)
    def _(off):
        depth = (d + off) % depths

        def forward(part):
            swap_copy(part, depth).wait_recv()
            first, length = parts[part]
            q = r * depths + depth
            count = jnp.broadcast_to(codes_ref[q, 0:1, 0:1], pack_ref.shape[2:])
            for place in range(first, first + length):
                rank = jnp.where(r == 1, jnp.where(diag, capacity, short) - 1 - place, place)
                merged_ref[depth, place] = jnp.where(
                    rank < count, pack_ref[q, place], merged_ref[depth, place]
                )
            list_copy(part, d, depth).start()

        each_part(diag, forward)

    chip_copy().start()

    @pl.loop(1, window)
    def _(off):
        code_copy(me, (me + off) % window).start()

    for copy in own:
        copy.wait()

    pass_on()
    end()

    @pl.loop(1, window)
    def _(off):
        other = (me + off) % window
        code_copy(other, other).wait_recv()
        code_copy(me, other).wait_send()

    chip_copy().wait()

    @pl.loop(1, depths)
    def _(off):
        depth = (d + off) % depths
        each_part(diag, lambda part: swap_copy(part, depth).wait_send())
        each_part(depth // panels == c, lambda part: list_copy(part, depth, depth).wait_recv())
        each_part(diag, lambda part: list_copy(part, d, depth).wait_send())


def exchange(pack, codes, blocks, sizes, short, ident):
    window, capacity, size, _ = pack.shape
    rows, cols, depths = sizes
    panels = blocks.shape[1]
    vmem = pl.BlockSpec(memory_space=pltpu.VMEM)
    lists = (depths, capacity, size, size)
    sem = pltpu.SemaphoreType.DMA
    return pl.pallas_call(
        functools.partial(exchange_kernel, sizes, panels, short),
        out_shape=(
            jax.ShapeDtypeStruct(lists, jnp.float32),
            jax.ShapeDtypeStruct(codes.shape, jnp.int32),
            jax.ShapeDtypeStruct((cols,) + blocks.shape[1:], jnp.float32),
        ),
        in_specs=[vmem, vmem, pl.BlockSpec(memory_space=pltpu.HBM)],
        out_specs=(vmem,) * 3,
        scratch_shapes=[
            pltpu.VMEM(lists, jnp.float32),
            sem((window,)), sem((window,)), sem((2, max(3, cols))), sem((2, cols)),
            sem((2, depths)), sem((2, depths)), sem((2, depths)), sem((2, depths)), sem((2,)),
        ],
        compiler_params=pltpu.CompilerParams(
            collective_id=ident, has_side_effects=True, vmem_limit_bytes=VMEM_LIMIT
        ),
    )(pack, codes, blocks)


def multiply_into(acc_ref, lefts_ref, got_ref, blocks_ref, codes_ref, held, sems, sizes, short):
    rows, cols, depths = sizes
    window = rows * depths
    capacity = got_ref.shape[1]
    panels, slots = blocks_ref.shape[1:3]
    out_slots = panels * slots
    r, c, d = position()
    me_q = r * depths + d
    own = codes_ref[me_q, 0, 0]

    def fetch(n):
        at = codes_ref[me_q, 0, SOURCE + n]
        row = at // out_slots
        block = blocks_ref.at[row, (at // slots) % panels, at % slots]
        return pltpu.make_async_copy(block, held.at[n], sems.at[n])

    @pl.loop(0, own)
    def _(n):
        fetch(n).start()

    acc_ref[...] = jnp.zeros_like(acc_ref)

    def add(q, n, right):
        code = codes_ref[q, 0, HEAD + n]
        depth = q % depths
        left = lefts_ref[depth // panels, depth % panels, code // out_slots]
        s = code % out_slots
        acc_ref[s // slots, s % slots] += jnp.dot(
            left, right, precision=lax.Precision.HIGHEST, preferred_element_type=jnp.float32
        )

    @pl.loop(0, window)
    def _(q):
        depth = q % depths
        on_chip = depth == d
        room = jnp.where(on_chip | (depth // panels == c), capacity, short)
        from_back = (q // depths == 1) & jnp.logical_not(on_chip)
        count = jnp.where(q == me_q, 0, jnp.minimum(codes_ref[q, 0, 0], room))

        @pl.loop(0, count)
        def _(n):
            add(q, n, got_ref[depth, jnp.where(from_back, room - 1 - n, n)])

    @pl.loop(0, own)
    def _(n):
        fetch(n).wait()
        add(me_q, n, held[n])


def square_kernel(
    sizes, short, codes_ref, got_ref, blocks_ref, lefts_ref, out_ref, flag_ref, held, sems
):
    flag = lax.fori_loop(0, codes_ref.shape[0], lambda q, f: f | codes_ref[q, 0, 1], jnp.int32(0))
    flag_ref[...] = jnp.full(flag_ref.shape, flag, jnp.int32)
    multiply_into(out_ref, lefts_ref, got_ref, blocks_ref, codes_ref, held, sems, sizes, short)


def cube_kernel(
    sizes, short, codes_ref, got_ref, blocks_ref, lefts_ref, square_ref, out_ref, held, sems
):
    multiply_into(out_ref, lefts_ref, got_ref, blocks_ref, codes_ref, held, sems, sizes, short)
    out_ref[...] = 3.0 * square_ref[...] - 2.0 * out_ref[...]


def local_product(kernel, codes, got, blocks, lefts, extra, out_shape, out_specs):
    vmem = pl.BlockSpec(memory_space=pltpu.VMEM)
    _, panels, slots, size, _ = blocks.shape
    most = slots * slots * panels
    return pl.pallas_call(
        kernel,
        out_shape=out_shape,
        in_specs=[
            pl.BlockSpec(memory_space=pltpu.SMEM),
            vmem,
            pl.BlockSpec(memory_space=pltpu.HBM),
            vmem,
        ] + [vmem] * len(extra),
        out_specs=out_specs,
        scratch_shapes=[
            pltpu.VMEM((most, size, size), jnp.float32),
            pltpu.SemaphoreType.DMA((most,)),
        ],
        compiler_params=pltpu.CompilerParams(vmem_limit_bytes=VMEM_LIMIT),
    )(codes, got, blocks, lefts, *extra)


def gather_kernel(
    cols, square_ref, flag_ref, squares_ref, any_ref, flags_ref,
    send_sem, recv_sem, flag_send, flag_recv, own_sem,
):
    r, c, d = position()
    barrier = pltpu.get_barrier_semaphore()

    @pl.loop(1, cols)
    def _(off):
        pl.semaphore_signal(barrier, inc=1, device_id=(r, (c + off) % cols, d), device_id_type=MESH)

    own = [
        pltpu.make_async_copy(square_ref, squares_ref.at[c], own_sem.at[0]),
        pltpu.make_async_copy(flag_ref, flags_ref.at[c], own_sem.at[1]),
    ]
    for copy in own:
        copy.start()
    begin, pass_on, end = spread(
        cols, square_ref.shape[1], square_ref, squares_ref, send_sem, recv_sem
    )
    pl.semaphore_wait(barrier, cols - 1)

    def flag_copy(slot, other):
        return pltpu.make_async_remote_copy(
            src_ref=flag_ref,
            dst_ref=flags_ref.at[slot],
            send_sem=flag_send.at[other],
            recv_sem=flag_recv.at[slot],
            device_id=(r, other, d),
            device_id_type=MESH,
        )

    begin()

    @pl.loop(1, cols)
    def _(off):
        flag_copy(c, (c + off) % cols).start()

    pass_on()
    for copy in own:
        copy.wait()

    @pl.loop(1, cols)
    def _(off):
        other = (c + off) % cols
        flag_copy(other, other).wait_recv()
        flag_copy(c, other).wait_send()

    end()
    any_ref[...] = jnp.max(flags_ref[...], axis=0)


def gather_square(square, flag, cols, ident):
    vmem = pl.BlockSpec(memory_space=pltpu.VMEM)
    return pl.pallas_call(
        functools.partial(gather_kernel, cols),
        out_shape=(
            jax.ShapeDtypeStruct((cols,) + square.shape, jnp.float32),
            jax.ShapeDtypeStruct(flag.shape, jnp.int32),
        ),
        in_specs=[vmem] * 2,
        out_specs=(vmem,) * 2,
        scratch_shapes=[
            pltpu.VMEM((cols,) + flag.shape, jnp.int32),
            pltpu.SemaphoreType.DMA((2, max(3, cols))),
            pltpu.SemaphoreType.DMA((2, cols)),
            pltpu.SemaphoreType.DMA((cols,)),
            pltpu.SemaphoreType.DMA((cols,)),
            pltpu.SemaphoreType.DMA((2,)),
        ],
        compiler_params=pltpu.CompilerParams(collective_id=ident, has_side_effects=True),
    )(square, flag)


def body(sizes, blocks, columns, counts):
    rows, cols, depths = sizes
    local_rows, panels, slots, size, _ = blocks.shape
    most = slots * slots * panels
    local = jnp.concatenate([columns.reshape(local_rows, 1, panels * slots), counts[:, None, :]], 2)
    local = jnp.pad(local, ((0, 0), (0, 0), (0, LANES - local.shape[2])))
    win, sibling = gather_meta(local, sizes, panels)
    block_shape = jax.ShapeDtypeStruct(blocks.shape[1:], jnp.float32)
    vmem = pl.BlockSpec(memory_space=pltpu.VMEM)

    def square_step(short, capacity, ident):
        pack, codes = pack_lists(win, local, sibling, blocks, sizes, short, capacity)
        got, got_codes, lefts = exchange(pack, codes, blocks, sizes, short, ident)
        square, flag = local_product(
            functools.partial(square_kernel, sizes, short),
            got_codes, got, blocks, lefts, (),
            (block_shape, jax.ShapeDtypeStruct((1, LANES), jnp.int32)),
            (vmem, vmem),
        )
        squares, too_long = gather_square(square, flag, cols, ident + 1)
        return got, got_codes, square, squares, too_long

    def cube_step(short, got, got_codes, square, squares):
        return local_product(
            functools.partial(cube_kernel, sizes, short),
            got_codes, got, blocks, squares, (square,), block_shape, vmem,
        )

    short = min(SHORT, most)
    *lists, too_long = square_step(short, min(SHORT_DIAG, most), 1)

    def again():
        *lists, _ = square_step(most, most, 3)
        return cube_step(most, *lists)

    out = lax.cond(too_long[0, 0] != 0, again, lambda: cube_step(short, *lists))
    return out[None]


def solution(mesh):
    placed = (
        P(("row", "depth"), "col", None, None, None),
        P(("row", "depth"), "col", None),
        P(("row", "depth"), "col"),
    )
    sizes = (mesh.shape["row"], mesh.shape["col"], mesh.shape["depth"])
    return jax.shard_map(
        functools.partial(body, sizes),
        mesh=mesh,
        in_specs=placed,
        out_specs=P(("row", "depth"), "col", None, None, None),
        check_vma=False,
    )
```

```python
import functools

import jax
import jax.numpy as jnp
from jax import lax
from jax.experimental import pallas as pl
from jax.experimental.pallas import tpu as pltpu
from jax.sharding import PartitionSpec as P

MESH = pl.DeviceIdType.MESH
LANES = 128
VMEM_LIMIT = 48 << 20
TIERS = ((2, 6), (4, 8))
HEAD = 2
SOURCE = LANES // 2


def position():
    return lax.axis_index("row"), lax.axis_index("col"), lax.axis_index("depth")


def spread(cols, slots, src_ref, dst_ref, send, recv):
    r, c, d = position()

    def remote(src, dst, send, recv, column):
        return pltpu.make_async_remote_copy(
            src_ref=src, dst_ref=dst, send_sem=send, recv_sem=recv,
            device_id=(r, column, d), device_id_type=MESH,
        )

    if cols != 4 or slots % 2:
        def copy(slot, other):
            return remote(src_ref, dst_ref.at[slot], send.at[0, other], recv.at[0, slot], other)

        def begin():
            @pl.loop(1, cols)
            def _(off):
                copy(c, (c + off) % cols).start()

        def end():
            @pl.loop(1, cols)
            def _(off):
                other = (c + off) % cols
                copy(other, other).wait_recv()
                copy(c, other).wait_send()

        return begin, lambda: None, end

    def half(ref, h):
        return ref.at[:, pl.ds(h * (slots // 2), slots // 2)]

    def direct(h, way):
        return remote(
            half(src_ref, h), half(dst_ref.at[c], h), send.at[h, way - 1], recv.at[h, c], c ^ way
        )

    def arrival(h, way):
        there = half(dst_ref.at[c ^ way], h)
        return remote(half(src_ref, h), there, send.at[h, 0], recv.at[h, c ^ way], c ^ 1)

    def onward(h):
        origin = c ^ (1 + h)
        there = half(dst_ref.at[origin], h)
        return remote(there, there, send.at[h, 2], recv.at[h, origin], c ^ (2 - h))

    sent = [(0, 1), (1, 2), (1, 1), (0, 2)]

    def begin():
        for h, way in sent:
            direct(h, way).start()

    def pass_on():
        for h in (0, 1):
            arrival(h, 1 + h).wait_recv()
            onward(h).start()

    def end():
        for h, way in ((1, 1), (0, 2), (0, 3), (1, 3)):
            arrival(h, way).wait_recv()
        for h, way in sent:
            direct(h, way).wait_send()
        for h in (0, 1):
            onward(h).wait_send()

    return begin, pass_on, end


def meta_kernel(
    sizes, panels, local_ref, all_ref, sibling_ref, send_sem, recv_sem, own_sem, swap_sems
):
    rows, cols, depths = sizes
    window = rows * depths
    r, c, d = position()
    me_q = r * depths + d
    owner = d // panels
    meta_ref = local_ref.at[0]

    def column_mate(off):
        q = (me_q + off) % window
        return q, c

    def inner_mate(i):
        col = (c + 1 + i // (rows * panels)) % cols
        row = (i // panels) % rows
        return row * depths + c * panels + i % panels, col

    def left_source(i):
        return i, owner

    mates = window - 1
    inner = rows * panels * (cols - 1)
    sources = jnp.where(owner == c, 0, window)

    def device(q, col):
        return (q // depths, col, q % depths)

    barrier = pltpu.get_barrier_semaphore()

    def greet(q, col):
        pl.semaphore_signal(barrier, inc=1, device_id=device(q, col), device_id_type=MESH)

    @pl.loop(1, window)
    def _(off):
        greet(*column_mate(off))

    @pl.loop(0, sources)
    def _(i):
        greet(*left_source(i))

    own = pltpu.make_async_copy(meta_ref, all_ref.at[me_q * cols + c], own_sem)
    own.start()
    pl.semaphore_wait(barrier, mates + inner)

    def copy(slot, q, col):
        return pltpu.make_async_remote_copy(
            src_ref=meta_ref,
            dst_ref=all_ref.at[slot],
            send_sem=send_sem.at[q * cols + col],
            recv_sem=recv_sem.at[slot],
            device_id=device(q, col),
            device_id_type=MESH,
        )

    me = me_q * cols + c
    swap = pltpu.make_async_remote_copy(
        src_ref=local_ref,
        dst_ref=sibling_ref,
        send_sem=swap_sems.at[0],
        recv_sem=swap_sems.at[1],
        device_id=(1 - r, c, d),
        device_id_type=MESH,
    )

    @pl.loop(0, inner)
    def _(i):
        copy(me, *inner_mate(i)).start()

    @pl.loop(1, window)
    def _(off):
        copy(me, *column_mate(off)).start()

    swap.start()
    own.wait()

    @pl.loop(1, window)
    def _(off):
        q, col = column_mate(off)
        copy(q * cols + col, q, col).wait_recv()
        copy(me, q, col).wait_send()

    @pl.loop(0, sources)
    def _(i):
        q, col = left_source(i)
        copy(q * cols + col, q, col).wait_recv()

    @pl.loop(0, inner)
    def _(i):
        copy(me, *inner_mate(i)).wait_send()

    swap.wait()


def gather_meta(local, sizes, panels):
    devices = sizes[0] * sizes[1] * sizes[2]
    return pl.pallas_call(
        functools.partial(meta_kernel, sizes, panels),
        out_shape=(
            jax.ShapeDtypeStruct((devices, 1, LANES), jnp.int32),
            jax.ShapeDtypeStruct(local.shape, jnp.int32),
        ),
        in_specs=[pl.BlockSpec(memory_space=pltpu.VMEM)],
        out_specs=(pl.BlockSpec(memory_space=pltpu.VMEM),) * 2,
        scratch_shapes=[
            pltpu.SemaphoreType.DMA((devices,)),
            pltpu.SemaphoreType.DMA((devices,)),
            pltpu.SemaphoreType.DMA,
            pltpu.SemaphoreType.DMA((2,)),
        ],
        compiler_params=pltpu.CompilerParams(collective_id=0, has_side_effects=True),
    )(local)


def pack_kernel(
    sizes, dims, short, win_ref, local_ref, sibling_ref, blocks_ref, pack_ref, codes_ref, sem
):
    rows, cols, depths = sizes
    local_rows, panels, slots = dims
    window = rows * depths
    capacity = pack_ref.shape[1]
    r, c, d = position()
    me_q = r * depths + d
    owner = d // panels
    left_panel = d % panels
    counts_at = panels * slots
    limit = jnp.where(owner == c, capacity, short)

    def entry(q, n, row, panel, slot):
        return pltpu.make_async_copy(blocks_ref.at[row, panel, slot], pack_ref.at[q, n], sem)

    def pack_row(q, carry):
        too_long, copies = carry
        left_at = q * cols + owner
        out_at = q * cols + c
        left_count = win_ref[left_at, 0, counts_at + left_panel]
        on_chip = q % depths == d
        limit_q = jnp.where(on_chip, capacity, limit)
        room = jnp.where(q == me_q, 0, limit_q)
        from_back = (r == 1) & jnp.logical_not(on_chip)

        def left_step(a, counts):
            place = win_ref[left_at, 0, left_panel * slots + a]
            row = place % local_rows
            mine = place // local_rows == r

            def matches(inner_ref, found, n):
                def panel_step(panel, n):
                    out_count = win_ref[out_at, 0, counts_at + panel]
                    inner_count = inner_ref[row, 0, counts_at + panel]

                    def inner_step(t, n):
                        column = inner_ref[row, 0, panel * slots + t]

                        def out_step(s, n):
                            hit = win_ref[out_at, 0, panel * slots + s] == column
                            found(hit, n, panel, t, s)
                            return n + hit.astype(jnp.int32)

                        return lax.fori_loop(0, out_count, out_step, n)

                    return lax.fori_loop(0, inner_count, inner_step, n)

                return lax.fori_loop(0, panels, panel_step, n)

            def keep(hit, n, panel, t, s):
                @pl.when(hit)
                def _():
                    codes_ref[q, 0, HEAD + n] = a * counts_at + panel * slots + s
                    codes_ref[q, 0, SOURCE + n] = (row * panels + panel) * slots + t

                @pl.when(hit & (n < room))
                def _():
                    entry(q, jnp.where(from_back, limit - 1 - n, n), row, panel, t).start()

            def skip(hit, n, panel, t, s):
                pass

            n, other = counts
            return lax.cond(
                mine,
                lambda: (matches(local_ref, keep, n), other),
                lambda: (n, matches(sibling_ref, skip, other)),
            )

        zero = jnp.int32(0)
        n, other = lax.fori_loop(0, left_count, left_step, (zero, zero))
        codes_ref[q, 0, 0] = n
        total = jnp.where(on_chip, n, n + other)
        over = ((total > limit_q) & (q != me_q)).astype(jnp.int32)
        return too_long | over, copies + jnp.minimum(n, room)

    zero = jnp.int32(0)
    too_long, copies = lax.fori_loop(0, window, pack_row, (zero, zero))

    @pl.loop(0, window)
    def _(q):
        codes_ref[q, 0, 1] = too_long

    @pl.loop(0, copies)
    def _(n):
        entry(0, 0, 0, 0, 0).wait()


def pack_lists(win, local, sibling, blocks, sizes, short, capacity):
    local_rows, panels, slots, size, _ = blocks.shape
    window = sizes[0] * sizes[2]
    smem = pl.BlockSpec(memory_space=pltpu.SMEM)
    return pl.pallas_call(
        functools.partial(pack_kernel, sizes, (local_rows, panels, slots), short),
        out_shape=(
            jax.ShapeDtypeStruct((window, capacity, size, size), jnp.float32),
            jax.ShapeDtypeStruct((window, 1, LANES), jnp.int32),
        ),
        in_specs=[smem, smem, smem, pl.BlockSpec(memory_space=pltpu.HBM)],
        out_specs=(pl.BlockSpec(memory_space=pltpu.VMEM), smem),
        scratch_shapes=[pltpu.SemaphoreType.DMA],
        compiler_params=pltpu.CompilerParams(vmem_limit_bytes=VMEM_LIMIT),
    )(win, local, sibling, blocks)


def exchange_kernel(
    sizes, panels, short, pack_ref, codes_ref, blocks_ref,
    got_ref, got_codes_ref, lefts_ref,
    merged_ref, code_send, code_recv, left_send, left_recv,
    swap_send, swap_recv, list_send, list_recv, relay_ref, relay_send, relay_recv, own_sem,
):
    rows, cols, depths = sizes
    window = rows * depths
    capacity = pack_ref.shape[1]
    left_ref = blocks_ref.at[0]
    r, c, d = position()
    me = r * depths + d
    diag = d // panels == c
    parts = [(0, short, 0)]
    extra = capacity - short
    ways = [1, 2] if cols == 4 and extra >= 4 else []
    straight = extra // 4 if ways else extra
    if extra:
        parts.append((short, straight, 0))
    if ways:
        parts.append((short + straight, straight, 1))
        parts.append((short + 2 * straight, extra - 2 * straight, 2))

    barrier = pltpu.get_barrier_semaphore()

    @pl.loop(1, window)
    def _(off):
        q = (me + off) % window
        pl.semaphore_signal(barrier, inc=1, device_id=(q // depths, c, q % depths), device_id_type=MESH)

    @pl.loop(1, cols)
    def _(off):
        pl.semaphore_signal(barrier, inc=1, device_id=(r, (c + off) % cols, d), device_id_type=MESH)

    for way in ways:
        @pl.loop(1, depths)
        def _(off):
            device = (r, c ^ way, (d + off) % depths)
            pl.semaphore_signal(barrier, inc=1, device_id=device, device_id_type=MESH)

    own = [
        pltpu.make_async_copy(codes_ref.at[me], got_codes_ref.at[me], own_sem.at[0]),
        pltpu.make_async_copy(left_ref, lefts_ref.at[c], own_sem.at[1]),
    ]
    for copy in own:
        copy.start()
    pl.semaphore_wait(barrier, window - 1 + cols - 1 + len(ways) * (depths - 1))

    def remote(src, dst, send, recv, device):
        return pltpu.make_async_remote_copy(
            src_ref=src, dst_ref=dst, send_sem=send, recv_sem=recv,
            device_id=device, device_id_type=MESH,
        )

    begin, pass_on, end = spread(
        cols, blocks_ref.shape[2], left_ref, lefts_ref, left_send, left_recv
    )

    def code_copy(slot, other):
        return remote(
            codes_ref.at[other], got_codes_ref.at[slot], code_send.at[other], code_recv.at[slot],
            (other // depths, c, other % depths),
        )

    def swap_copy(part, depth):
        first, length, way = parts[part]
        there = pl.ds(first, length)
        return remote(
            pack_ref.at[(1 - r) * depths + depth, there], merged_ref.at[depth, there],
            swap_send.at[part, depth], swap_recv.at[part, depth], (1 - r, c, d),
        )

    def chip_copy():
        return remote(
            pack_ref.at[(1 - r) * depths + d], got_ref.at[d],
            swap_send.at[0, d], swap_recv.at[0, d], (1 - r, c, d),
        )

    def list_copy(part, slot, depth):
        first, length, way = parts[part]
        there = pl.ds(first, length)
        if way:
            target, device = relay_ref.at[way - 1, depth, pl.ds(0, length)], (r, c ^ way, d)
        else:
            target, device = got_ref.at[slot, there], (r, c, depth)
        return remote(
            merged_ref.at[depth, there], target,
            list_send.at[part, depth], list_recv.at[part, depth if way else slot], device,
        )

    def relay_copy(part, slot, depth):
        first, length, way = parts[part]
        return remote(
            relay_ref.at[way - 1, depth, pl.ds(0, length)],
            got_ref.at[slot, pl.ds(first, length)],
            relay_send.at[part, depth], relay_recv.at[part, slot], (r, c ^ way, depth),
        )

    def arrival(part, depth):
        copy = relay_copy if parts[part][2] else list_copy
        return copy(part, depth, depth)

    def each_part(wide, action):
        if len(parts) > 1:
            @pl.when(wide)
            def _():
                for part in reversed(range(1, len(parts))):
                    action(part)
        action(0)

    def each_relay(action):
        for part, (first, length, way) in enumerate(parts):
            if way:
                @pl.when(d // panels == c ^ way)
                def _():
                    @pl.loop(1, depths)
                    def _(off):
                        action(part, (d + off) % depths)

    @pl.loop(1, depths)
    def _(off):
        depth = (d + off) % depths
        each_part(diag, lambda part: swap_copy(part, depth).start())

    @pl.loop(1, depths)
    def _(off):
        depth = (d + off) % depths

        def forward(part):
            swap_copy(part, depth).wait_recv()
            first, length, way = parts[part]
            q = r * depths + depth
            count = jnp.broadcast_to(codes_ref[q, 0:1, 0:1], pack_ref.shape[2:])
            for place in range(first, first + length):
                rank = jnp.where(r == 1, jnp.where(diag, capacity, short) - 1 - place, place)
                merged_ref[depth, place] = jnp.where(
                    rank < count, pack_ref[q, place], merged_ref[depth, place]
                )
            list_copy(part, d, depth).start()

        each_part(diag, forward)

    begin()
    chip_copy().start()

    @pl.loop(1, window)
    def _(off):
        code_copy(me, (me + off) % window).start()

    def relay(part, depth):
        list_copy(part, d, depth).wait_recv()
        relay_copy(part, d, depth).start()

    each_relay(relay)

    for copy in own:
        copy.wait()

    pass_on()
    end()

    @pl.loop(1, window)
    def _(off):
        other = (me + off) % window
        code_copy(other, other).wait_recv()
        code_copy(me, other).wait_send()

    chip_copy().wait()

    @pl.loop(1, depths)
    def _(off):
        depth = (d + off) % depths
        each_part(diag, lambda part: swap_copy(part, depth).wait_send())
        each_part(depth // panels == c, lambda part: arrival(part, depth).wait_recv())
        each_part(diag, lambda part: list_copy(part, d, depth).wait_send())

    each_relay(lambda part, depth: relay_copy(part, d, depth).wait_send())


def exchange(pack, codes, blocks, sizes, short, ident):
    window, capacity, size, _ = pack.shape
    rows, cols, depths = sizes
    panels = blocks.shape[1]
    vmem = pl.BlockSpec(memory_space=pltpu.VMEM)
    lists = (depths, capacity, size, size)
    sem = pltpu.SemaphoreType.DMA
    return pl.pallas_call(
        functools.partial(exchange_kernel, sizes, panels, short),
        out_shape=(
            jax.ShapeDtypeStruct(lists, jnp.float32),
            jax.ShapeDtypeStruct(codes.shape, jnp.int32),
            jax.ShapeDtypeStruct((cols,) + blocks.shape[1:], jnp.float32),
        ),
        in_specs=[vmem, vmem, pl.BlockSpec(memory_space=pltpu.HBM)],
        out_specs=(vmem,) * 3,
        scratch_shapes=[
            pltpu.VMEM(lists, jnp.float32),
            sem((window,)), sem((window,)), sem((2, max(3, cols))), sem((2, cols)),
            sem((4, depths)), sem((4, depths)), sem((4, depths)), sem((4, depths)),
            pltpu.VMEM((2, depths, max(1, (capacity - short) // 2), size, size), jnp.float32),
            sem((4, depths)), sem((4, depths)), sem((2,)),
        ],
        compiler_params=pltpu.CompilerParams(
            collective_id=ident, has_side_effects=True, vmem_limit_bytes=VMEM_LIMIT
        ),
    )(pack, codes, blocks)


def multiply_into(acc_ref, lefts_ref, got_ref, blocks_ref, codes_ref, held, sems, sizes, short):
    rows, cols, depths = sizes
    window = rows * depths
    capacity = got_ref.shape[1]
    panels, slots = blocks_ref.shape[1:3]
    out_slots = panels * slots
    r, c, d = position()
    me_q = r * depths + d
    own = codes_ref[me_q, 0, 0]

    def fetch(n):
        at = codes_ref[me_q, 0, SOURCE + n]
        row = at // out_slots
        block = blocks_ref.at[row, (at // slots) % panels, at % slots]
        return pltpu.make_async_copy(block, held.at[n], sems.at[n])

    @pl.loop(0, own)
    def _(n):
        fetch(n).start()

    acc_ref[...] = jnp.zeros_like(acc_ref)

    def add(q, n, right):
        code = codes_ref[q, 0, HEAD + n]
        depth = q % depths
        left = lefts_ref[depth // panels, depth % panels, code // out_slots]
        s = code % out_slots
        acc_ref[s // slots, s % slots] += jnp.dot(
            left, right, precision=lax.Precision.HIGHEST, preferred_element_type=jnp.float32
        )

    @pl.loop(0, window)
    def _(q):
        depth = q % depths
        on_chip = depth == d
        room = jnp.where(on_chip | (depth // panels == c), capacity, short)
        from_back = (q // depths == 1) & jnp.logical_not(on_chip)
        count = jnp.where(q == me_q, 0, jnp.minimum(codes_ref[q, 0, 0], room))

        @pl.loop(0, count)
        def _(n):
            add(q, n, got_ref[depth, jnp.where(from_back, room - 1 - n, n)])

    @pl.loop(0, own)
    def _(n):
        fetch(n).wait()
        add(me_q, n, held[n])


def square_kernel(
    sizes, short, codes_ref, got_ref, blocks_ref, lefts_ref, out_ref, flag_ref, held, sems
):
    flag = lax.fori_loop(0, codes_ref.shape[0], lambda q, f: f | codes_ref[q, 0, 1], jnp.int32(0))
    flag_ref[...] = jnp.full(flag_ref.shape, flag, jnp.int32)
    multiply_into(out_ref, lefts_ref, got_ref, blocks_ref, codes_ref, held, sems, sizes, short)


def cube_kernel(
    sizes, short, codes_ref, got_ref, blocks_ref, lefts_ref, square_ref, out_ref, held, sems
):
    multiply_into(out_ref, lefts_ref, got_ref, blocks_ref, codes_ref, held, sems, sizes, short)
    out_ref[...] = 3.0 * square_ref[...] - 2.0 * out_ref[...]


def local_product(kernel, codes, got, blocks, lefts, extra, out_shape, out_specs):
    vmem = pl.BlockSpec(memory_space=pltpu.VMEM)
    _, panels, slots, size, _ = blocks.shape
    most = slots * slots * panels
    return pl.pallas_call(
        kernel,
        out_shape=out_shape,
        in_specs=[
            pl.BlockSpec(memory_space=pltpu.SMEM),
            vmem,
            pl.BlockSpec(memory_space=pltpu.HBM),
            vmem,
        ] + [vmem] * len(extra),
        out_specs=out_specs,
        scratch_shapes=[
            pltpu.VMEM((most, size, size), jnp.float32),
            pltpu.SemaphoreType.DMA((most,)),
        ],
        compiler_params=pltpu.CompilerParams(vmem_limit_bytes=VMEM_LIMIT),
    )(codes, got, blocks, lefts, *extra)


def gather_kernel(
    cols, square_ref, flag_ref, squares_ref, any_ref, flags_ref,
    send_sem, recv_sem, flag_send, flag_recv, own_sem,
):
    r, c, d = position()
    barrier = pltpu.get_barrier_semaphore()

    @pl.loop(1, cols)
    def _(off):
        pl.semaphore_signal(barrier, inc=1, device_id=(r, (c + off) % cols, d), device_id_type=MESH)

    own = [
        pltpu.make_async_copy(square_ref, squares_ref.at[c], own_sem.at[0]),
        pltpu.make_async_copy(flag_ref, flags_ref.at[c], own_sem.at[1]),
    ]
    for copy in own:
        copy.start()
    begin, pass_on, end = spread(
        cols, square_ref.shape[1], square_ref, squares_ref, send_sem, recv_sem
    )
    pl.semaphore_wait(barrier, cols - 1)

    def flag_copy(slot, other):
        return pltpu.make_async_remote_copy(
            src_ref=flag_ref,
            dst_ref=flags_ref.at[slot],
            send_sem=flag_send.at[other],
            recv_sem=flag_recv.at[slot],
            device_id=(r, other, d),
            device_id_type=MESH,
        )

    begin()

    @pl.loop(1, cols)
    def _(off):
        flag_copy(c, (c + off) % cols).start()

    pass_on()
    for copy in own:
        copy.wait()

    @pl.loop(1, cols)
    def _(off):
        other = (c + off) % cols
        flag_copy(other, other).wait_recv()
        flag_copy(c, other).wait_send()

    end()
    any_ref[...] = jnp.max(flags_ref[...], axis=0)


def gather_square(square, flag, cols, ident):
    vmem = pl.BlockSpec(memory_space=pltpu.VMEM)
    return pl.pallas_call(
        functools.partial(gather_kernel, cols),
        out_shape=(
            jax.ShapeDtypeStruct((cols,) + square.shape, jnp.float32),
            jax.ShapeDtypeStruct(flag.shape, jnp.int32),
        ),
        in_specs=[vmem] * 2,
        out_specs=(vmem,) * 2,
        scratch_shapes=[
            pltpu.VMEM((cols,) + flag.shape, jnp.int32),
            pltpu.SemaphoreType.DMA((2, max(3, cols))),
            pltpu.SemaphoreType.DMA((2, cols)),
            pltpu.SemaphoreType.DMA((cols,)),
            pltpu.SemaphoreType.DMA((cols,)),
            pltpu.SemaphoreType.DMA((2,)),
        ],
        compiler_params=pltpu.CompilerParams(collective_id=ident, has_side_effects=True),
    )(square, flag)


def body(sizes, blocks, columns, counts):
    rows, cols, depths = sizes
    local_rows, panels, slots, size, _ = blocks.shape
    most = slots * slots * panels
    local = jnp.concatenate([columns.reshape(local_rows, 1, panels * slots), counts[:, None, :]], 2)
    local = jnp.pad(local, ((0, 0), (0, 0), (0, LANES - local.shape[2])))
    win, sibling = gather_meta(local, sizes, panels)
    block_shape = jax.ShapeDtypeStruct(blocks.shape[1:], jnp.float32)
    vmem = pl.BlockSpec(memory_space=pltpu.VMEM)

    def square_step(short, capacity, ident):
        pack, codes = pack_lists(win, local, sibling, blocks, sizes, short, capacity)
        got, got_codes, lefts = exchange(pack, codes, blocks, sizes, short, ident)
        square, flag = local_product(
            functools.partial(square_kernel, sizes, short),
            got_codes, got, blocks, lefts, (),
            (block_shape, jax.ShapeDtypeStruct((1, LANES), jnp.int32)),
            (vmem, vmem),
        )
        squares, too_long = gather_square(square, flag, cols, ident + 1)
        return got, got_codes, square, squares, too_long

    def cube_step(short, got, got_codes, square, squares):
        return local_product(
            functools.partial(cube_kernel, sizes, short),
            got_codes, got, blocks, squares, (square,), block_shape, vmem,
        )

    sizes_tried = []
    for short, capacity in TIERS:
        tier = (min(short, most), min(capacity, most))
        if tier not in sizes_tried:
            sizes_tried.append(tier)
    sizes_tried.append((most, most))

    def attempt(tier):
        short, capacity = sizes_tried[tier]
        *lists, too_long = square_step(short, capacity, 1 + 2 * tier)
        if (short, capacity) == (most, most):
            return cube_step(short, *lists)
        return lax.cond(
            too_long[0, 0] != 0, lambda: attempt(tier + 1), lambda: cube_step(short, *lists)
        )

    out = attempt(0)
    return out[None]


def solution(mesh):
    placed = (
        P(("row", "depth"), "col", None, None, None),
        P(("row", "depth"), "col", None),
        P(("row", "depth"), "col"),
    )
    sizes = (mesh.shape["row"], mesh.shape["col"], mesh.shape["depth"])
    return jax.shard_map(
        functools.partial(body, sizes),
        mesh=mesh,
        in_specs=placed,
        out_specs=P(("row", "depth"), "col", None, None, None),
        check_vma=False,
    )
```

```python
import functools

import jax
import jax.numpy as jnp
from jax import lax
from jax.experimental import pallas as pl
from jax.experimental.pallas import tpu as pltpu
from jax.sharding import PartitionSpec as P

MESH = pl.DeviceIdType.MESH
LANES = 128
VMEM_LIMIT = 48 << 20
TIERS = ((2, 6), (4, 8))
HEAD = 2
SOURCE = LANES // 2


def position():
    return lax.axis_index("row"), lax.axis_index("col"), lax.axis_index("depth")


def spread(cols, slots, src_ref, dst_ref, send, recv):
    r, c, d = position()

    def remote(src, dst, send, recv, column):
        return pltpu.make_async_remote_copy(
            src_ref=src, dst_ref=dst, send_sem=send, recv_sem=recv,
            device_id=(r, column, d), device_id_type=MESH,
        )

    if cols != 4 or slots % 2:
        def copy(slot, other):
            return remote(src_ref, dst_ref.at[slot], send.at[0, other], recv.at[0, slot], other)

        def begin():
            @pl.loop(1, cols)
            def _(off):
                copy(c, (c + off) % cols).start()

        def end():
            @pl.loop(1, cols)
            def _(off):
                other = (c + off) % cols
                copy(other, other).wait_recv()
                copy(c, other).wait_send()

        return begin, lambda: None, end

    def half(ref, h):
        return ref.at[:, pl.ds(h * (slots // 2), slots // 2)]

    def direct(h, way):
        return remote(
            half(src_ref, h), half(dst_ref.at[c], h), send.at[h, way - 1], recv.at[h, c], c ^ way
        )

    def arrival(h, way):
        there = half(dst_ref.at[c ^ way], h)
        return remote(half(src_ref, h), there, send.at[h, 0], recv.at[h, c ^ way], c ^ 1)

    def onward(h):
        origin = c ^ (1 + h)
        there = half(dst_ref.at[origin], h)
        return remote(there, there, send.at[h, 2], recv.at[h, origin], c ^ (2 - h))

    sent = [(0, 1), (1, 2), (1, 1), (0, 2)]

    def begin():
        for h, way in sent:
            direct(h, way).start()

    def pass_on():
        for h in (0, 1):
            arrival(h, 1 + h).wait_recv()
            onward(h).start()

    def end():
        for h, way in ((1, 1), (0, 2), (0, 3), (1, 3)):
            arrival(h, way).wait_recv()
        for h, way in sent:
            direct(h, way).wait_send()
        for h in (0, 1):
            onward(h).wait_send()

    return begin, pass_on, end


def meta_kernel(
    sizes, panels, entries, local_ref, all_ref, sibling_ref, meta_ref,
    send_sem, recv_sem, own_sem, swap_sems,
):
    rows, cols, depths = sizes
    window = rows * depths
    r, c, d = position()
    me_q = r * depths + d
    owner = d // panels
    lanes = lax.broadcasted_iota(jnp.int32, meta_ref.shape, 1)
    meta = jnp.zeros(meta_ref.shape, jnp.int32)
    for j in range(entries):
        value = jnp.broadcast_to(local_ref[j : j + 1, 0:1], meta_ref.shape)
        meta = jnp.where(lanes == j, value, meta)
    meta_ref[...] = meta

    def column_mate(off):
        q = (me_q + off) % window
        return q, c

    def inner_mate(i):
        col = (c + 1 + i // (rows * panels)) % cols
        row = (i // panels) % rows
        return row * depths + c * panels + i % panels, col

    def left_source(i):
        return i, owner

    mates = window - 1
    inner = rows * panels * (cols - 1)
    sources = jnp.where(owner == c, 0, window)

    def device(q, col):
        return (q // depths, col, q % depths)

    barrier = pltpu.get_barrier_semaphore()

    def greet(q, col):
        pl.semaphore_signal(barrier, inc=1, device_id=device(q, col), device_id_type=MESH)

    @pl.loop(1, window)
    def _(off):
        greet(*column_mate(off))

    @pl.loop(0, sources)
    def _(i):
        greet(*left_source(i))

    own = pltpu.make_async_copy(meta_ref, all_ref.at[me_q * cols + c], own_sem)
    own.start()
    pl.semaphore_wait(barrier, mates + inner)

    def copy(slot, q, col):
        return pltpu.make_async_remote_copy(
            src_ref=meta_ref,
            dst_ref=all_ref.at[slot],
            send_sem=send_sem.at[q * cols + col],
            recv_sem=recv_sem.at[slot],
            device_id=device(q, col),
            device_id_type=MESH,
        )

    me = me_q * cols + c
    swap = pltpu.make_async_remote_copy(
        src_ref=local_ref,
        dst_ref=sibling_ref,
        send_sem=swap_sems.at[0],
        recv_sem=swap_sems.at[1],
        device_id=(1 - r, c, d),
        device_id_type=MESH,
    )

    @pl.loop(0, inner)
    def _(i):
        copy(me, *inner_mate(i)).start()

    @pl.loop(1, window)
    def _(off):
        copy(me, *column_mate(off)).start()

    swap.start()
    own.wait()

    @pl.loop(1, window)
    def _(off):
        q, col = column_mate(off)
        copy(q * cols + col, q, col).wait_recv()
        copy(me, q, col).wait_send()

    @pl.loop(0, sources)
    def _(i):
        q, col = left_source(i)
        copy(q * cols + col, q, col).wait_recv()

    @pl.loop(0, inner)
    def _(i):
        copy(me, *inner_mate(i)).wait_send()

    swap.wait()


def gather_meta(local, sizes, panels, entries):
    devices = sizes[0] * sizes[1] * sizes[2]
    return pl.pallas_call(
        functools.partial(meta_kernel, sizes, panels, entries),
        out_shape=(
            jax.ShapeDtypeStruct((devices, 1, LANES), jnp.int32),
            jax.ShapeDtypeStruct(local.shape, jnp.int32),
        ),
        in_specs=[pl.BlockSpec(memory_space=pltpu.VMEM)],
        out_specs=(pl.BlockSpec(memory_space=pltpu.VMEM),) * 2,
        scratch_shapes=[
            pltpu.VMEM((1, LANES), jnp.int32),
            pltpu.SemaphoreType.DMA((devices,)),
            pltpu.SemaphoreType.DMA((devices,)),
            pltpu.SemaphoreType.DMA,
            pltpu.SemaphoreType.DMA((2,)),
        ],
        compiler_params=pltpu.CompilerParams(collective_id=0, has_side_effects=True),
    )(local)


def pack_kernel(
    sizes, dims, short, win_ref, local_ref, sibling_ref, blocks_ref, pack_ref, codes_ref, sem
):
    rows, cols, depths = sizes
    local_rows, panels, slots = dims
    window = rows * depths
    capacity = pack_ref.shape[1]
    r, c, d = position()
    me_q = r * depths + d
    owner = d // panels
    left_panel = d % panels
    counts_at = panels * slots
    limit = jnp.where(owner == c, capacity, short)

    def entry(q, n, row, panel, slot):
        return pltpu.make_async_copy(blocks_ref.at[row, panel, slot], pack_ref.at[q, n], sem)

    def pack_row(q, carry):
        too_long, copies = carry
        left_at = q * cols + owner
        out_at = q * cols + c
        left_count = win_ref[left_at, 0, counts_at + left_panel]
        on_chip = q % depths == d
        limit_q = jnp.where(on_chip, capacity, limit)
        room = jnp.where(q == me_q, 0, limit_q)
        from_back = (r == 1) & jnp.logical_not(on_chip)

        def left_step(a, counts):
            place = win_ref[left_at, 0, left_panel * slots + a]
            row = place % local_rows
            mine = place // local_rows == r

            def matches(inner_ref, found, n):
                def panel_step(panel, n):
                    out_count = win_ref[out_at, 0, counts_at + panel]
                    inner_count = inner_ref[counts_at + panel, row]

                    def inner_step(t, n):
                        column = inner_ref[panel * slots + t, row]

                        def out_step(s, n):
                            hit = win_ref[out_at, 0, panel * slots + s] == column
                            found(hit, n, panel, t, s)
                            return n + hit.astype(jnp.int32)

                        return lax.fori_loop(0, out_count, out_step, n)

                    return lax.fori_loop(0, inner_count, inner_step, n)

                return lax.fori_loop(0, panels, panel_step, n)

            def keep(hit, n, panel, t, s):
                @pl.when(hit)
                def _():
                    codes_ref[q, 0, HEAD + n] = a * counts_at + panel * slots + s
                    codes_ref[q, 0, SOURCE + n] = (row * panels + panel) * slots + t

                @pl.when(hit & (n < room))
                def _():
                    entry(q, jnp.where(from_back, limit - 1 - n, n), row, panel, t).start()

            def skip(hit, n, panel, t, s):
                pass

            n, other = counts
            return lax.cond(
                mine,
                lambda: (matches(local_ref, keep, n), other),
                lambda: (n, matches(sibling_ref, skip, other)),
            )

        zero = jnp.int32(0)
        n, other = lax.fori_loop(0, left_count, left_step, (zero, zero))
        codes_ref[q, 0, 0] = n
        total = jnp.where(on_chip, n, n + other)
        over = ((total > limit_q) & (q != me_q)).astype(jnp.int32)
        return too_long | over, copies + jnp.minimum(n, room)

    zero = jnp.int32(0)
    too_long, copies = lax.fori_loop(0, window, pack_row, (zero, zero))

    @pl.loop(0, window)
    def _(q):
        codes_ref[q, 0, 1] = too_long

    @pl.loop(0, copies)
    def _(n):
        entry(0, 0, 0, 0, 0).wait()


def pack_lists(win, local, sibling, blocks, sizes, short, capacity):
    local_rows, panels, slots, size, _ = blocks.shape
    window = sizes[0] * sizes[2]
    smem = pl.BlockSpec(memory_space=pltpu.SMEM)
    return pl.pallas_call(
        functools.partial(pack_kernel, sizes, (local_rows, panels, slots), short),
        out_shape=(
            jax.ShapeDtypeStruct((window, capacity, size, size), jnp.float32),
            jax.ShapeDtypeStruct((window, 1, LANES), jnp.int32),
        ),
        in_specs=[smem, smem, smem, pl.BlockSpec(memory_space=pltpu.HBM)],
        out_specs=(pl.BlockSpec(memory_space=pltpu.VMEM), smem),
        scratch_shapes=[pltpu.SemaphoreType.DMA],
        compiler_params=pltpu.CompilerParams(vmem_limit_bytes=VMEM_LIMIT),
    )(win, local, sibling, blocks)


def exchange_kernel(
    sizes, panels, short, pack_ref, codes_ref, blocks_ref,
    got_ref, got_codes_ref, lefts_ref,
    merged_ref, code_send, code_recv, left_send, left_recv,
    swap_send, swap_recv, list_send, list_recv, relay_ref, relay_send, relay_recv, own_sem,
):
    rows, cols, depths = sizes
    window = rows * depths
    capacity = pack_ref.shape[1]
    left_ref = blocks_ref.at[0]
    r, c, d = position()
    me = r * depths + d
    diag = d // panels == c
    parts = [(0, short, 0)]
    extra = capacity - short
    ways = [1, 2] if cols == 4 and extra >= 4 else []
    straight = extra // 4 if ways else extra
    if extra:
        parts.append((short, straight, 0))
    if ways:
        parts.append((short + straight, straight, 1))
        parts.append((short + 2 * straight, extra - 2 * straight, 2))

    barrier = pltpu.get_barrier_semaphore()

    @pl.loop(1, window)
    def _(off):
        q = (me + off) % window
        pl.semaphore_signal(barrier, inc=1, device_id=(q // depths, c, q % depths), device_id_type=MESH)

    @pl.loop(1, cols)
    def _(off):
        pl.semaphore_signal(barrier, inc=1, device_id=(r, (c + off) % cols, d), device_id_type=MESH)

    for way in ways:
        @pl.loop(1, depths)
        def _(off):
            device = (r, c ^ way, (d + off) % depths)
            pl.semaphore_signal(barrier, inc=1, device_id=device, device_id_type=MESH)

    own = [
        pltpu.make_async_copy(codes_ref.at[me], got_codes_ref.at[me], own_sem.at[0]),
        pltpu.make_async_copy(left_ref, lefts_ref.at[c], own_sem.at[1]),
    ]
    for copy in own:
        copy.start()
    pl.semaphore_wait(barrier, window - 1 + cols - 1 + len(ways) * (depths - 1))

    def remote(src, dst, send, recv, device):
        return pltpu.make_async_remote_copy(
            src_ref=src, dst_ref=dst, send_sem=send, recv_sem=recv,
            device_id=device, device_id_type=MESH,
        )

    begin, pass_on, end = spread(
        cols, blocks_ref.shape[2], left_ref, lefts_ref, left_send, left_recv
    )

    def code_copy(slot, other):
        return remote(
            codes_ref.at[other], got_codes_ref.at[slot], code_send.at[other], code_recv.at[slot],
            (other // depths, c, other % depths),
        )

    def swap_copy(part, depth):
        first, length, way = parts[part]
        there = pl.ds(first, length)
        return remote(
            pack_ref.at[(1 - r) * depths + depth, there], merged_ref.at[depth, there],
            swap_send.at[part, depth], swap_recv.at[part, depth], (1 - r, c, d),
        )

    def chip_copy():
        return remote(
            pack_ref.at[(1 - r) * depths + d], got_ref.at[d],
            swap_send.at[0, d], swap_recv.at[0, d], (1 - r, c, d),
        )

    def list_copy(part, slot, depth):
        first, length, way = parts[part]
        there = pl.ds(first, length)
        if way:
            target, device = relay_ref.at[way - 1, depth, pl.ds(0, length)], (r, c ^ way, d)
        else:
            target, device = got_ref.at[slot, there], (r, c, depth)
        return remote(
            merged_ref.at[depth, there], target,
            list_send.at[part, depth], list_recv.at[part, depth if way else slot], device,
        )

    def relay_copy(part, slot, depth):
        first, length, way = parts[part]
        return remote(
            relay_ref.at[way - 1, depth, pl.ds(0, length)],
            got_ref.at[slot, pl.ds(first, length)],
            relay_send.at[part, depth], relay_recv.at[part, slot], (r, c ^ way, depth),
        )

    def arrival(part, depth):
        copy = relay_copy if parts[part][2] else list_copy
        return copy(part, depth, depth)

    def each_part(wide, action):
        if len(parts) > 1:
            @pl.when(wide)
            def _():
                for part in reversed(range(1, len(parts))):
                    action(part)
        action(0)

    def each_relay(action):
        for part, (first, length, way) in enumerate(parts):
            if way:
                @pl.when(d // panels == c ^ way)
                def _():
                    @pl.loop(1, depths)
                    def _(off):
                        action(part, (d + off) % depths)

    @pl.loop(1, depths)
    def _(off):
        depth = (d + off) % depths
        each_part(diag, lambda part: swap_copy(part, depth).start())

    @pl.loop(1, depths)
    def _(off):
        depth = (d + off) % depths

        def forward(part):
            swap_copy(part, depth).wait_recv()
            first, length, way = parts[part]
            q = r * depths + depth
            count = jnp.broadcast_to(codes_ref[q, 0:1, 0:1], pack_ref.shape[2:])
            for place in range(first, first + length):
                rank = jnp.where(r == 1, jnp.where(diag, capacity, short) - 1 - place, place)
                merged_ref[depth, place] = jnp.where(
                    rank < count, pack_ref[q, place], merged_ref[depth, place]
                )
            list_copy(part, d, depth).start()

        each_part(diag, forward)

    begin()
    chip_copy().start()

    @pl.loop(1, window)
    def _(off):
        code_copy(me, (me + off) % window).start()

    def relay(part, depth):
        list_copy(part, d, depth).wait_recv()
        relay_copy(part, d, depth).start()

    each_relay(relay)

    for copy in own:
        copy.wait()

    pass_on()
    end()

    @pl.loop(1, window)
    def _(off):
        other = (me + off) % window
        code_copy(other, other).wait_recv()
        code_copy(me, other).wait_send()

    chip_copy().wait()

    @pl.loop(1, depths)
    def _(off):
        depth = (d + off) % depths
        each_part(diag, lambda part: swap_copy(part, depth).wait_send())
        each_part(depth // panels == c, lambda part: arrival(part, depth).wait_recv())
        each_part(diag, lambda part: list_copy(part, d, depth).wait_send())

    each_relay(lambda part, depth: relay_copy(part, d, depth).wait_send())


def exchange(pack, codes, blocks, sizes, short, ident):
    window, capacity, size, _ = pack.shape
    rows, cols, depths = sizes
    panels = blocks.shape[1]
    vmem = pl.BlockSpec(memory_space=pltpu.VMEM)
    lists = (depths, capacity, size, size)
    sem = pltpu.SemaphoreType.DMA
    return pl.pallas_call(
        functools.partial(exchange_kernel, sizes, panels, short),
        out_shape=(
            jax.ShapeDtypeStruct(lists, jnp.float32),
            jax.ShapeDtypeStruct(codes.shape, jnp.int32),
            jax.ShapeDtypeStruct((cols,) + blocks.shape[1:], jnp.float32),
        ),
        in_specs=[vmem, vmem, pl.BlockSpec(memory_space=pltpu.HBM)],
        out_specs=(vmem,) * 3,
        scratch_shapes=[
            pltpu.VMEM(lists, jnp.float32),
            sem((window,)), sem((window,)), sem((2, max(3, cols))), sem((2, cols)),
            sem((4, depths)), sem((4, depths)), sem((4, depths)), sem((4, depths)),
            pltpu.VMEM((2, depths, max(1, (capacity - short) // 2), size, size), jnp.float32),
            sem((4, depths)), sem((4, depths)), sem((2,)),
        ],
        compiler_params=pltpu.CompilerParams(
            collective_id=ident, has_side_effects=True, vmem_limit_bytes=VMEM_LIMIT
        ),
    )(pack, codes, blocks)


def halves(value):
    high = value.astype(jnp.bfloat16)
    return high, (value - high.astype(jnp.float32)).astype(jnp.bfloat16)


def product(left, right):
    left_high, left_low = halves(left)
    right_high, right_low = halves(right)
    dot = functools.partial(jnp.dot, preferred_element_type=jnp.float32)
    return dot(left_high, right_high) + (dot(left_high, right_low) + dot(left_low, right_high))


def multiply_into(acc_ref, lefts_ref, got_ref, blocks_ref, codes_ref, held, sems, sizes, short):
    rows, cols, depths = sizes
    window = rows * depths
    capacity = got_ref.shape[1]
    panels, slots = blocks_ref.shape[1:3]
    out_slots = panels * slots
    r, c, d = position()
    me_q = r * depths + d
    own = codes_ref[me_q, 0, 0]

    def fetch(n):
        at = codes_ref[me_q, 0, SOURCE + n]
        row = at // out_slots
        block = blocks_ref.at[row, (at // slots) % panels, at % slots]
        return pltpu.make_async_copy(block, held.at[n], sems.at[n])

    @pl.loop(0, own)
    def _(n):
        fetch(n).start()

    acc_ref[...] = jnp.zeros_like(acc_ref)

    def add(q, n, right):
        code = codes_ref[q, 0, HEAD + n]
        depth = q % depths
        left = lefts_ref[depth // panels, depth % panels, code // out_slots]
        s = code % out_slots
        acc_ref[s // slots, s % slots] += product(left, right)

    @pl.loop(0, window)
    def _(q):
        depth = q % depths
        on_chip = depth == d
        room = jnp.where(on_chip | (depth // panels == c), capacity, short)
        from_back = (q // depths == 1) & jnp.logical_not(on_chip)
        count = jnp.where(q == me_q, 0, jnp.minimum(codes_ref[q, 0, 0], room))

        @pl.loop(0, count)
        def _(n):
            add(q, n, got_ref[depth, jnp.where(from_back, room - 1 - n, n)])

    @pl.loop(0, own)
    def _(n):
        fetch(n).wait()
        add(me_q, n, held[n])


def square_kernel(
    sizes, short, codes_ref, got_ref, blocks_ref, lefts_ref, out_ref, flag_ref, held, sems
):
    flag = lax.fori_loop(0, codes_ref.shape[0], lambda q, f: f | codes_ref[q, 0, 1], jnp.int32(0))
    flag_ref[...] = jnp.full(flag_ref.shape, flag, jnp.int32)
    multiply_into(out_ref, lefts_ref, got_ref, blocks_ref, codes_ref, held, sems, sizes, short)


def cube_kernel(
    sizes, short, codes_ref, got_ref, blocks_ref, lefts_ref, square_ref, out_ref, held, sems
):
    multiply_into(out_ref, lefts_ref, got_ref, blocks_ref, codes_ref, held, sems, sizes, short)
    out_ref[...] = 3.0 * square_ref[...] - 2.0 * out_ref[...]


def local_product(kernel, codes, got, blocks, lefts, extra, out_shape, out_specs):
    vmem = pl.BlockSpec(memory_space=pltpu.VMEM)
    _, panels, slots, size, _ = blocks.shape
    most = slots * slots * panels
    return pl.pallas_call(
        kernel,
        out_shape=out_shape,
        in_specs=[
            pl.BlockSpec(memory_space=pltpu.SMEM),
            vmem,
            pl.BlockSpec(memory_space=pltpu.HBM),
            vmem,
        ] + [vmem] * len(extra),
        out_specs=out_specs,
        scratch_shapes=[
            pltpu.VMEM((most, size, size), jnp.float32),
            pltpu.SemaphoreType.DMA((most,)),
        ],
        compiler_params=pltpu.CompilerParams(vmem_limit_bytes=VMEM_LIMIT),
    )(codes, got, blocks, lefts, *extra)


def gather_kernel(
    cols, square_ref, flag_ref, squares_ref, any_ref, flags_ref,
    send_sem, recv_sem, flag_send, flag_recv, own_sem,
):
    r, c, d = position()
    barrier = pltpu.get_barrier_semaphore()

    @pl.loop(1, cols)
    def _(off):
        pl.semaphore_signal(barrier, inc=1, device_id=(r, (c + off) % cols, d), device_id_type=MESH)

    own = [
        pltpu.make_async_copy(square_ref, squares_ref.at[c], own_sem.at[0]),
        pltpu.make_async_copy(flag_ref, flags_ref.at[c], own_sem.at[1]),
    ]
    for copy in own:
        copy.start()
    begin, pass_on, end = spread(
        cols, square_ref.shape[1], square_ref, squares_ref, send_sem, recv_sem
    )
    pl.semaphore_wait(barrier, cols - 1)

    def flag_copy(slot, other):
        return pltpu.make_async_remote_copy(
            src_ref=flag_ref,
            dst_ref=flags_ref.at[slot],
            send_sem=flag_send.at[other],
            recv_sem=flag_recv.at[slot],
            device_id=(r, other, d),
            device_id_type=MESH,
        )

    begin()

    @pl.loop(1, cols)
    def _(off):
        flag_copy(c, (c + off) % cols).start()

    pass_on()
    for copy in own:
        copy.wait()

    @pl.loop(1, cols)
    def _(off):
        other = (c + off) % cols
        flag_copy(other, other).wait_recv()
        flag_copy(c, other).wait_send()

    end()
    any_ref[...] = jnp.max(flags_ref[...], axis=0)


def gather_square(square, flag, cols, ident):
    vmem = pl.BlockSpec(memory_space=pltpu.VMEM)
    return pl.pallas_call(
        functools.partial(gather_kernel, cols),
        out_shape=(
            jax.ShapeDtypeStruct((cols,) + square.shape, jnp.float32),
            jax.ShapeDtypeStruct(flag.shape, jnp.int32),
        ),
        in_specs=[vmem] * 2,
        out_specs=(vmem,) * 2,
        scratch_shapes=[
            pltpu.VMEM((cols,) + flag.shape, jnp.int32),
            pltpu.SemaphoreType.DMA((2, max(3, cols))),
            pltpu.SemaphoreType.DMA((2, cols)),
            pltpu.SemaphoreType.DMA((cols,)),
            pltpu.SemaphoreType.DMA((cols,)),
            pltpu.SemaphoreType.DMA((2,)),
        ],
        compiler_params=pltpu.CompilerParams(collective_id=ident, has_side_effects=True),
    )(square, flag)


def body(sizes, blocks, columns, counts):
    rows, cols, depths = sizes
    local_rows, panels, slots, size, _ = blocks.shape
    most = slots * slots * panels
    local = jnp.concatenate([columns.reshape(local_rows, panels * slots).T, counts.T], 0)
    entries = local.shape[0]
    local = jnp.pad(local, ((0, -entries % 8), (0, -local_rows % LANES)))
    win, sibling = gather_meta(local, sizes, panels, entries)
    block_shape = jax.ShapeDtypeStruct(blocks.shape[1:], jnp.float32)
    vmem = pl.BlockSpec(memory_space=pltpu.VMEM)

    def square_step(short, capacity, ident):
        pack, codes = pack_lists(win, local, sibling, blocks, sizes, short, capacity)
        got, got_codes, lefts = exchange(pack, codes, blocks, sizes, short, ident)
        square, flag = local_product(
            functools.partial(square_kernel, sizes, short),
            got_codes, got, blocks, lefts, (),
            (block_shape, jax.ShapeDtypeStruct((1, LANES), jnp.int32)),
            (vmem, vmem),
        )
        squares, too_long = gather_square(square, flag, cols, ident + 1)
        return got, got_codes, square, squares, too_long

    def cube_step(short, got, got_codes, square, squares):
        return local_product(
            functools.partial(cube_kernel, sizes, short),
            got_codes, got, blocks, squares, (square,), block_shape, vmem,
        )

    sizes_tried = []
    for short, capacity in TIERS:
        tier = (min(short, most), min(capacity, most))
        if tier not in sizes_tried:
            sizes_tried.append(tier)
    sizes_tried.append((most, most))

    def attempt(tier):
        short, capacity = sizes_tried[tier]
        *lists, too_long = square_step(short, capacity, 1 + 2 * tier)
        if (short, capacity) == (most, most):
            return cube_step(short, *lists)
        return lax.cond(
            too_long[0, 0] != 0, lambda: attempt(tier + 1), lambda: cube_step(short, *lists)
        )

    out = attempt(0)
    return out[None]


def solution(mesh):
    placed = (
        P(("row", "depth"), "col", None, None, None),
        P(("row", "depth"), "col", None),
        P(("row", "depth"), "col"),
    )
    sizes = (mesh.shape["row"], mesh.shape["col"], mesh.shape["depth"])
    return jax.shard_map(
        functools.partial(body, sizes),
        mesh=mesh,
        in_specs=placed,
        out_specs=P(("row", "depth"), "col", None, None, None),
        check_vma=False,
    )
```

```python
import functools

import jax
import jax.numpy as jnp
from jax import lax
from jax.experimental import pallas as pl
from jax.experimental.pallas import tpu as pltpu
from jax.sharding import PartitionSpec as P

MESH = pl.DeviceIdType.MESH
LANES = 128
VMEM_LIMIT = 48 << 20
TIERS = ((2, 6), (4, 8))
HEAD = 2
SOURCE = LANES // 2


def position():
    return lax.axis_index("row"), lax.axis_index("col"), lax.axis_index("depth")


def spread(cols, slots, src_ref, dst_ref, send, recv):
    r, c, d = position()

    def remote(src, dst, send, recv, column):
        return pltpu.make_async_remote_copy(
            src_ref=src, dst_ref=dst, send_sem=send, recv_sem=recv,
            device_id=(r, column, d), device_id_type=MESH,
        )

    if cols != 4 or slots % 2:
        def copy(slot, other):
            return remote(src_ref, dst_ref.at[slot], send.at[0, other], recv.at[0, slot], other)

        def begin():
            @pl.loop(1, cols)
            def _(off):
                copy(c, (c + off) % cols).start()

        def end():
            @pl.loop(1, cols)
            def _(off):
                other = (c + off) % cols
                copy(other, other).wait_recv()
                copy(c, other).wait_send()

        return begin, lambda: None, end

    def half(ref, h):
        return ref.at[:, pl.ds(h * (slots // 2), slots // 2)]

    def direct(h, way):
        return remote(
            half(src_ref, h), half(dst_ref.at[c], h), send.at[h, way - 1], recv.at[h, c], c ^ way
        )

    def arrival(h, way):
        there = half(dst_ref.at[c ^ way], h)
        return remote(half(src_ref, h), there, send.at[h, 0], recv.at[h, c ^ way], c ^ 1)

    def onward(h):
        origin = c ^ (1 + h)
        there = half(dst_ref.at[origin], h)
        return remote(there, there, send.at[h, 2], recv.at[h, origin], c ^ (2 - h))

    sent = [(0, 1), (1, 2), (1, 1), (0, 2)]

    def begin():
        for h, way in sent:
            direct(h, way).start()

    def pass_on():
        for h in (0, 1):
            arrival(h, 1 + h).wait_recv()
            onward(h).start()

    def end():
        for h, way in ((1, 1), (0, 2), (0, 3), (1, 3)):
            arrival(h, way).wait_recv()
        for h, way in sent:
            direct(h, way).wait_send()
        for h in (0, 1):
            onward(h).wait_send()

    return begin, pass_on, end


def meta_kernel(
    sizes, panels, entries, local_ref, all_ref, sibling_ref, meta_ref,
    send_sem, recv_sem, own_sem, swap_sems,
):
    rows, cols, depths = sizes
    window = rows * depths
    r, c, d = position()
    me_q = r * depths + d
    owner = d // panels
    lanes = lax.broadcasted_iota(jnp.int32, meta_ref.shape, 1)
    meta = jnp.zeros(meta_ref.shape, jnp.int32)
    for j in range(entries):
        value = jnp.broadcast_to(local_ref[j : j + 1, 0:1], meta_ref.shape)
        meta = jnp.where(lanes == j, value, meta)
    meta_ref[...] = meta

    def column_mate(off):
        q = (me_q + off) % window
        return q, c

    def inner_mate(i):
        col = (c + 1 + i // (rows * panels)) % cols
        row = (i // panels) % rows
        return row * depths + c * panels + i % panels, col

    def left_source(i):
        return i, owner

    mates = window - 1
    inner = rows * panels * (cols - 1)
    sources = jnp.where(owner == c, 0, window)

    def device(q, col):
        return (q // depths, col, q % depths)

    barrier = pltpu.get_barrier_semaphore()

    def greet(q, col):
        pl.semaphore_signal(barrier, inc=1, device_id=device(q, col), device_id_type=MESH)

    @pl.loop(1, window)
    def _(off):
        greet(*column_mate(off))

    @pl.loop(0, sources)
    def _(i):
        greet(*left_source(i))

    own = pltpu.make_async_copy(meta_ref, all_ref.at[me_q * cols + c], own_sem)
    own.start()
    pl.semaphore_wait(barrier, mates + inner)

    def copy(slot, q, col):
        return pltpu.make_async_remote_copy(
            src_ref=meta_ref,
            dst_ref=all_ref.at[slot],
            send_sem=send_sem.at[q * cols + col],
            recv_sem=recv_sem.at[slot],
            device_id=device(q, col),
            device_id_type=MESH,
        )

    me = me_q * cols + c
    swap = pltpu.make_async_remote_copy(
        src_ref=local_ref,
        dst_ref=sibling_ref,
        send_sem=swap_sems.at[0],
        recv_sem=swap_sems.at[1],
        device_id=(1 - r, c, d),
        device_id_type=MESH,
    )

    @pl.loop(0, inner)
    def _(i):
        copy(me, *inner_mate(i)).start()

    @pl.loop(1, window)
    def _(off):
        copy(me, *column_mate(off)).start()

    swap.start()
    own.wait()

    @pl.loop(1, window)
    def _(off):
        q, col = column_mate(off)
        copy(q * cols + col, q, col).wait_recv()
        copy(me, q, col).wait_send()

    @pl.loop(0, sources)
    def _(i):
        q, col = left_source(i)
        copy(q * cols + col, q, col).wait_recv()

    @pl.loop(0, inner)
    def _(i):
        copy(me, *inner_mate(i)).wait_send()

    swap.wait()


def gather_meta(local, sizes, panels, entries):
    devices = sizes[0] * sizes[1] * sizes[2]
    return pl.pallas_call(
        functools.partial(meta_kernel, sizes, panels, entries),
        out_shape=(
            jax.ShapeDtypeStruct((devices, 1, LANES), jnp.int32),
            jax.ShapeDtypeStruct(local.shape, jnp.int32),
        ),
        in_specs=[pl.BlockSpec(memory_space=pltpu.VMEM)],
        out_specs=(pl.BlockSpec(memory_space=pltpu.VMEM),) * 2,
        scratch_shapes=[
            pltpu.VMEM((1, LANES), jnp.int32),
            pltpu.SemaphoreType.DMA((devices,)),
            pltpu.SemaphoreType.DMA((devices,)),
            pltpu.SemaphoreType.DMA,
            pltpu.SemaphoreType.DMA((2,)),
        ],
        compiler_params=pltpu.CompilerParams(collective_id=0, has_side_effects=True),
    )(local)


def pack_kernel(
    sizes, dims, short, win_ref, local_ref, sibling_ref, blocks_ref, pack_ref, codes_ref, sem
):
    rows, cols, depths = sizes
    local_rows, panels, slots = dims
    window = rows * depths
    capacity = pack_ref.shape[1]
    r, c, d = position()
    me_q = r * depths + d
    owner = d // panels
    left_panel = d % panels
    counts_at = panels * slots
    limit = jnp.where(owner == c, capacity, short)

    def entry(q, n, row, panel, slot):
        return pltpu.make_async_copy(blocks_ref.at[row, panel, slot], pack_ref.at[q, n], sem)

    def pack_row(q, carry):
        too_long, copies = carry
        left_at = q * cols + owner
        out_at = q * cols + c
        left_count = win_ref[left_at, 0, counts_at + left_panel]
        on_chip = q % depths == d
        limit_q = jnp.where(on_chip, capacity, limit)
        room = jnp.where(q == me_q, 0, limit_q)
        from_back = (r == 1) & jnp.logical_not(on_chip)

        def left_step(a, counts):
            place = win_ref[left_at, 0, left_panel * slots + a]
            row = place % local_rows
            mine = place // local_rows == r

            def matches(inner_ref, found, n):
                def panel_step(panel, n):
                    out_count = win_ref[out_at, 0, counts_at + panel]
                    inner_count = inner_ref[counts_at + panel, row]

                    def inner_step(t, n):
                        column = inner_ref[panel * slots + t, row]

                        def out_step(s, n):
                            hit = win_ref[out_at, 0, panel * slots + s] == column
                            found(hit, n, panel, t, s)
                            return n + hit.astype(jnp.int32)

                        return lax.fori_loop(0, out_count, out_step, n)

                    return lax.fori_loop(0, inner_count, inner_step, n)

                return lax.fori_loop(0, panels, panel_step, n)

            def keep(hit, n, panel, t, s):
                @pl.when(hit)
                def _():
                    codes_ref[q, 0, HEAD + n] = a * counts_at + panel * slots + s
                    codes_ref[q, 0, SOURCE + n] = (row * panels + panel) * slots + t

                @pl.when(hit & (n < room))
                def _():
                    entry(q, jnp.where(from_back, limit - 1 - n, n), row, panel, t).start()

            def skip(hit, n, panel, t, s):
                pass

            n, other = counts
            return lax.cond(
                mine,
                lambda: (matches(local_ref, keep, n), other),
                lambda: (n, matches(sibling_ref, skip, other)),
            )

        zero = jnp.int32(0)
        n, other = lax.fori_loop(0, left_count, left_step, (zero, zero))
        codes_ref[q, 0, 0] = n
        total = jnp.where(on_chip, n, n + other)
        over = ((total > limit_q) & (q != me_q)).astype(jnp.int32)
        return too_long | over, copies + jnp.minimum(n, room)

    zero = jnp.int32(0)
    too_long, copies = lax.fori_loop(0, window, pack_row, (zero, zero))

    @pl.loop(0, window)
    def _(q):
        codes_ref[q, 0, 1] = too_long

    @pl.loop(0, copies)
    def _(n):
        entry(0, 0, 0, 0, 0).wait()


def pack_lists(win, local, sibling, blocks, sizes, short, capacity):
    local_rows, panels, slots, size, _ = blocks.shape
    window = sizes[0] * sizes[2]
    smem = pl.BlockSpec(memory_space=pltpu.SMEM)
    return pl.pallas_call(
        functools.partial(pack_kernel, sizes, (local_rows, panels, slots), short),
        out_shape=(
            jax.ShapeDtypeStruct((window, capacity, size, size), jnp.float32),
            jax.ShapeDtypeStruct((window, 1, LANES), jnp.int32),
        ),
        in_specs=[smem, smem, smem, pl.BlockSpec(memory_space=pltpu.HBM)],
        out_specs=(pl.BlockSpec(memory_space=pltpu.VMEM), smem),
        scratch_shapes=[pltpu.SemaphoreType.DMA],
        compiler_params=pltpu.CompilerParams(vmem_limit_bytes=VMEM_LIMIT),
    )(win, local, sibling, blocks)


def exchange_kernel(
    sizes, panels, short, pack_ref, codes_ref, blocks_ref,
    got_ref, got_codes_ref, lefts_ref,
    merged_ref, code_send, code_recv, left_send, left_recv,
    swap_send, swap_recv, list_send, list_recv, relay_ref, relay_send, relay_recv, own_sem,
):
    rows, cols, depths = sizes
    window = rows * depths
    capacity = pack_ref.shape[1]
    left_ref = blocks_ref.at[0]
    r, c, d = position()
    me = r * depths + d
    diag = d // panels == c
    parts = [(0, short, 0)]
    extra = capacity - short
    ways = [1, 2] if cols == 4 and extra >= 4 else []
    straight = extra // 4 if ways else extra
    if extra:
        parts.append((short, straight, 0))
    if ways:
        parts.append((short + straight, straight, 1))
        parts.append((short + 2 * straight, extra - 2 * straight, 2))

    barrier = pltpu.get_barrier_semaphore()

    @pl.loop(1, window)
    def _(off):
        q = (me + off) % window
        pl.semaphore_signal(barrier, inc=1, device_id=(q // depths, c, q % depths), device_id_type=MESH)

    @pl.loop(1, cols)
    def _(off):
        pl.semaphore_signal(barrier, inc=1, device_id=(r, (c + off) % cols, d), device_id_type=MESH)

    for way in ways:
        @pl.loop(1, depths)
        def _(off):
            device = (r, c ^ way, (d + off) % depths)
            pl.semaphore_signal(barrier, inc=1, device_id=device, device_id_type=MESH)

    own = [
        pltpu.make_async_copy(codes_ref.at[me], got_codes_ref.at[me], own_sem.at[0]),
        pltpu.make_async_copy(left_ref, lefts_ref.at[c], own_sem.at[1]),
    ]
    for copy in own:
        copy.start()
    pl.semaphore_wait(barrier, window - 1 + cols - 1 + len(ways) * (depths - 1))

    def remote(src, dst, send, recv, device):
        return pltpu.make_async_remote_copy(
            src_ref=src, dst_ref=dst, send_sem=send, recv_sem=recv,
            device_id=device, device_id_type=MESH,
        )

    begin, pass_on, end = spread(
        cols, blocks_ref.shape[2], left_ref, lefts_ref, left_send, left_recv
    )

    def code_copy(slot, other):
        return remote(
            codes_ref.at[other], got_codes_ref.at[slot], code_send.at[other], code_recv.at[slot],
            (other // depths, c, other % depths),
        )

    def swap_copy(part, depth):
        first, length, way = parts[part]
        there = pl.ds(first, length)
        return remote(
            pack_ref.at[(1 - r) * depths + depth, there], merged_ref.at[depth, there],
            swap_send.at[part, depth], swap_recv.at[part, depth], (1 - r, c, d),
        )

    def chip_copy():
        return remote(
            pack_ref.at[(1 - r) * depths + d], got_ref.at[d],
            swap_send.at[0, d], swap_recv.at[0, d], (1 - r, c, d),
        )

    def list_copy(part, slot, depth):
        first, length, way = parts[part]
        there = pl.ds(first, length)
        if way:
            target, device = relay_ref.at[way - 1, depth, pl.ds(0, length)], (r, c ^ way, d)
        else:
            target, device = got_ref.at[slot, there], (r, c, depth)
        return remote(
            merged_ref.at[depth, there], target,
            list_send.at[part, depth], list_recv.at[part, depth if way else slot], device,
        )

    def relay_copy(part, slot, depth):
        first, length, way = parts[part]
        return remote(
            relay_ref.at[way - 1, depth, pl.ds(0, length)],
            got_ref.at[slot, pl.ds(first, length)],
            relay_send.at[part, depth], relay_recv.at[part, slot], (r, c ^ way, depth),
        )

    def arrival(part, depth):
        copy = relay_copy if parts[part][2] else list_copy
        return copy(part, depth, depth)

    def each_part(wide, action):
        if len(parts) > 1:
            @pl.when(wide)
            def _():
                for part in reversed(range(1, len(parts))):
                    action(part)
        action(0)

    def each_relay(action):
        for part, (first, length, way) in enumerate(parts):
            if way:
                @pl.when(d // panels == c ^ way)
                def _():
                    @pl.loop(1, depths)
                    def _(off):
                        action(part, (d + off) % depths)

    @pl.loop(1, depths)
    def _(off):
        depth = (d + off) % depths
        each_part(diag, lambda part: swap_copy(part, depth).start())

    @pl.loop(1, depths)
    def _(off):
        depth = (d + off) % depths

        def forward(part):
            swap_copy(part, depth).wait_recv()
            first, length, way = parts[part]
            q = r * depths + depth
            count = jnp.broadcast_to(codes_ref[q, 0:1, 0:1], pack_ref.shape[2:])
            for place in range(first, first + length):
                rank = jnp.where(r == 1, jnp.where(diag, capacity, short) - 1 - place, place)
                merged_ref[depth, place] = jnp.where(
                    rank < count, pack_ref[q, place], merged_ref[depth, place]
                )
            list_copy(part, d, depth).start()

        each_part(diag, forward)

    begin()
    chip_copy().start()

    @pl.loop(1, window)
    def _(off):
        code_copy(me, (me + off) % window).start()

    def relay(part, depth):
        list_copy(part, d, depth).wait_recv()
        relay_copy(part, d, depth).start()

    each_relay(relay)

    for copy in own:
        copy.wait()

    pass_on()
    end()

    @pl.loop(1, window)
    def _(off):
        other = (me + off) % window
        code_copy(other, other).wait_recv()
        code_copy(me, other).wait_send()

    chip_copy().wait()

    @pl.loop(1, depths)
    def _(off):
        depth = (d + off) % depths
        each_part(diag, lambda part: swap_copy(part, depth).wait_send())
        each_part(depth // panels == c, lambda part: arrival(part, depth).wait_recv())
        each_part(diag, lambda part: list_copy(part, d, depth).wait_send())

    each_relay(lambda part, depth: relay_copy(part, d, depth).wait_send())


def exchange(pack, codes, blocks, sizes, short, ident):
    window, capacity, size, _ = pack.shape
    rows, cols, depths = sizes
    panels = blocks.shape[1]
    vmem = pl.BlockSpec(memory_space=pltpu.VMEM)
    lists = (depths, capacity, size, size)
    sem = pltpu.SemaphoreType.DMA
    return pl.pallas_call(
        functools.partial(exchange_kernel, sizes, panels, short),
        out_shape=(
            jax.ShapeDtypeStruct(lists, jnp.float32),
            jax.ShapeDtypeStruct(codes.shape, jnp.int32),
            jax.ShapeDtypeStruct((cols,) + blocks.shape[1:], jnp.float32),
        ),
        in_specs=[vmem, vmem, pl.BlockSpec(memory_space=pltpu.HBM)],
        out_specs=(vmem,) * 3,
        scratch_shapes=[
            pltpu.VMEM(lists, jnp.float32),
            sem((window,)), sem((window,)), sem((2, max(3, cols))), sem((2, cols)),
            sem((4, depths)), sem((4, depths)), sem((4, depths)), sem((4, depths)),
            pltpu.VMEM((2, depths, max(1, (capacity - short) // 2), size, size), jnp.float32),
            sem((4, depths)), sem((4, depths)), sem((2,)),
        ],
        compiler_params=pltpu.CompilerParams(
            collective_id=ident, has_side_effects=True, vmem_limit_bytes=VMEM_LIMIT
        ),
    )(pack, codes, blocks)


def halves(value):
    high = value.astype(jnp.bfloat16)
    return high, (value - high.astype(jnp.float32)).astype(jnp.bfloat16)


def product(left, right):
    left_high, left_low = halves(left)
    right_high, right_low = halves(right)
    dot = functools.partial(jnp.dot, preferred_element_type=jnp.float32)
    return dot(left_high, right_high) + (dot(left_high, right_low) + dot(left_low, right_high))


def multiply_into(acc_ref, lefts_ref, got_ref, blocks_ref, codes_ref, held, sems, sizes, short):
    rows, cols, depths = sizes
    window = rows * depths
    capacity = got_ref.shape[1]
    panels, slots = blocks_ref.shape[1:3]
    out_slots = panels * slots
    r, c, d = position()
    me_q = r * depths + d
    own = codes_ref[me_q, 0, 0]

    def fetch(n):
        at = codes_ref[me_q, 0, SOURCE + n]
        row = at // out_slots
        block = blocks_ref.at[row, (at // slots) % panels, at % slots]
        return pltpu.make_async_copy(block, held.at[n], sems.at[n])

    @pl.loop(0, own)
    def _(n):
        fetch(n).start()

    acc_ref[...] = jnp.zeros_like(acc_ref)

    def add(q, n, right):
        code = codes_ref[q, 0, HEAD + n]
        depth = q % depths
        left = lefts_ref[depth // panels, depth % panels, code // out_slots]
        s = code % out_slots
        acc_ref[s // slots, s % slots] += product(left, right)

    @pl.loop(0, window)
    def _(q):
        depth = q % depths
        on_chip = depth == d
        room = jnp.where(on_chip | (depth // panels == c), capacity, short)
        from_back = (q // depths == 1) & jnp.logical_not(on_chip)
        count = jnp.where(q == me_q, 0, jnp.minimum(codes_ref[q, 0, 0], room))

        @pl.loop(0, count)
        def _(n):
            add(q, n, got_ref[depth, jnp.where(from_back, room - 1 - n, n)])

    @pl.loop(0, own)
    def _(n):
        fetch(n).wait()
        add(me_q, n, held[n])


def square_kernel(
    sizes, short, codes_ref, got_ref, blocks_ref, lefts_ref, out_ref, held, sems
):
    multiply_into(out_ref, lefts_ref, got_ref, blocks_ref, codes_ref, held, sems, sizes, short)


def cube_kernel(
    sizes, short, codes_ref, got_ref, blocks_ref, lefts_ref, square_ref, out_ref, held, sems
):
    multiply_into(out_ref, lefts_ref, got_ref, blocks_ref, codes_ref, held, sems, sizes, short)
    out_ref[...] = 3.0 * square_ref[...] - 2.0 * out_ref[...]


def local_product(kernel, codes, got, blocks, lefts, extra, out_shape, out_specs):
    vmem = pl.BlockSpec(memory_space=pltpu.VMEM)
    _, panels, slots, size, _ = blocks.shape
    most = slots * slots * panels
    return pl.pallas_call(
        kernel,
        out_shape=out_shape,
        in_specs=[
            pl.BlockSpec(memory_space=pltpu.SMEM),
            vmem,
            pl.BlockSpec(memory_space=pltpu.HBM),
            vmem,
        ] + [vmem] * len(extra),
        out_specs=out_specs,
        scratch_shapes=[
            pltpu.VMEM((most, size, size), jnp.float32),
            pltpu.SemaphoreType.DMA((most,)),
        ],
        compiler_params=pltpu.CompilerParams(vmem_limit_bytes=VMEM_LIMIT),
    )(codes, got, blocks, lefts, *extra)


def gather_kernel(
    cols, square_ref, codes_ref, squares_ref, any_ref, flag_ref, flags_ref,
    send_sem, recv_sem, flag_send, flag_recv, own_sem,
):
    r, c, d = position()
    barrier = pltpu.get_barrier_semaphore()

    @pl.loop(1, cols)
    def _(off):
        pl.semaphore_signal(barrier, inc=1, device_id=(r, (c + off) % cols, d), device_id_type=MESH)

    flag_ref[...] = jnp.max(codes_ref[...], axis=0)
    own = [
        pltpu.make_async_copy(square_ref, squares_ref.at[c], own_sem.at[0]),
        pltpu.make_async_copy(flag_ref, flags_ref.at[c], own_sem.at[1]),
    ]
    for copy in own:
        copy.start()
    begin, pass_on, end = spread(
        cols, square_ref.shape[1], square_ref, squares_ref, send_sem, recv_sem
    )
    pl.semaphore_wait(barrier, cols - 1)

    def flag_copy(slot, other):
        return pltpu.make_async_remote_copy(
            src_ref=flag_ref,
            dst_ref=flags_ref.at[slot],
            send_sem=flag_send.at[other],
            recv_sem=flag_recv.at[slot],
            device_id=(r, other, d),
            device_id_type=MESH,
        )

    begin()

    @pl.loop(1, cols)
    def _(off):
        flag_copy(c, (c + off) % cols).start()

    pass_on()
    for copy in own:
        copy.wait()

    @pl.loop(1, cols)
    def _(off):
        other = (c + off) % cols
        flag_copy(other, other).wait_recv()
        flag_copy(c, other).wait_send()

    end()
    any_ref[...] = jnp.max(flags_ref[...], axis=0)


def gather_square(square, codes, cols, ident):
    vmem = pl.BlockSpec(memory_space=pltpu.VMEM)
    return pl.pallas_call(
        functools.partial(gather_kernel, cols),
        out_shape=(
            jax.ShapeDtypeStruct((cols,) + square.shape, jnp.float32),
            jax.ShapeDtypeStruct(codes.shape[1:], jnp.int32),
        ),
        in_specs=[vmem] * 2,
        out_specs=(vmem,) * 2,
        scratch_shapes=[
            pltpu.VMEM(codes.shape[1:], jnp.int32),
            pltpu.VMEM((cols,) + codes.shape[1:], jnp.int32),
            pltpu.SemaphoreType.DMA((2, max(3, cols))),
            pltpu.SemaphoreType.DMA((2, cols)),
            pltpu.SemaphoreType.DMA((cols,)),
            pltpu.SemaphoreType.DMA((cols,)),
            pltpu.SemaphoreType.DMA((2,)),
        ],
        compiler_params=pltpu.CompilerParams(collective_id=ident, has_side_effects=True),
    )(square, codes)


def body(sizes, blocks, columns, counts):
    rows, cols, depths = sizes
    local_rows, panels, slots, size, _ = blocks.shape
    most = slots * slots * panels
    local = jnp.concatenate([columns.reshape(local_rows, panels * slots).T, counts.T], 0)
    entries = local.shape[0]
    local = jnp.pad(local, ((0, -entries % 8), (0, -local_rows % LANES)))
    win, sibling = gather_meta(local, sizes, panels, entries)
    block_shape = jax.ShapeDtypeStruct(blocks.shape[1:], jnp.float32)
    vmem = pl.BlockSpec(memory_space=pltpu.VMEM)

    def square_step(short, capacity, ident):
        pack, codes = pack_lists(win, local, sibling, blocks, sizes, short, capacity)
        got, got_codes, lefts = exchange(pack, codes, blocks, sizes, short, ident)
        square = local_product(
            functools.partial(square_kernel, sizes, short),
            got_codes, got, blocks, lefts, (), block_shape, vmem,
        )
        squares, too_long = gather_square(square, got_codes, cols, ident + 1)
        return got, got_codes, square, squares, too_long

    def cube_step(short, got, got_codes, square, squares):
        return local_product(
            functools.partial(cube_kernel, sizes, short),
            got_codes, got, blocks, squares, (square,), block_shape, vmem,
        )

    sizes_tried = []
    for short, capacity in TIERS:
        tier = (min(short, most), min(capacity, most))
        if tier not in sizes_tried:
            sizes_tried.append(tier)
    sizes_tried.append((most, most))

    def attempt(tier):
        short, capacity = sizes_tried[tier]
        *lists, too_long = square_step(short, capacity, 1 + 2 * tier)
        if (short, capacity) == (most, most):
            return cube_step(short, *lists)
        return lax.cond(
            too_long[0, 1] != 0, lambda: attempt(tier + 1), lambda: cube_step(short, *lists)
        )

    out = attempt(0)
    return out[None]


def solution(mesh):
    placed = (
        P(("row", "depth"), "col", None, None, None),
        P(("row", "depth"), "col", None),
        P(("row", "depth"), "col"),
    )
    sizes = (mesh.shape["row"], mesh.shape["col"], mesh.shape["depth"])
    return jax.shard_map(
        functools.partial(body, sizes),
        mesh=mesh,
        in_specs=placed,
        out_specs=P(("row", "depth"), "col", None, None, None),
        check_vma=False,
    )
```

```python
import functools

import jax
import jax.numpy as jnp
from jax import lax
from jax.experimental import pallas as pl
from jax.experimental.pallas import tpu as pltpu
from jax.sharding import PartitionSpec as P

MESH = pl.DeviceIdType.MESH
LANES = 128
VMEM_LIMIT = 48 << 20
TIERS = ((2, 6), (4, 8))
HEAD = 2
SOURCE = LANES // 2


def position():
    return lax.axis_index("row"), lax.axis_index("col"), lax.axis_index("depth")


def spread(cols, slots, src_ref, dst_ref, send, recv):
    r, c, d = position()

    def remote(src, dst, send, recv, column):
        return pltpu.make_async_remote_copy(
            src_ref=src, dst_ref=dst, send_sem=send, recv_sem=recv,
            device_id=(r, column, d), device_id_type=MESH,
        )

    if cols != 4 or slots % 2:
        def copy(slot, other):
            return remote(src_ref, dst_ref.at[slot], send.at[0, other], recv.at[0, slot], other)

        def begin():
            @pl.loop(1, cols)
            def _(off):
                copy(c, (c + off) % cols).start()

        def end():
            @pl.loop(1, cols)
            def _(off):
                other = (c + off) % cols
                copy(other, other).wait_recv()
                copy(c, other).wait_send()

        return begin, lambda: None, end

    def half(ref, h):
        return ref.at[:, pl.ds(h * (slots // 2), slots // 2)]

    def direct(h, way):
        return remote(
            half(src_ref, h), half(dst_ref.at[c], h), send.at[h, way - 1], recv.at[h, c], c ^ way
        )

    def arrival(h, way):
        there = half(dst_ref.at[c ^ way], h)
        return remote(half(src_ref, h), there, send.at[h, 0], recv.at[h, c ^ way], c ^ 1)

    def onward(h):
        origin = c ^ (1 + h)
        there = half(dst_ref.at[origin], h)
        return remote(there, there, send.at[h, 2], recv.at[h, origin], c ^ (2 - h))

    sent = [(0, 1), (1, 2), (1, 1), (0, 2)]

    def begin():
        for h, way in sent:
            direct(h, way).start()

    def pass_on():
        for h in (0, 1):
            arrival(h, 1 + h).wait_recv()
            onward(h).start()

    def end():
        for h, way in ((1, 1), (0, 2), (0, 3), (1, 3)):
            arrival(h, way).wait_recv()
        for h, way in sent:
            direct(h, way).wait_send()
        for h in (0, 1):
            onward(h).wait_send()

    return begin, pass_on, end


def meta_kernel(
    sizes, panels, entries, local_ref, all_ref, sibling_ref, meta_ref,
    send_sem, recv_sem, own_sem, swap_sems,
):
    rows, cols, depths = sizes
    window = rows * depths
    r, c, d = position()
    me_q = r * depths + d
    owner = d // panels
    lanes = lax.broadcasted_iota(jnp.int32, meta_ref.shape, 1)
    meta = jnp.zeros(meta_ref.shape, jnp.int32)
    for j in range(entries):
        value = jnp.broadcast_to(local_ref[j : j + 1, 0:1], meta_ref.shape)
        meta = jnp.where(lanes == j, value, meta)
    meta_ref[...] = meta

    def column_mate(off):
        q = (me_q + off) % window
        return q, c

    def inner_mate(i):
        col = (c + 1 + i // (rows * panels)) % cols
        row = (i // panels) % rows
        return row * depths + c * panels + i % panels, col

    def left_source(i):
        return i, owner

    mates = window - 1
    inner = rows * panels * (cols - 1)
    sources = jnp.where(owner == c, 0, window)

    def device(q, col):
        return (q // depths, col, q % depths)

    barrier = pltpu.get_barrier_semaphore()

    def greet(q, col):
        pl.semaphore_signal(barrier, inc=1, device_id=device(q, col), device_id_type=MESH)

    @pl.loop(1, window)
    def _(off):
        greet(*column_mate(off))

    @pl.loop(0, sources)
    def _(i):
        greet(*left_source(i))

    own = pltpu.make_async_copy(meta_ref, all_ref.at[me_q * cols + c], own_sem)
    own.start()
    pl.semaphore_wait(barrier, mates + inner)

    def copy(slot, q, col):
        return pltpu.make_async_remote_copy(
            src_ref=meta_ref,
            dst_ref=all_ref.at[slot],
            send_sem=send_sem.at[q * cols + col],
            recv_sem=recv_sem.at[slot],
            device_id=device(q, col),
            device_id_type=MESH,
        )

    me = me_q * cols + c
    swap = pltpu.make_async_remote_copy(
        src_ref=local_ref,
        dst_ref=sibling_ref,
        send_sem=swap_sems.at[0],
        recv_sem=swap_sems.at[1],
        device_id=(1 - r, c, d),
        device_id_type=MESH,
    )

    @pl.loop(0, inner)
    def _(i):
        copy(me, *inner_mate(i)).start()

    @pl.loop(1, window)
    def _(off):
        copy(me, *column_mate(off)).start()

    swap.start()
    own.wait()

    @pl.loop(1, window)
    def _(off):
        q, col = column_mate(off)
        copy(q * cols + col, q, col).wait_recv()
        copy(me, q, col).wait_send()

    @pl.loop(0, sources)
    def _(i):
        q, col = left_source(i)
        copy(q * cols + col, q, col).wait_recv()

    @pl.loop(0, inner)
    def _(i):
        copy(me, *inner_mate(i)).wait_send()

    swap.wait()


def gather_meta(local, sizes, panels, entries):
    devices = sizes[0] * sizes[1] * sizes[2]
    return pl.pallas_call(
        functools.partial(meta_kernel, sizes, panels, entries),
        out_shape=(
            jax.ShapeDtypeStruct((devices, 1, LANES), jnp.int32),
            jax.ShapeDtypeStruct(local.shape, jnp.int32),
        ),
        in_specs=[pl.BlockSpec(memory_space=pltpu.VMEM)],
        out_specs=(pl.BlockSpec(memory_space=pltpu.VMEM),) * 2,
        scratch_shapes=[
            pltpu.VMEM((1, LANES), jnp.int32),
            pltpu.SemaphoreType.DMA((devices,)),
            pltpu.SemaphoreType.DMA((devices,)),
            pltpu.SemaphoreType.DMA,
            pltpu.SemaphoreType.DMA((2,)),
        ],
        compiler_params=pltpu.CompilerParams(collective_id=0, has_side_effects=True),
    )(local)


def pack_kernel(
    sizes, dims, short, win_ref, local_ref, sibling_ref, blocks_ref, pack_ref, codes_ref, sem
):
    rows, cols, depths = sizes
    local_rows, panels, slots = dims
    window = rows * depths
    capacity = pack_ref.shape[1]
    r, c, d = position()
    me_q = r * depths + d
    owner = d // panels
    left_panel = d % panels
    counts_at = panels * slots
    limit = jnp.where(owner == c, capacity, short)

    def entry(q, n, row, panel, slot):
        return pltpu.make_async_copy(blocks_ref.at[row, panel, slot], pack_ref.at[q, n], sem)

    def pack_row(q, carry):
        too_long, copies = carry
        left_at = q * cols + owner
        out_at = q * cols + c
        left_count = win_ref[left_at, 0, counts_at + left_panel]
        on_chip = q % depths == d
        limit_q = jnp.where(on_chip, capacity, limit)
        room = jnp.where(q == me_q, 0, limit_q)
        from_back = (r == 1) & jnp.logical_not(on_chip)

        def left_step(a, counts):
            place = win_ref[left_at, 0, left_panel * slots + a]
            row = place % local_rows
            mine = place // local_rows == r

            def matches(inner_ref, found, n):
                def panel_step(panel, n):
                    out_count = win_ref[out_at, 0, counts_at + panel]
                    inner_count = inner_ref[counts_at + panel, row]

                    def inner_step(t, n):
                        column = inner_ref[panel * slots + t, row]

                        def out_step(s, n):
                            hit = win_ref[out_at, 0, panel * slots + s] == column
                            found(hit, n, panel, t, s)
                            return n + hit.astype(jnp.int32)

                        return lax.fori_loop(0, out_count, out_step, n)

                    return lax.fori_loop(0, inner_count, inner_step, n)

                return lax.fori_loop(0, panels, panel_step, n)

            def keep(hit, n, panel, t, s):
                @pl.when(hit)
                def _():
                    codes_ref[q, 0, HEAD + n] = a * counts_at + panel * slots + s
                    codes_ref[q, 0, SOURCE + n] = (row * panels + panel) * slots + t

                @pl.when(hit & (n < room))
                def _():
                    entry(q, jnp.where(from_back, limit - 1 - n, n), row, panel, t).start()

            def skip(hit, n, panel, t, s):
                pass

            n, other = counts
            return lax.cond(
                mine,
                lambda: (matches(local_ref, keep, n), other),
                lambda: (n, matches(sibling_ref, skip, other)),
            )

        zero = jnp.int32(0)
        n, other = lax.fori_loop(0, left_count, left_step, (zero, zero))
        codes_ref[q, 0, 0] = n
        total = jnp.where(on_chip, n, n + other)
        over = ((total > limit_q) & (q != me_q)).astype(jnp.int32)
        return too_long | over, copies + jnp.minimum(n, room)

    zero = jnp.int32(0)
    too_long, copies = lax.fori_loop(0, window, pack_row, (zero, zero))

    @pl.loop(0, window)
    def _(q):
        codes_ref[q, 0, 1] = too_long

    @pl.loop(0, copies)
    def _(n):
        entry(0, 0, 0, 0, 0).wait()


def pack_lists(win, local, sibling, blocks, sizes, short, capacity):
    local_rows, panels, slots, size, _ = blocks.shape
    window = sizes[0] * sizes[2]
    smem = pl.BlockSpec(memory_space=pltpu.SMEM)
    return pl.pallas_call(
        functools.partial(pack_kernel, sizes, (local_rows, panels, slots), short),
        out_shape=(
            jax.ShapeDtypeStruct((window, capacity, size, size), jnp.float32),
            jax.ShapeDtypeStruct((window, 1, LANES), jnp.int32),
        ),
        in_specs=[smem, smem, smem, pl.BlockSpec(memory_space=pltpu.HBM)],
        out_specs=(pl.BlockSpec(memory_space=pltpu.VMEM), smem),
        scratch_shapes=[pltpu.SemaphoreType.DMA],
        compiler_params=pltpu.CompilerParams(vmem_limit_bytes=VMEM_LIMIT),
    )(win, local, sibling, blocks)


def exchange_kernel(
    sizes, panels, short, pack_ref, codes_ref, blocks_ref,
    got_ref, got_codes_ref, lefts_ref,
    merged_ref, code_send, code_recv, left_send, left_recv,
    swap_send, swap_recv, list_send, list_recv, relay_ref, relay_send, relay_recv, own_sem,
):
    rows, cols, depths = sizes
    window = rows * depths
    capacity = pack_ref.shape[1]
    left_ref = blocks_ref.at[0]
    r, c, d = position()
    me = r * depths + d
    diag = d // panels == c
    parts = [(0, short, 0)]
    extra = capacity - short
    ways = [1, 2] if cols == 4 and extra >= 4 else []
    straight = extra // 4 if ways else extra
    if extra:
        parts.append((short, straight, 0))
    if ways:
        parts.append((short + straight, straight, 1))
        parts.append((short + 2 * straight, extra - 2 * straight, 2))

    barrier = pltpu.get_barrier_semaphore()

    @pl.loop(1, window)
    def _(off):
        q = (me + off) % window
        pl.semaphore_signal(barrier, inc=1, device_id=(q // depths, c, q % depths), device_id_type=MESH)

    @pl.loop(1, cols)
    def _(off):
        pl.semaphore_signal(barrier, inc=1, device_id=(r, (c + off) % cols, d), device_id_type=MESH)

    for way in ways:
        @pl.loop(1, depths)
        def _(off):
            device = (r, c ^ way, (d + off) % depths)
            pl.semaphore_signal(barrier, inc=1, device_id=device, device_id_type=MESH)

    own = [
        pltpu.make_async_copy(codes_ref.at[me], got_codes_ref.at[me], own_sem.at[0]),
        pltpu.make_async_copy(left_ref, lefts_ref.at[c], own_sem.at[1]),
    ]
    for copy in own:
        copy.start()
    pl.semaphore_wait(barrier, window - 1 + cols - 1 + len(ways) * (depths - 1))

    def remote(src, dst, send, recv, device):
        return pltpu.make_async_remote_copy(
            src_ref=src, dst_ref=dst, send_sem=send, recv_sem=recv,
            device_id=device, device_id_type=MESH,
        )

    begin, pass_on, end = spread(
        cols, blocks_ref.shape[2], left_ref, lefts_ref, left_send, left_recv
    )

    def code_copy(slot, other):
        return remote(
            codes_ref.at[other], got_codes_ref.at[slot], code_send.at[other], code_recv.at[slot],
            (other // depths, c, other % depths),
        )

    def swap_copy(part, depth):
        first, length, way = parts[part]
        there = pl.ds(first, length)
        return remote(
            pack_ref.at[(1 - r) * depths + depth, there], merged_ref.at[depth, there],
            swap_send.at[part, depth], swap_recv.at[part, depth], (1 - r, c, d),
        )

    def chip_copy():
        return remote(
            pack_ref.at[(1 - r) * depths + d], got_ref.at[d],
            swap_send.at[0, d], swap_recv.at[0, d], (1 - r, c, d),
        )

    def list_copy(part, slot, depth):
        first, length, way = parts[part]
        there = pl.ds(first, length)
        if way:
            target, device = relay_ref.at[way - 1, depth, pl.ds(0, length)], (r, c ^ way, d)
        else:
            target, device = got_ref.at[slot, there], (r, c, depth)
        return remote(
            merged_ref.at[depth, there], target,
            list_send.at[part, depth], list_recv.at[part, depth if way else slot], device,
        )

    def relay_copy(part, slot, depth):
        first, length, way = parts[part]
        return remote(
            relay_ref.at[way - 1, depth, pl.ds(0, length)],
            got_ref.at[slot, pl.ds(first, length)],
            relay_send.at[part, depth], relay_recv.at[part, slot], (r, c ^ way, depth),
        )

    def arrival(part, depth):
        copy = relay_copy if parts[part][2] else list_copy
        return copy(part, depth, depth)

    def each_part(wide, action):
        if len(parts) > 1:
            @pl.when(wide)
            def _():
                for part in reversed(range(1, len(parts))):
                    action(part)
        action(0)

    def each_relay(action):
        for part, (first, length, way) in enumerate(parts):
            if way:
                @pl.when(d // panels == c ^ way)
                def _():
                    @pl.loop(1, depths)
                    def _(off):
                        action(part, (d + off) % depths)

    @pl.loop(1, depths)
    def _(off):
        depth = (d + off) % depths
        each_part(diag, lambda part: swap_copy(part, depth).start())

    @pl.loop(1, depths)
    def _(off):
        depth = (d + off) % depths

        def forward(part):
            swap_copy(part, depth).wait_recv()
            first, length, way = parts[part]
            q = r * depths + depth
            count = jnp.broadcast_to(codes_ref[q, 0:1, 0:1], pack_ref.shape[2:])
            for place in range(first, first + length):
                rank = jnp.where(r == 1, jnp.where(diag, capacity, short) - 1 - place, place)
                merged_ref[depth, place] = jnp.where(
                    rank < count, pack_ref[q, place], merged_ref[depth, place]
                )
            list_copy(part, d, depth).start()

        each_part(diag, forward)

    begin()
    chip_copy().start()

    @pl.loop(1, window)
    def _(off):
        code_copy(me, (me + off) % window).start()

    def relay(part, depth):
        list_copy(part, d, depth).wait_recv()
        relay_copy(part, d, depth).start()

    each_relay(relay)

    for copy in own:
        copy.wait()

    pass_on()
    end()

    @pl.loop(1, window)
    def _(off):
        other = (me + off) % window
        code_copy(other, other).wait_recv()
        code_copy(me, other).wait_send()

    chip_copy().wait()

    @pl.loop(1, depths)
    def _(off):
        depth = (d + off) % depths
        each_part(diag, lambda part: swap_copy(part, depth).wait_send())
        each_part(depth // panels == c, lambda part: arrival(part, depth).wait_recv())
        each_part(diag, lambda part: list_copy(part, d, depth).wait_send())

    each_relay(lambda part, depth: relay_copy(part, d, depth).wait_send())


def exchange(pack, codes, blocks, sizes, short, ident):
    window, capacity, size, _ = pack.shape
    rows, cols, depths = sizes
    panels = blocks.shape[1]
    vmem = pl.BlockSpec(memory_space=pltpu.VMEM)
    lists = (depths, capacity, size, size)
    sem = pltpu.SemaphoreType.DMA
    return pl.pallas_call(
        functools.partial(exchange_kernel, sizes, panels, short),
        out_shape=(
            jax.ShapeDtypeStruct(lists, jnp.float32),
            jax.ShapeDtypeStruct(codes.shape, jnp.int32),
            jax.ShapeDtypeStruct((cols,) + blocks.shape[1:], jnp.float32),
        ),
        in_specs=[vmem, vmem, pl.BlockSpec(memory_space=pltpu.HBM)],
        out_specs=(vmem,) * 3,
        scratch_shapes=[
            pltpu.VMEM(lists, jnp.float32),
            sem((window,)), sem((window,)), sem((2, max(3, cols))), sem((2, cols)),
            sem((4, depths)), sem((4, depths)), sem((4, depths)), sem((4, depths)),
            pltpu.VMEM((2, depths, max(1, (capacity - short) // 2), size, size), jnp.float32),
            sem((4, depths)), sem((4, depths)), sem((2,)),
        ],
        compiler_params=pltpu.CompilerParams(
            collective_id=ident, has_side_effects=True, vmem_limit_bytes=VMEM_LIMIT
        ),
    )(pack, codes, blocks)


def halves(value):
    high = value.astype(jnp.bfloat16)
    return high, (value - high.astype(jnp.float32)).astype(jnp.bfloat16)


def product(left, right):
    left_high, left_low = halves(left)
    right_high, right_low = halves(right)
    dot = functools.partial(jnp.dot, preferred_element_type=jnp.float32)
    return dot(left_high, right_high) + (dot(left_high, right_low) + dot(left_low, right_high))


def multiply_into(acc_ref, lefts_ref, got_ref, blocks_ref, codes_ref, held, sems, sizes, short):
    rows, cols, depths = sizes
    window = rows * depths
    capacity = got_ref.shape[1]
    panels, slots = blocks_ref.shape[1:3]
    out_slots = panels * slots
    r, c, d = position()
    me_q = r * depths + d
    own = codes_ref[me_q, 0, 0]

    def fetch(n):
        at = codes_ref[me_q, 0, SOURCE + n]
        row = at // out_slots
        block = blocks_ref.at[row, (at // slots) % panels, at % slots]
        return pltpu.make_async_copy(block, held.at[n], sems.at[n])

    @pl.loop(0, own)
    def _(n):
        fetch(n).start()

    acc_ref[...] = jnp.zeros_like(acc_ref)

    def add(q, n, right):
        code = codes_ref[q, 0, HEAD + n]
        depth = q % depths
        left = lefts_ref[depth // panels, depth % panels, code // out_slots]
        s = code % out_slots
        acc_ref[s // slots, s % slots] += product(left, right)

    @pl.loop(0, window)
    def _(q):
        depth = q % depths
        on_chip = depth == d
        room = jnp.where(on_chip | (depth // panels == c), capacity, short)
        from_back = (q // depths == 1) & jnp.logical_not(on_chip)
        count = jnp.where(q == me_q, 0, jnp.minimum(codes_ref[q, 0, 0], room))

        @pl.loop(0, count)
        def _(n):
            add(q, n, got_ref[depth, jnp.where(from_back, room - 1 - n, n)])

    @pl.loop(0, own)
    def _(n):
        fetch(n).wait()
        add(me_q, n, held[n])


def square_kernel(
    sizes, short, codes_ref, got_ref, blocks_ref, lefts_ref, out_ref, held, sems
):
    multiply_into(out_ref, lefts_ref, got_ref, blocks_ref, codes_ref, held, sems, sizes, short)


def cube_kernel(
    sizes, short, codes_ref, got_ref, blocks_ref, lefts_ref, square_ref, out_ref, held, sems
):
    multiply_into(out_ref, lefts_ref, got_ref, blocks_ref, codes_ref, held, sems, sizes, short)
    out_ref[...] = 3.0 * square_ref[...] - 2.0 * out_ref[...]


def local_product(kernel, codes, got, blocks, lefts, extra, out_shape, out_specs):
    vmem = pl.BlockSpec(memory_space=pltpu.VMEM)
    _, panels, slots, size, _ = blocks.shape
    most = slots * slots * panels
    return pl.pallas_call(
        kernel,
        out_shape=out_shape,
        in_specs=[
            pl.BlockSpec(memory_space=pltpu.SMEM),
            vmem,
            pl.BlockSpec(memory_space=pltpu.HBM),
            vmem,
        ] + [vmem] * len(extra),
        out_specs=out_specs,
        scratch_shapes=[
            pltpu.VMEM((most, size, size), jnp.float32),
            pltpu.SemaphoreType.DMA((most,)),
        ],
        compiler_params=pltpu.CompilerParams(vmem_limit_bytes=VMEM_LIMIT),
    )(codes, got, blocks, lefts, *extra)


def gather_kernel(
    cols, square_ref, codes_ref, squares_ref, any_ref, flag_ref, flags_ref,
    send_sem, recv_sem, flag_send, flag_recv, own_sem,
):
    r, c, d = position()
    barrier = pltpu.get_barrier_semaphore()

    @pl.loop(1, cols)
    def _(off):
        pl.semaphore_signal(barrier, inc=1, device_id=(r, (c + off) % cols, d), device_id_type=MESH)

    flag_ref[...] = jnp.max(codes_ref[...], axis=0)
    own = [
        pltpu.make_async_copy(square_ref, squares_ref.at[c], own_sem.at[0]),
        pltpu.make_async_copy(flag_ref, flags_ref.at[c], own_sem.at[1]),
    ]
    for copy in own:
        copy.start()
    begin, pass_on, end = spread(
        cols, square_ref.shape[1], square_ref, squares_ref, send_sem, recv_sem
    )
    pl.semaphore_wait(barrier, cols - 1)

    def flag_copy(slot, other):
        return pltpu.make_async_remote_copy(
            src_ref=flag_ref,
            dst_ref=flags_ref.at[slot],
            send_sem=flag_send.at[other],
            recv_sem=flag_recv.at[slot],
            device_id=(r, other, d),
            device_id_type=MESH,
        )

    begin()

    @pl.loop(1, cols)
    def _(off):
        flag_copy(c, (c + off) % cols).start()

    pass_on()
    for copy in own:
        copy.wait()

    @pl.loop(1, cols)
    def _(off):
        other = (c + off) % cols
        flag_copy(other, other).wait_recv()
        flag_copy(c, other).wait_send()

    end()
    flags = jnp.max(flags_ref[...], axis=0)
    any_ref[...] = jnp.broadcast_to(flags[:, 1:2], flags.shape)


def gather_square(square, codes, cols, ident):
    vmem = pl.BlockSpec(memory_space=pltpu.VMEM)
    return pl.pallas_call(
        functools.partial(gather_kernel, cols),
        out_shape=(
            jax.ShapeDtypeStruct((cols,) + square.shape, jnp.float32),
            jax.ShapeDtypeStruct(codes.shape[1:], jnp.int32),
        ),
        in_specs=[vmem] * 2,
        out_specs=(vmem,) * 2,
        scratch_shapes=[
            pltpu.VMEM(codes.shape[1:], jnp.int32),
            pltpu.VMEM((cols,) + codes.shape[1:], jnp.int32),
            pltpu.SemaphoreType.DMA((2, max(3, cols))),
            pltpu.SemaphoreType.DMA((2, cols)),
            pltpu.SemaphoreType.DMA((cols,)),
            pltpu.SemaphoreType.DMA((cols,)),
            pltpu.SemaphoreType.DMA((2,)),
        ],
        compiler_params=pltpu.CompilerParams(collective_id=ident, has_side_effects=True),
    )(square, codes)


def body(sizes, blocks, columns, counts):
    rows, cols, depths = sizes
    local_rows, panels, slots, size, _ = blocks.shape
    most = slots * slots * panels
    local = jnp.concatenate([columns.reshape(local_rows, panels * slots).T, counts.T], 0)
    entries = local.shape[0]
    local = jnp.pad(local, ((0, -entries % 8), (0, -local_rows % LANES)))
    win, sibling = gather_meta(local, sizes, panels, entries)
    block_shape = jax.ShapeDtypeStruct(blocks.shape[1:], jnp.float32)
    vmem = pl.BlockSpec(memory_space=pltpu.VMEM)

    def square_step(short, capacity, ident):
        pack, codes = pack_lists(win, local, sibling, blocks, sizes, short, capacity)
        got, got_codes, lefts = exchange(pack, codes, blocks, sizes, short, ident)
        square = local_product(
            functools.partial(square_kernel, sizes, short),
            got_codes, got, blocks, lefts, (), block_shape, vmem,
        )
        squares, too_long = gather_square(square, got_codes, cols, ident + 1)
        return got, got_codes, square, squares, too_long

    def cube_step(short, got, got_codes, square, squares):
        return local_product(
            functools.partial(cube_kernel, sizes, short),
            got_codes, got, blocks, squares, (square,), block_shape, vmem,
        )

    sizes_tried = []
    for short, capacity in TIERS:
        tier = (min(short, most), min(capacity, most))
        if tier not in sizes_tried:
            sizes_tried.append(tier)
    sizes_tried.append((most, most))

    def attempt(tier):
        short, capacity = sizes_tried[tier]
        *lists, too_long = square_step(short, capacity, 1 + 2 * tier)
        if (short, capacity) == (most, most):
            return cube_step(short, *lists)
        return lax.cond(
            too_long[0, 0] != 0, lambda: attempt(tier + 1), lambda: cube_step(short, *lists)
        )

    out = attempt(0)
    return out[None]


def solution(mesh):
    placed = (
        P(("row", "depth"), "col", None, None, None),
        P(("row", "depth"), "col", None),
        P(("row", "depth"), "col"),
    )
    sizes = (mesh.shape["row"], mesh.shape["col"], mesh.shape["depth"])
    return jax.shard_map(
        functools.partial(body, sizes),
        mesh=mesh,
        in_specs=placed,
        out_specs=P(("row", "depth"), "col", None, None, None),
        check_vma=False,
    )
```
